32 devices in a mesh: fsdp: 4 (over x, core), ctx: 4 (over z), tp: 2 (over y).
Axes of the slice: x: 2, y: 2, z: 4, core: 2. Of those that a mesh axis runs over, the one named last changes fastest.
Arguments:
- tokens: bfloat16 [16384, 2560], P(('fsdp', 'ctx')), may hold values from -6 to 6
- query_weight: bfloat16 [2560, 2560], P(('fsdp', 'ctx'), 'tp'), may hold values from -0.125 to 0.125
- keyval_weight: bfloat16 [2560, 512], P(('fsdp', 'ctx')), may hold values from -0.125 to 0.125
- out_weight: bfloat16 [2560, 2560], P(('fsdp', 'ctx'), 'tp'), may hold values from -3.5 to 3.5
- gate_weight: bfloat16 [2560, 7680], P(('fsdp', 'ctx'), 'tp'), may hold values from -0.125 to 0.125
- up_weight: bfloat16 [2560, 7680], P(('fsdp', 'ctx'), 'tp'), may hold values from -0.125 to 0.125
- down_weight: bfloat16 [2560, 7680], P(('fsdp', 'ctx'), 'tp'), may hold values from -0.125 to 0.125
- first_gain: bfloat16 [2560], P(('fsdp', 'ctx')), may hold values from -0.8984375 to 0.8984375
- second_gain: bfloat16 [2560], P(('fsdp', 'ctx')), may hold values from -0.8984375 to 0.8984375
- cotangent: bfloat16 [16384, 2560], P(('fsdp', 'ctx')), may hold values from -6 to 6
Outputs:
- output: bfloat16 [16384, 2560], P(('fsdp', 'ctx'))
- input_grad: bfloat16 [16384, 2560], P(('fsdp', 'ctx'))
- query_grad: float32 [2560, 2560], P(('fsdp', 'ctx'), 'tp')
- keyval_grad: float32 [2560, 512], P(('fsdp', 'ctx'))
- out_grad: float32 [2560, 2560], P(('fsdp', 'ctx'), 'tp')
- gate_grad: float32 [2560, 7680], P(('fsdp', 'ctx'), 'tp')
- up_grad: float32 [2560, 7680], P(('fsdp', 'ctx'), 'tp')
- down_grad: float32 [2560, 7680], P(('fsdp', 'ctx'), 'tp')
- first_grad: float32 [2560], P(('fsdp', 'ctx'))
- second_grad: float32 [2560], P(('fsdp', 'ctx'))
The draws below stay inside these ranges and needn't reach their ends.
All inputs are finite; a program needn't handle non-finite values.
Results may differ from the reference program's by a relative error of at most 0.018.
Values may be sent and summed in bfloat16 or wider, within the bound.
A program may use at most 448 MiB of HBM per device.

```python
import jax
import jax.numpy as jnp
from jax import lax

D = 2560
H = 10
HD = 256
FF = 7680
W = 2048
LEN = 4096
Q = 2560
TOKENS = 16384


def with_spikes(entries, key, source, target, blocks, factor):
    owner, partner = [(jnp.arange(entries.shape[dim]) // (entries.shape[dim] // blocks)).reshape([-1 if axis == dim else 1 for axis in range(entries.ndim)]) for dim in (source, target)]
    chosen = jax.random.permutation(key, blocks)[partner]
    strong = (owner == chosen) | (owner == (partner + blocks // 2) % blocks)
    return jnp.where(strong, factor * entries, entries)


def shard_levels(rng, dims, pieces, smallest, largest):
    loudness = 1.0
    for position, parts in pieces:
        steps = jax.random.uniform(jax.random.fold_in(jax.random.fold_in(rng, 6), position), (parts,), jnp.float32, smallest / len(pieces), largest / len(pieces))
        loudness = loudness * jnp.repeat(jnp.exp(steps), dims[position] // parts).reshape((-1,) + (1,) * (len(dims) - 1 - position))
    return loudness


def centred(key, extent, width, limit, pieces=(), kind=jnp.bfloat16):
    level = shard_levels(key, extent, pieces, -0.22, 0.18) if pieces else 1.0
    values = jax.random.normal(key, extent, jnp.float32) * width * level
    return jnp.minimum(jnp.maximum(values, -limit), limit).astype(kind)


def heavy_noise(rng, shape, width, most, split, heavy, kind=jnp.bfloat16):
    entries = width * jax.random.normal(rng, shape, jnp.float32)
    if split:
        entries = entries * shard_levels(rng, shape, split, -0.22, 0.18)
    return jnp.clip(with_spikes(entries, jax.random.fold_in(rng, 3), *heavy), -most, most).astype(kind)


def setup_inputs(seed: int = 0) -> dict:
    key_of = jax.random.split(jax.random.key(seed), 11)
    return {
        "tokens": heavy_noise(key_of[0], (TOKENS, D), 1.0, 6.0, ((0, 16),), (0, 1, 16, 2.0)),
        "query_weight": centred(key_of[1], (D, Q), D ** -0.5, 0.125, ((0, 16), (1, 2))),
        "keyval_weight": centred(key_of[2], (D, 2 * HD), D ** -0.5, 0.125, ((0, 16),)),
        "out_weight": centred(key_of[3], (D, Q), (Q * 3 // W) ** -0.5, 3.5, ((0, 16), (1, 2))),
        "gate_weight": centred(key_of[4], (D, FF), D ** -0.5, 0.125, ((0, 16), (1, 2))),
        "up_weight": centred(key_of[5], (D, FF), D ** -0.5, 0.125, ((0, 16), (1, 2))),
        "down_weight": centred(key_of[6], (D, FF), (FF // 4) ** -0.5, 0.125, ((0, 16), (1, 2))),
        "first_gain": centred(key_of[7], (D,), 0.3, 0.8984375, ((0, 16),)),
        "second_gain": centred(key_of[8], (D,), 0.3, 0.8984375, ((0, 16),)),
        "cotangent": heavy_noise(key_of[9], (TOKENS, D), 1.0, 6.0, ((0, 16),), (0, 1, 16, 2.0)),
    }


EPS = 1e-06
FAR = -1e+30
HIGH = lax.Precision.HIGHEST

@jax.custom_vjp
def low(v):
    return lax.optimization_barrier(v.astype(jnp.bfloat16)).astype(jnp.float32)

@jax.custom_vjp
def low_back(v):
    return v

def low_keep(v):
    return (low(v), None)

def low_pass(kept, grad):
    return (grad,)

def back_keep(v):
    return (v, None)

def back_low(kept, grad):
    return (low(grad),)
low.defvjp(low_keep, low_pass)
low_back.defvjp(back_keep, back_low)

def matmul(left, right):
    return jnp.dot(left, right, precision=HIGH, preferred_element_type=jnp.float32)

def rms_scale(values, gain):
    inverse = lax.rsqrt(lax.optimization_barrier(jnp.mean(values * values, axis=-1, keepdims=True)) + EPS)
    return values * inverse * (1.0 + gain)

def window_attention(queries, keys, values):
    rows = min(512, LEN)
    blocks = LEN // rows
    padding = jnp.zeros((W, HD), jnp.float32)
    keys_padded = jnp.concatenate([padding, keys], 0)
    values_padded = jnp.concatenate([padding, values], 0)

    def one_block(index):
        start = index * rows
        query_block = lax.dynamic_slice_in_dim(queries, start, rows, 0)
        key_block = lax.dynamic_slice_in_dim(keys_padded, start, W + rows, 0)
        value_block = lax.dynamic_slice_in_dim(values_padded, start, W + rows, 0)
        scores = jnp.einsum('qhd,kd->hqk', query_block, key_block, precision=HIGH)
        scores = low_back(scores)
        query_pos = start + jnp.arange(rows, dtype=jnp.int32)
        key_pos = start - W + jnp.arange(W + rows, dtype=jnp.int32)
        gap = query_pos[:, None] - key_pos[None, :]
        live = (gap >= 0) & (gap < W) & (key_pos[None, :] >= 0)
        scores = jnp.where(live[None], scores, FAR)
        top = lax.optimization_barrier(jnp.max(scores, axis=-1, keepdims=True))
        weights = jnp.exp(scores - top)
        probs = weights / lax.optimization_barrier(jnp.sum(weights, axis=-1, keepdims=True))
        return jnp.einsum('hqk,kd->qhd', low(probs), value_block, precision=HIGH)
    result = lax.map(jax.checkpoint(one_block), jnp.arange(blocks, dtype=jnp.int32))
    return result.reshape(LEN, H, HD)

def layer(inputs, params):
    query_w, keyval_w, out_w, gate_w, up_w, down_w, gain_one, gain_two = params
    first_norm = low(rms_scale(inputs, gain_one))
    queries = low(low_back(matmul(first_norm, query_w) * HD ** (-0.5)))
    keyval = low(low_back(matmul(first_norm, keyval_w)))
    attended = window_attention(queries.reshape(LEN, H, HD), keyval[:, :HD], keyval[:, HD:])
    attended = low(low_back(attended.reshape(LEN, H * HD)))
    middle = inputs + low_back(matmul(attended, out_w.T))
    second_norm = low(rms_scale(middle, gain_two))
    gate = low_back(matmul(second_norm, gate_w))
    upward = low_back(matmul(second_norm, up_w))
    hidden = low(jax.nn.gelu(gate, approximate=True) * upward)
    return middle + low_back(matmul(hidden, down_w.T))

def reference(tokens, query_weight, keyval_weight, out_weight, gate_weight, up_weight, down_weight, first_gain, second_gain, cotangent):
    weights = tuple((item.astype(jnp.float32) for item in (query_weight, keyval_weight, out_weight, gate_weight, up_weight, down_weight, first_gain, second_gain)))
    sequences = tokens.astype(jnp.float32).reshape(-1, LEN, D)
    cotangents = cotangent.astype(jnp.float32).reshape(-1, LEN, D)

    def forward(params, inputs):
        return lax.map(lambda single: jax.checkpoint(layer)(single, params), inputs)
    result, pullback = jax.vjp(forward, weights, sequences)
    weight_grads, input_grads = pullback(cotangents)
    return (result.reshape(-1, D).astype(jnp.bfloat16), input_grads.reshape(-1, D).astype(jnp.bfloat16), weight_grads[0], weight_grads[1], weight_grads[2], weight_grads[3], weight_grads[4], weight_grads[5], weight_grads[6], weight_grads[7])
```

```python
import functools

import jax
import jax.numpy as jnp
from jax import lax
from jax.experimental import pallas as pl
from jax.experimental.pallas import tpu as pltpu
from jax.sharding import PartitionSpec as P

HD = 256
W = 2048
EPS = 1e-06
FAR = -1e30
LOW = jnp.bfloat16
WIDE = jnp.float32
CONTRACT_ROWS = (((0,), (0,)), ((), ()))
CONTRACT_LAST = (((1,), (1,)), ((), ()))
VMEM = 56 * 1024 * 1024


def matmul(left, right):
    return jnp.dot(left, right, preferred_element_type=WIDE)


def rows_product(left, right):
    return lax.dot_general(left, right, CONTRACT_ROWS, preferred_element_type=WIDE)


def right_transposed(left, right):
    return lax.dot_general(left, right, CONTRACT_LAST, preferred_element_type=WIDE)


def gelu_parts(gate):
    c = 0.7978845608028654
    inner = c * (gate + 0.044715 * gate * gate * gate)
    t = jnp.tanh(inner)
    value = 0.5 * gate * (1.0 + t)
    slope = 0.5 * (1.0 + t) + 0.5 * gate * (1.0 - t * t) * c * (1.0 + 3 * 0.044715 * gate * gate)
    return value, slope


def attend_kernel(place_ref, q_ref, win_ref, out_ref, probs_ref, bias_ref, *, heads, hops, rows, block):
    span = W + block
    start = pl.program_id(0) * block
    first = (hops - place_ref[0]) * rows - start
    row = lax.broadcasted_iota(jnp.int32, (block, span), 0)
    col = lax.broadcasted_iota(jnp.int32, (block, span), 1)
    live = (col > row) & (col <= row + W) & (col >= first)
    bias_ref[...] = jnp.where(live, 0.0, FAR)
    window = pl.ds(pl.multiple_of(start, block), span)
    for h in range(heads):
        cols = slice(h * HD, (h + 1) * HD)
        scores = right_transposed(q_ref[:, cols], win_ref[window, :HD]) + bias_ref[...]
        top = jnp.max(scores, axis=1, keepdims=True)
        weights = jnp.exp(scores - top)
        total = jnp.sum(weights, axis=1, keepdims=True)
        probs_ref[h] = (weights * (1.0 / total)).astype(LOW)
        out_ref[:, cols] = matmul(probs_ref[h], win_ref[window, HD:]).astype(LOW)


def attend(queries, window, place, hops):
    rows, width = queries.shape
    heads = width // HD
    block = min(256, rows)
    span = W + block
    return pl.pallas_call(
        functools.partial(attend_kernel, heads=heads, hops=hops, rows=rows, block=block),
        grid=(rows // block,),
        in_specs=[
            pl.BlockSpec(memory_space=pltpu.SMEM),
            pl.BlockSpec((block, width), lambda i: (i, 0)),
            pl.BlockSpec(window.shape, lambda i: (0, 0)),
        ],
        out_specs=[
            pl.BlockSpec((block, width), lambda i: (i, 0)),
            pl.BlockSpec((heads, block, span), lambda i: (0, i, 0)),
        ],
        out_shape=[
            jax.ShapeDtypeStruct((rows, width), LOW),
            jax.ShapeDtypeStruct((heads, rows, span), LOW),
        ],
        scratch_shapes=[pltpu.VMEM((block, span), WIDE)],
        compiler_params=pltpu.CompilerParams(vmem_limit_bytes=VMEM),
        cost_estimate=pl.CostEstimate(
            flops=4 * rows * span * width, bytes_accessed=2 * heads * rows * span, transcendentals=heads * rows * span
        ),
        name="attend",
    )(place, queries, window)


def attend_back_kernel(q_ref, win_ref, out_ref, probs_ref, back_ref, dq_ref, dwin_ref, ds_ref, *, heads, block):
    span = W + block
    step = pl.program_id(0)

    @pl.when(step == 0)
    def _():
        dwin_ref[...] = jnp.zeros_like(dwin_ref)

    window = pl.ds(pl.multiple_of(step * block, block), span)
    for h in range(heads):
        cols = slice(h * HD, (h + 1) * HD)
        back = back_ref[:, cols]
        along = jnp.sum(back.astype(WIDE) * out_ref[:, cols].astype(WIDE), axis=1, keepdims=True)
        grad_probs = right_transposed(back, win_ref[window, HD:])
        ds_ref[h] = (probs_ref[h].astype(WIDE) * (grad_probs - along)).astype(LOW)
        dq = matmul(ds_ref[h], win_ref[window, :HD]).astype(LOW)
        dq_ref[:, cols] = (dq.astype(WIDE) * HD ** (-0.5)).astype(LOW)
    queries = jnp.concatenate([q_ref[:, h * HD : (h + 1) * HD] for h in range(heads)], axis=0)
    backs = jnp.concatenate([back_ref[:, h * HD : (h + 1) * HD] for h in range(heads)], axis=0)
    dwin_ref[window, :HD] += rows_product(ds_ref[...].reshape(heads * block, span), queries)
    dwin_ref[window, HD:] += rows_product(probs_ref[...].reshape(heads * block, span), backs)


def attend_back(queries, window, attended, probs, grad_attended):
    rows, width = queries.shape
    heads = width // HD
    block = min(256, rows)
    span = W + block
    by_rows = pl.BlockSpec((block, width), lambda i: (i, 0))
    return pl.pallas_call(
        functools.partial(attend_back_kernel, heads=heads, block=block),
        grid=(rows // block,),
        in_specs=[
            by_rows,
            pl.BlockSpec(window.shape, lambda i: (0, 0)),
            by_rows,
            pl.BlockSpec((heads, block, span), lambda i: (0, i, 0)),
            by_rows,
        ],
        out_specs=[by_rows, pl.BlockSpec(window.shape, lambda i: (0, 0))],
        out_shape=[
            jax.ShapeDtypeStruct((rows, width), LOW),
            jax.ShapeDtypeStruct(window.shape, WIDE),
        ],
        scratch_shapes=[pltpu.VMEM((heads, block, span), LOW)],
        compiler_params=pltpu.CompilerParams(vmem_limit_bytes=VMEM),
        cost_estimate=pl.CostEstimate(
            flops=8 * rows * span * width, bytes_accessed=2 * heads * rows * span, transcendentals=0
        ),
        name="attend_back",
    )(queries, window, attended, probs, grad_attended)


def swap(array, axis, flip):
    count = lax.axis_size(axis)
    return lax.ppermute(array, axis, [(i, i ^ flip) for i in range(count)])


def from_place(array, by):
    count = lax.axis_size("ctx")
    return lax.ppermute(array, "ctx", [(i, i + by) for i in range(count) if 0 <= i + by < count])


def tp_sum(partial):
    own = partial.astype(LOW)
    return own.astype(WIDE) + swap(own, "tp", 1).astype(WIDE)


def scattered_product(left, right):
    place = lax.axis_index("fsdp")
    span = left.shape[1] // lax.axis_size("fsdp")

    def part(flip):
        return lax.dynamic_slice_in_dim(left, (place ^ flip) * span, span, 1)

    away = rows_product(jnp.concatenate([part(3), part(1)], axis=1), right).astype(LOW)
    got = swap(away, "fsdp", 1)
    far = (rows_product(part(2), right) + got[:span].astype(WIDE)).astype(LOW)
    arrived = swap(far, "fsdp", 2)
    near = rows_product(part(0), right) + got[span:].astype(WIDE) + arrived.astype(WIDE)
    return lax.psum_scatter(near.astype(LOW), "ctx", scatter_dimension=0, tiled=True).astype(WIDE)


def gathered(shard):
    return lax.all_gather(shard, ("fsdp", "ctx"), axis=0, tiled=True)


def on_device(
    tokens,
    query_weight,
    keyval_weight,
    out_weight,
    gate_weight,
    up_weight,
    down_weight,
    first_gain,
    second_gain,
    cotangent,
):
    rows = tokens.shape[0]
    width = query_weight.shape[1]
    scale = HD ** (-0.5)
    hops = min(-(-W // rows), lax.axis_size("ctx") - 1)
    place = lax.axis_index("ctx")

    gains = jnp.pad(jnp.stack([first_gain, second_gain], axis=1), ((0, 0), (0, 126)))
    qkv_full = gathered(jnp.concatenate([query_weight, keyval_weight, gains], axis=1))
    out_full = gathered(out_weight)
    gate_full = gathered(gate_weight)
    up_full = gathered(up_weight)
    down_full = gathered(down_weight)
    query_full = qkv_full[:, :width]
    keyval_full = qkv_full[:, width : width + 2 * HD]
    both_gains = 1.0 + qkv_full[:, width + 2 * HD :][:, :2].astype(WIDE).T
    gain_one, gain_two = both_gains[:1], both_gains[1:]

    source = tokens.astype(WIDE)
    first_inverse = lax.rsqrt(jnp.mean(source * source, axis=-1, keepdims=True) + EPS)
    first_low = (source * first_inverse * gain_one).astype(LOW)
    keyval = matmul(first_low, keyval_full).astype(LOW)
    before = [from_place(keyval, by) for by in range(hops, 0, -1)]
    queries = (matmul(first_low, query_full) * scale).astype(LOW)
    window = jnp.concatenate(before + [keyval], axis=0)
    attended, probs = attend(queries, window, place.reshape(1), hops)
    middle = source + tp_sum(right_transposed(attended, out_full))
    second_inverse = lax.rsqrt(jnp.mean(middle * middle, axis=-1, keepdims=True) + EPS)
    second_low = (middle * second_inverse * gain_two).astype(LOW)
    gate = matmul(second_low, gate_full)
    upward = matmul(second_low, up_full)
    value, slope = gelu_parts(gate)
    hidden = (value * upward).astype(LOW)
    to_up = value.astype(LOW)
    to_gate = (slope * upward).astype(LOW)
    output = (middle + tp_sum(right_transposed(hidden, down_full))).astype(LOW)

    down_grad = scattered_product(cotangent, hidden)
    grad_hidden = matmul(cotangent, down_full)
    gate_back = (grad_hidden * to_gate.astype(WIDE)).astype(LOW)
    up_back = (grad_hidden * to_up.astype(WIDE)).astype(LOW)
    grad_second = tp_sum(right_transposed(gate_back, gate_full) + right_transposed(up_back, up_full))
    gate_grad = scattered_product(second_low, gate_back)
    up_grad = scattered_product(second_low, up_back)

    scaled = grad_second * gain_two
    along = jnp.mean(scaled * middle, axis=-1, keepdims=True)
    grad_middle = (
        cotangent.astype(WIDE)
        + second_inverse * scaled
        - middle * second_inverse * second_inverse * second_inverse * along
    )
    middle_low = grad_middle.astype(LOW)
    grad_attended = matmul(middle_low, out_full).astype(LOW)
    out_grad = scattered_product(middle_low, attended)
    query_back, window_back = attend_back(queries, window, attended, probs, grad_attended)
    own = window_back[hops * rows :]
    for by in range(1, hops + 1):
        sent = window_back[(hops - by) * rows : (hops - by + 1) * rows].astype(LOW)
        own = own + from_place(sent, -by).astype(WIDE)
    keyval_back = tp_sum(own).astype(LOW)
    query_share = tp_sum(right_transposed(query_back, query_full))
    qkv_grad = scattered_product(first_low, jnp.concatenate([query_back, keyval_back], axis=1))
    query_grad = qkv_grad[:, :width]
    keyval_grad = qkv_grad[:, width:]
    grad_first = query_share + right_transposed(keyval_back, keyval_full)
    scaled = grad_first * gain_one
    along = jnp.mean(scaled * source, axis=-1, keepdims=True)
    input_grad = (
        grad_middle
        + first_inverse * scaled
        - source * first_inverse * first_inverse * first_inverse * along
    ).astype(LOW)

    def row_sum(weight, grad):
        return jnp.sum(weight.astype(WIDE) * grad, axis=1)

    sums = jnp.stack(
        [
            row_sum(query_weight, query_grad),
            row_sum(gate_weight, gate_grad) + row_sum(up_weight, up_grad),
        ]
    )
    sums = sums + swap(sums, "tp", 1)
    first_grad = (sums[0] + row_sum(keyval_weight, keyval_grad)) / (1.0 + first_gain.astype(WIDE))
    second_grad = sums[1] / (1.0 + second_gain.astype(WIDE))
    return (
        output,
        input_grad,
        query_grad,
        keyval_grad,
        out_grad,
        gate_grad,
        up_grad,
        down_grad,
        first_grad,
        second_grad,
    )


def solution(mesh):
    rows = P(("fsdp", "ctx"), None)
    split = P(("fsdp", "ctx"), "tp")
    vector = P(("fsdp", "ctx"))
    return jax.shard_map(
        on_device,
        mesh=mesh,
        in_specs=(rows, split, rows, split, split, split, split, vector, vector, rows),
        out_specs=(rows, rows, split, rows, split, split, split, split, vector, vector),
        check_vma=False,
    )
```

```python
import functools

import jax
import jax.numpy as jnp
from jax import lax
from jax.experimental import pallas as pl
from jax.experimental.pallas import tpu as pltpu
from jax.sharding import PartitionSpec as P

HD = 256
W = 2048
EPS = 1e-06
FAR = -1e30
LOW = jnp.bfloat16
WIDE = jnp.float32
CONTRACT_ROWS = (((0,), (0,)), ((), ()))
CONTRACT_LAST = (((1,), (1,)), ((), ()))
VMEM = 60 * 1024 * 1024


def matmul(left, right):
    return jnp.dot(left, right, preferred_element_type=WIDE)


def rows_product(left, right):
    return lax.dot_general(left, right, CONTRACT_ROWS, preferred_element_type=WIDE)


def right_transposed(left, right):
    return lax.dot_general(left, right, CONTRACT_LAST, preferred_element_type=WIDE)


def gelu_parts(gate):
    c = 0.7978845608028654
    inner = c * (gate + 0.044715 * gate * gate * gate)
    t = jnp.tanh(inner)
    value = 0.5 * gate * (1.0 + t)
    slope = 0.5 * (1.0 + t) + 0.5 * gate * (1.0 - t * t) * c * (1.0 + 3 * 0.044715 * gate * gate)
    return value, slope


def attend_kernel(place_ref, q_ref, win_ref, out_ref, probs_ref, bias_ref, *, heads, hops, rows, block):
    span = W + block
    start = pl.program_id(0) * block
    first = (hops - place_ref[0]) * rows - start
    row = lax.broadcasted_iota(jnp.int32, (block, span), 0)
    col = lax.broadcasted_iota(jnp.int32, (block, span), 1)
    live = (col > row) & (col <= row + W) & (col >= first)
    bias_ref[...] = jnp.where(live, 0.0, FAR)
    window = pl.ds(pl.multiple_of(start, block), span)
    for h in range(heads):
        cols = slice(h * HD, (h + 1) * HD)
        scores = right_transposed(q_ref[:, cols], win_ref[window, :HD]) + bias_ref[...]
        top = jnp.max(scores, axis=1, keepdims=True)
        weights = jnp.exp(scores - top)
        total = jnp.sum(weights, axis=1, keepdims=True)
        probs_ref[h] = (weights * (1.0 / total)).astype(LOW)
        out_ref[:, cols] = matmul(probs_ref[h], win_ref[window, HD:]).astype(LOW)


def attend(queries, window, place, hops):
    rows, width = queries.shape
    heads = width // HD
    block = min(256, rows)
    span = W + block
    return pl.pallas_call(
        functools.partial(attend_kernel, heads=heads, hops=hops, rows=rows, block=block),
        grid=(rows // block,),
        in_specs=[
            pl.BlockSpec(memory_space=pltpu.SMEM),
            pl.BlockSpec((block, width), lambda i: (i, 0)),
            pl.BlockSpec(window.shape, lambda i: (0, 0)),
        ],
        out_specs=[
            pl.BlockSpec((block, width), lambda i: (i, 0)),
            pl.BlockSpec((heads, block, span), lambda i: (0, i, 0)),
        ],
        out_shape=[
            jax.ShapeDtypeStruct((rows, width), LOW),
            jax.ShapeDtypeStruct((heads, rows, span), LOW),
        ],
        scratch_shapes=[pltpu.VMEM((block, span), WIDE)],
        compiler_params=pltpu.CompilerParams(vmem_limit_bytes=VMEM),
        name="attend",
    )(place, queries, window)


CONTRACT = {"nn": (((1,), (0,)), ((), ())), "nt": CONTRACT_LAST, "tn": CONTRACT_ROWS}


def products_body(kind, n_pairs, n_extras, finish, sub, keep):
    def body(*refs):
        pairs = [(refs[2 * p], refs[2 * p + 1]) for p in range(n_pairs)]
        extras = refs[2 * n_pairs : 2 * n_pairs + n_extras]
        outs = refs[2 * n_pairs + n_extras :]
        bn = pairs[0][1].shape[0 if kind == "nt" else 1]
        step = sub or bn
        for start in range(0, bn, step):
            cols = slice(start, start + step)
            total = None
            for left, right in pairs:
                part = right[cols, :] if kind == "nt" else right[:, cols]
                term = lax.dot_general(left[...], part, CONTRACT[kind], preferred_element_type=WIDE)
                total = term if total is None else total + term
            given = [e[:, cols].astype(WIDE) for e in extras]
            keep(outs, cols, finish(total, *given) if finish else [sum(given, total)])

    return body


def keep_blocks(outs, cols, results):
    for out, result in zip(outs, results, strict=True):
        out[:, cols] = result.astype(out.dtype)


def products_specs(kind, depths, bm, bn, left_block, right_col):
    specs = []
    for depth in depths:
        if kind == "tn":
            specs.append(pl.BlockSpec((depth, bm), lambda i, j: (0, left_block(i))))
        else:
            specs.append(pl.BlockSpec((bm, depth), lambda i, j: (left_block(i), 0)))
        if kind == "nt":
            specs.append(pl.BlockSpec((bn, depth), lambda i, j: (j, right_col)))
        else:
            specs.append(pl.BlockSpec((depth, bn), lambda i, j: (0, right_col + j)))
    return specs


def product(kind, left, right, *, bm, bn, width, col=0, extras=(), finish=None, outs=(LOW,), sub=0):
    depth = left.shape[1]
    by_block = pl.BlockSpec((bm, bn), lambda i, j: (i, j))
    return pl.pallas_call(
        products_body(kind, 1, len(extras), finish, sub, keep_blocks),
        grid=(left.shape[0] // bm, width // bn),
        in_specs=products_specs(kind, [depth], bm, bn, lambda i: i, col) + [by_block] * len(extras),
        out_specs=[by_block] * len(outs),
        out_shape=[jax.ShapeDtypeStruct((left.shape[0], width), each) for each in outs],
        compiler_params=pltpu.CompilerParams(vmem_limit_bytes=VMEM),
        name="product",
    )(left, right, *extras)


def by_rows(body, sliced, whole, outs, block):
    rows = sliced[0].shape[0]
    n_in = len(sliced) + len(whole)
    specs = [pl.BlockSpec((block, a.shape[1]), lambda i: (i, 0)) for a in sliced]
    specs += [pl.BlockSpec(a.shape, lambda i: (0, 0)) for a in whole]
    return pl.pallas_call(
        lambda *refs: body(refs[:n_in], refs[n_in:]),
        grid=(rows // block,),
        in_specs=specs,
        out_specs=[pl.BlockSpec((block, cols), lambda i: (i, 0)) for cols, _ in outs],
        out_shape=[jax.ShapeDtypeStruct((rows, cols), kind) for cols, kind in outs],
        compiler_params=pltpu.CompilerParams(vmem_limit_bytes=VMEM),
        name="by_rows",
    )(*sliced, *whole)


def add_norm(ins, outs):
    tokens, own, other, gain = ins
    middle = tokens[...].astype(WIDE) + (own[...].astype(WIDE) + other[...].astype(WIDE))
    inverse = lax.rsqrt(jnp.mean(middle * middle, axis=1, keepdims=True) + EPS)
    outs[0][...] = middle.astype(LOW)
    outs[1][...] = (middle * inverse * gain[...]).astype(LOW)
    outs[2][...] = jnp.broadcast_to(inverse, outs[2].shape)


def norm_back(values, grad, gain, inverse):
    scaled = grad * gain
    along = jnp.sum(scaled * values, axis=1, keepdims=True) * (1.0 / values.shape[1])
    return inverse * scaled - values * (inverse * inverse * inverse * along)


def middle_back(ins, outs):
    cotangent, middle, inverse, own, other, gain, out_full = ins
    grad = own[...].astype(WIDE) + other[...].astype(WIDE)
    back = norm_back(middle[...].astype(WIDE), grad, gain[...], inverse[:, :1])
    low = (cotangent[...].astype(WIDE) + back).astype(LOW)
    outs[0][...] = low
    outs[1][...] = matmul(low, out_full[...]).astype(LOW)


def source_back(ins, outs):
    tokens, middle_low, own, other, keyval_back, gain, keyval_full = ins
    grad = own[...].astype(WIDE) + other[...].astype(WIDE)
    grad = grad + right_transposed(keyval_back[...], keyval_full[...])
    values = tokens[...].astype(WIDE)
    inverse = lax.rsqrt(jnp.mean(values * values, axis=1, keepdims=True) + EPS)
    back = middle_low[...].astype(WIDE) + norm_back(values, grad, gain[...], inverse)
    outs[0][...] = back.astype(LOW)


def finish_up(upward, gate):
    value, slope = gelu_parts(gate)
    return value * upward, value, slope * upward


def finish_hidden(grad_hidden, to_gate, to_up):
    return grad_hidden * to_gate, grad_hidden * to_up


MESH = pl.DeviceIdType.MESH


class Links:
    def __init__(self, send_sems, recv_sems):
        self.send_sems, self.recv_sems = send_sems, recv_sems
        self.count = 0
        self.open = []
        self.fsdp = lax.axis_index("fsdp")
        self.place = lax.axis_index("ctx")
        self.core = {"fsdp": self.fsdp + 1 - 2 * lax.rem(self.fsdp, 2)}
        self.chip = {"fsdp": lax.rem(self.fsdp + 2, 4)}
        self.tp = {"tp": 1 - lax.axis_index("tp")}

    def block(self, flip):
        return (self.fsdp, self.core["fsdp"], self.chip["fsdp"], 3 - self.fsdp)[flip]

    def along(self, bit):
        return {"ctx": self.place + bit - 2 * bit * lax.rem(lax.div(self.place, bit), 2)}

    def meet(self, partners):
        barrier = pltpu.get_barrier_semaphore()
        for partner in partners:
            pl.semaphore_signal(barrier, inc=1, device_id=partner, device_id_type=MESH)
        pl.semaphore_wait(barrier, len(partners))

    def copy(self, source, target, partner):
        made = pltpu.make_async_remote_copy(
            src_ref=source,
            dst_ref=target,
            send_sem=self.send_sems.at[self.count],
            recv_sem=self.recv_sems.at[self.count],
            device_id=partner,
            device_id_type=MESH,
        )
        self.count += 1
        return made

    def send(self, source, target, partner):
        made = self.copy(source, target, partner)
        made.start()
        self.open.append(made)
        return made

    def close(self):
        for made in self.open:
            made.wait_send()


def job(kind, pairs, outs, *, bm, bn, steps=1, left_block=None, right_col=0, extras=(), finish=None, sub=0):
    depths = [left.shape[0 if kind == "tn" else 1] for left, _ in pairs]
    width = outs[0].shape[1]
    specs = products_specs(kind, depths, bm, bn, left_block or (lambda i: i), right_col)
    specs += [pl.BlockSpec((bm, bn), lambda i, j, at=at: (i + at, j)) for _, at in extras]
    pltpu.emit_pipeline(
        products_body(kind, len(pairs), len(extras), finish, sub, keep_blocks),
        grid=(steps, width // bn),
        in_specs=specs,
        out_specs=[pl.BlockSpec((bm, bn), lambda i, j: (i, j))] * len(outs),
    )(*[ref for pair in pairs for ref in pair], *[ref for ref, _ in extras], *outs)


def rows_job(body, sliced, whole, outs, block):
    n_in = len(sliced) + len(whole)
    specs = [pl.BlockSpec((block, a.shape[1]), lambda i: (i, 0)) for a in sliced]
    specs += [pl.BlockSpec(a.shape, lambda i: (0, 0)) for a in whole]
    pltpu.emit_pipeline(
        lambda *refs: body(refs[:n_in], refs[n_in:]),
        grid=(sliced[0].shape[0] // block,),
        in_specs=specs,
        out_specs=[pl.BlockSpec((block, a.shape[1]), lambda i: (i, 0)) for a in outs],
    )(*sliced, *whole, *outs)


def bits_of(count):
    bits = []
    while 1 << len(bits) < count:
        bits.append(1 << len(bits))
    return bits


def piece_order(count):
    order = [0]
    for bit in reversed(bits_of(count)):
        order = order + [r + bit for r in order]
    return order


class Scatter:
    @staticmethod
    def shapes(prefix, features, width, count):
        part = features // 4
        size = part // count
        out = {"away": (2 * part, width), "got": (2 * part, width), "far": (part, width), "arrived": (part, width)}
        left = count
        out["near"] = (left, size, width)
        for k in range(len(bits_of(count))):
            left //= 2
            out[f"recv{k}"] = (left, size, width)
            if left > 1:
                out[f"mid{k}"] = (left, size, width)
        return {prefix + key: jax.ShapeDtypeStruct(shape, LOW) for key, shape in out.items()}

    def __init__(self, prefix, refs, links, left, right, bn, count, total=None):
        self.refs, self.prefix, self.links, self.bn, self.total = refs, prefix, links, bn, total
        self.pairs = [(refs[left], refs[right])]
        self.part = refs[left].shape[1] // 4
        self.bits = bits_of(count)
        self.moving = {}

    def ref(self, key):
        return self.refs[self.prefix + key]

    def wait(self, key):
        if key in self.moving:
            self.moving.pop(key).wait_recv()

    def away(self):
        core, both = self.links.block(1), self.links.block(3)
        job(
            "tn",
            self.pairs,
            [self.ref("away")],
            bm=self.part,
            bn=self.bn,
            steps=2,
            left_block=lambda i: both + i * (core - both),
        )
        self.moving["got"] = self.links.send(self.ref("away"), self.ref("got"), self.links.core)

    def far(self):
        self.wait("got")
        chip = self.links.block(2)
        job(
            "tn",
            self.pairs,
            [self.ref("far")],
            bm=self.part,
            bn=self.bn,
            left_block=lambda i: chip,
            extras=[(self.ref("got"), 0)],
        )

    def cross(self):
        self.moving["arrived"] = self.links.send(self.ref("far"), self.ref("arrived"), self.links.chip)

    def near(self):
        self.wait("arrived")
        own, place = self.links.block(0), self.links.place
        near, total = self.ref("near"), self.total
        count, size = near.shape[0], near.shape[1]
        order = piece_order(count)

        def keep(outs, cols, results):
            total[:, cols] = results[0]
            for k in range(count):
                at = 0
                for bit in self.bits:
                    mine = lax.rem(lax.div(place, bit), 2)
                    at = at + bit * (1 - mine if order[k] & bit else mine)
                rows = pl.ds(pl.multiple_of(at * size, size), size)
                outs[0][k, :, cols] = total[rows, cols].astype(LOW)

        bm, bn = self.part, self.bn
        left, right = self.pairs[0]
        pltpu.emit_pipeline(
            products_body("tn", 1, 2, None, 0, keep),
            grid=(1, right.shape[1] // bn),
            in_specs=products_specs("tn", [left.shape[0]], bm, bn, lambda i: own, 0)
            + [pl.BlockSpec((bm, bn), lambda i, j: (1, j)), pl.BlockSpec((bm, bn), lambda i, j: (0, j))],
            out_specs=[pl.BlockSpec((count, size, bn), lambda i, j: (0, 0, j))],
        )(left, right, self.ref("got"), self.ref("arrived"), near)

    def kept(self, k):
        return self.ref(f"mid{k - 1}" if k else "near")

    def halve(self, k):
        now = self.kept(k)
        half = now.shape[0] // 2
        self.moving[f"recv{k}"] = self.links.send(
            now.at[pl.ds(half, half)], self.ref(f"recv{k}"), self.links.along(self.bits[k])
        )

    def add(self, k):
        self.wait(f"recv{k}")
        if k + 1 == len(self.bits):
            return
        now, mid = self.kept(k), self.ref(f"mid{k}")
        half, size, bn = mid.shape[0], mid.shape[1], self.bn

        def body(own, other, out):
            out[...] = (own[...].astype(WIDE) + other[...].astype(WIDE)).astype(LOW)

        block = pl.BlockSpec((half, size, bn), lambda j: (0, 0, j))
        pltpu.emit_pipeline(body, grid=(mid.shape[2] // bn,), in_specs=[block, block], out_specs=[block])(
            now, self.ref(f"recv{k}"), mid
        )

    def rest(self, k):
        self.add(k)
        for later in range(k + 1, len(self.bits)):
            self.halve(later)
            self.add(later)


def scatter_result(prefix, arrays):
    last = len(bits_of(arrays[prefix + "near"].shape[0])) - 1
    now = arrays[prefix + (f"mid{last - 1}" if last else "near")]
    return now[0].astype(WIDE) + arrays[prefix + f"recv{last}"][0].astype(WIDE)


def remote_call(kernel, inputs, outputs, scratch, collective_id, name):
    anywhere = pl.BlockSpec(memory_space=pl.ANY)
    sems = pltpu.SemaphoreType.DMA((32,))
    return pl.pallas_call(
        kernel,
        in_specs=[anywhere] * len(inputs),
        out_specs=[anywhere] * len(outputs),
        out_shape=outputs,
        scratch_shapes=scratch + [sems, sems],
        compiler_params=pltpu.CompilerParams(
            collective_id=collective_id, has_side_effects=True, vmem_limit_bytes=VMEM
        ),
        name=name,
    )


def by_name(body, reads, writes, n_scratch):
    names = reads + writes

    def kernel(*refs):
        rest = refs[len(names) :]
        body(dict(zip(names, refs)), Links(rest[-2], rest[-1]), *rest[:n_scratch])

    return kernel


def down_start(r, links, *, count):
    links.meet([links.core])
    down = Scatter("d_", r, links, "cotangent", "hidden", r["hidden"].shape[1] // 3, count)
    down.away()
    down.far()
    links.close()


def attend_back(refs, rows, heads, block):
    span = W + block
    steps = rows // block
    queries, backs, outs, probs = (refs[k] for k in ("queries", "grad_attended", "attended", "probs"))

    def scoped(win, dwin, q, back, out, dq, p, ds, sems):
        loads = [
            pltpu.make_async_copy(a, b, sems.at[k])
            for k, (a, b) in enumerate([(refs["window"], win), (queries, q), (backs, back), (outs, out)])
        ]

        def fetch(i):
            slot = lax.rem(i, 2)
            at = pl.ds(pl.multiple_of(i * block, block), block)
            return pltpu.make_async_copy(probs.at[:, at, :], p.at[slot], sems.at[4 + slot])

        fetch(0).start()
        for load in loads:
            load.start()
        dwin[...] = jnp.zeros_like(dwin)
        for load in loads:
            load.wait()

        def step(i, carry):
            @pl.when(i + 1 < steps)
            def _():
                fetch(i + 1).start()

            fetch(i).wait()
            slot = lax.rem(i, 2)
            at = pl.ds(pl.multiple_of(i * block, block), block)
            window = pl.ds(pl.multiple_of(i * block, block), span)
            for h in range(heads):
                cols = slice(h * HD, (h + 1) * HD)
                g = back[at, cols]
                along = jnp.sum(g.astype(WIDE) * out[at, cols].astype(WIDE), axis=1, keepdims=True)
                grad_probs = right_transposed(g, win[window, HD:])
                ds[h] = (p[slot, h].astype(WIDE) * (grad_probs - along)).astype(LOW)
                part = matmul(ds[h], win[window, :HD]).astype(LOW)
                dq[at, cols] = (part.astype(WIDE) * HD ** (-0.5)).astype(LOW)
            q_all = jnp.concatenate([q[at, h * HD : (h + 1) * HD] for h in range(heads)], axis=0)
            g_all = jnp.concatenate([back[at, h * HD : (h + 1) * HD] for h in range(heads)], axis=0)
            dwin[window, :HD] += rows_product(ds[...].reshape(heads * block, span), q_all)
            dwin[window, HD:] += rows_product(p[slot].reshape(heads * block, span), g_all)
            return carry

        lax.fori_loop(0, steps, step, 0)
        win[...] = dwin[...].astype(LOW)
        stores = [
            pltpu.make_async_copy(win, refs["window_back"], sems.at[0]),
            pltpu.make_async_copy(dq, refs["query_back"], sems.at[1]),
        ]
        for store in stores:
            store.start()
        for store in stores:
            store.wait()

    width = heads * HD
    length = refs["window"].shape[0]
    pl.run_scoped(
        scoped,
        pltpu.VMEM((length, 2 * HD), LOW),
        pltpu.VMEM((length, 2 * HD), WIDE),
        pltpu.VMEM((rows, width), LOW),
        pltpu.VMEM((rows, width), LOW),
        pltpu.VMEM((rows, width), LOW),
        pltpu.VMEM((rows, width), LOW),
        pltpu.VMEM((2, heads, block, span), LOW),
        pltpu.VMEM((heads, block, span), LOW),
        pltpu.SemaphoreType.DMA((6,)),
    )


def window_sum(place, count, hops):
    def body(ins, outs):
        total = ins[0][...].astype(WIDE)
        for by in range(1, hops + 1):
            total = total + jnp.where(place + by < count, ins[by][...].astype(WIDE), 0.0)
        outs[0][...] = total.astype(LOW)

    return body


def pair_sum(ins, outs):
    outs[0][...] = (ins[0][...].astype(WIDE) + ins[1][...].astype(WIDE)).astype(LOW)


def feed_back(r, links, total, *, rows, heads, count):
    half, block = rows // 2, min(256, rows)
    features = r["cotangent"].shape[1]
    width = heads * HD
    third = r["hidden"].shape[1] // 3
    bits = bits_of(count)
    links.meet([links.core, links.chip, links.tp] + [links.along(bit) for bit in bits])
    down = Scatter("d_", r, links, "cotangent", "hidden", third, count, total)
    gate = Scatter("g_", r, links, "second_low", "gate_back", third, count, total)
    up = Scatter("u_", r, links, "second_low", "up_back", third, count, total)
    out = Scatter("o_", r, links, "middle_low", "attended", width, count, total)
    top, bottom = pl.ds(0, half), pl.ds(half, half)

    down.cross()
    job(
        "nn",
        [(r["cotangent"], r["down_full"])],
        [r["gate_back"], r["up_back"]],
        bm=rows,
        bn=third * 3 // 5,
        sub=third // 5,
        extras=[(r["to_gate"], 0), (r["to_up"], 0)],
        finish=finish_hidden,
    )

    def second(part):
        job(
            "nt",
            [(r["gate_back"].at[part], r["gate_full"]), (r["up_back"].at[part], r["up_full"])],
            [r["second"].at[part]],
            bm=half,
            bn=256,
        )
        return links.send(r["second"].at[part], r["second_other"].at[part], links.tp)

    first = second(top)
    last = second(bottom)
    gate.away()
    down.near()
    down.halve(0)
    gate.far()
    gate.cross()
    up.away()
    job("nt", [(r["hidden"].at[top], r["down_full"])], [r["feed0"]], bm=half, bn=512)
    job("nt", [(r["hidden"].at[bottom], r["down_full"])], [r["feed1"]], bm=half, bn=512)
    up.far()
    first.wait_recv()
    last.wait_recv()
    feed = links.send(r["feed0"], r["feed_other0"], links.tp)
    rows_job(
        middle_back,
        [r["cotangent"], r["middle"], r["second_inverse"], r["second"], r["second_other"]],
        [r["gain_two"], r["small_full"].at[:, pl.ds(width, width)]],
        [r["middle_low"], r["grad_attended"]],
        block,
    )
    out.away()
    down.add(0)
    out.far()
    gate.wait("arrived")
    feed.wait_recv()
    links.close()


def scores_back(r, links, total, *, rows, heads, hops, count):
    half, block = rows // 2, min(256, rows)
    width = heads * HD
    third = r["up_back"].shape[1] // 3
    links.meet([links.core, links.chip, links.tp] + [{"ctx": lax.rem(links.place + k, count)} for k in range(1, count)])
    down = Scatter("d_", r, links, "cotangent", "hidden", third, count, total)
    gate = Scatter("g_", r, links, "second_low", "gate_back", third, count, total)
    up = Scatter("u_", r, links, "second_low", "up_back", third, count, total)
    query = Scatter("q_", r, links, "first_low", "query_back", width, count, total)
    keyval = Scatter("k_", r, links, "first_low", "keyval_back", 2 * HD, count, total)

    up.cross()
    feed = links.send(r["feed1"], r["feed_other1"], links.tp)
    down.halve(1)
    attend_back(r, rows, heads, block)
    windows = []
    for by in range(1, hops + 1):
        move = links.copy(
            r["window_back"].at[pl.ds((hops - by) * rows, rows)],
            r["window_other"].at[by - 1],
            {"ctx": lax.rem(links.place + count - by, count)},
        )

        @pl.when(links.place >= by)
        def _(move=move):
            move.start()

        windows.append(move)
    gate.near()
    gate.halve(0)
    job("nt", [(r["query_back"], r["small_full"].at[:, pl.ds(0, width)])], [r["share"]], bm=rows, bn=512)
    feed.wait_recv()
    share = links.send(r["share"].at[pl.ds(0, half)], r["share_other0"], links.tp)
    query.away()
    for by in range(1, hops + 1):

        @pl.when(links.place + by < count)
        def _(move=windows[by - 1]):
            move.wait_recv()

    rows_job(
        window_sum(links.place, count, hops),
        [r["window_back"].at[pl.ds(hops * rows, rows)]] + [r["window_other"].at[by] for by in range(hops)],
        [],
        [r["keyval_own"]],
        block,
    )
    swap = links.send(r["keyval_own"], r["keyval_other"], links.tp)
    query.far()
    gate.add(0)
    swap.wait_recv()
    rows_job(pair_sum, [r["keyval_own"], r["keyval_other"]], [], [r["keyval_back"]], block)
    keyval.away()
    down.rest(1)
    keyval.far()
    up.wait("arrived")
    share.wait_recv()
    for by in range(1, hops + 1):

        @pl.when(links.place >= by)
        def _(move=windows[by - 1]):
            move.wait_send()

    links.close()


def last_sums(r, links, total, *, rows, heads, count):
    half = rows // 2
    width = heads * HD
    third = r["up_back"].shape[1] // 3
    bits = bits_of(count)
    links.meet([links.chip, links.tp] + [links.along(bit) for bit in bits])
    gate = Scatter("g_", r, links, "second_low", "gate_back", third, count, total)
    up = Scatter("u_", r, links, "second_low", "up_back", third, count, total)
    out = Scatter("o_", r, links, "middle_low", "attended", width, count, total)
    query = Scatter("q_", r, links, "first_low", "query_back", width, count, total)
    keyval = Scatter("k_", r, links, "first_low", "keyval_back", 2 * HD, count, total)
    share = links.send(r["share"].at[pl.ds(half, half)], r["share_other1"], links.tp)
    out.cross()
    gate.halve(1)
    up.near()
    up.halve(0)
    out.near()
    out.halve(0)
    query.cross()
    keyval.cross()
    up.add(0)
    up.halve(1)
    query.near()
    query.halve(0)
    out.add(0)
    out.halve(1)
    keyval.near()
    keyval.halve(0)
    query.add(0)
    query.halve(1)
    keyval.add(0)
    keyval.halve(1)
    for each in (gate, up, out, query, keyval):
        each.rest(1)
    share.wait_recv()
    links.close()


def from_place(array, by):
    count = lax.axis_size("ctx")
    return lax.ppermute(array, "ctx", [(i, i + by) for i in range(count) if i + by < count])


def swap_tp(array):
    return lax.ppermute(array, "tp", [(0, 1), (1, 0)])


def gathered(shard):
    return lax.all_gather(shard, ("fsdp", "ctx"), axis=0, tiled=True)


def on_device(
    tokens,
    query_weight,
    keyval_weight,
    out_weight,
    gate_weight,
    up_weight,
    down_weight,
    first_gain,
    second_gain,
    cotangent,
):
    rows, features = tokens.shape
    width = query_weight.shape[1]
    units = gate_weight.shape[1]
    heads = width // HD
    scale = HD ** (-0.5)
    count = lax.axis_size("ctx")
    hops = min(-(-W // rows), count - 1)
    place = lax.axis_index("ctx")
    block = min(256, rows)

    gains = jnp.pad(jnp.stack([first_gain, second_gain], axis=1), ((0, 0), (0, 126)))
    small_full = gathered(jnp.concatenate([query_weight, out_weight, keyval_weight, gains], axis=1))
    gate_full = gathered(gate_weight)
    up_full = gathered(up_weight)
    down_full = gathered(down_weight)
    query_full = small_full[:, :width]
    keyval_full = small_full[:, 2 * width : 2 * width + 2 * HD]
    both_gains = 1.0 + small_full[:, 2 * width + 2 * HD :][:, :2].astype(WIDE).T
    gain_one, gain_two = both_gains[:1], both_gains[1:]

    source = tokens.astype(WIDE)
    first_inverse = lax.rsqrt(jnp.mean(source * source, axis=-1, keepdims=True) + EPS)
    first_low = (source * first_inverse * gain_one).astype(LOW)
    keyval = matmul(first_low, keyval_full).astype(LOW)
    before = [from_place(keyval, by) for by in range(hops, 0, -1)]
    queries = (matmul(first_low, query_full) * scale).astype(LOW)
    window = jnp.concatenate(before + [keyval], axis=0)
    attended, probs = attend(queries, window, place.reshape(1), hops)
    (branch,) = product("nt", attended, small_full, bm=rows, bn=512, width=features, col=1)
    middle, second_low, second_inverse = by_rows(
        add_norm,
        [tokens, branch, swap_tp(branch)],
        [gain_two],
        [(features, LOW), (features, LOW), (128, WIDE)],
        block,
    )
    (gate,) = product("nn", second_low, gate_full, bm=rows, bn=768, width=units, outs=(WIDE,))
    hidden, to_up, to_gate = product(
        "nn",
        second_low,
        up_full,
        bm=rows,
        bn=768,
        width=units,
        sub=256,
        extras=[gate],
        finish=finish_up,
        outs=(LOW, LOW, LOW),
    )

    plain = {
        "gate_back": (rows, units),
        "up_back": (rows, units),
        "second": (rows, features),
        "second_other": (rows, features),
        "feed0": (rows // 2, features),
        "feed1": (rows // 2, features),
        "feed_other0": (rows // 2, features),
        "feed_other1": (rows // 2, features),
        "middle_low": (rows, features),
        "grad_attended": (rows, width),
        "query_back": (rows, width),
        "window_back": window.shape,
        "window_other": (hops, rows, 2 * HD),
        "keyval_own": (rows, 2 * HD),
        "keyval_other": (rows, 2 * HD),
        "keyval_back": (rows, 2 * HD),
        "share": (rows, features),
        "share_other0": (rows // 2, features),
        "share_other1": (rows // 2, features),
    }
    shapes = {key: jax.ShapeDtypeStruct(shape, LOW) for key, shape in plain.items()}
    for prefix, each in (("d_", units), ("g_", units), ("u_", units), ("o_", width), ("q_", width), ("k_", 2 * HD)):
        shapes |= Scatter.shapes(prefix, features, each, count)
    done = dict(
        cotangent=cotangent,
        down_full=down_full,
        gate_full=gate_full,
        up_full=up_full,
        small_full=small_full,
        to_gate=to_gate,
        to_up=to_up,
        hidden=hidden,
        first_low=first_low,
        second_low=second_low,
        middle=middle,
        second_inverse=second_inverse,
        gain_two=gain_two,
        queries=queries,
        window=window,
        attended=attended,
        probs=probs,
    )
    total = pltpu.VMEM((features // 4, max(width, units // 3)), WIDE)
    sizes = dict(rows=rows, heads=heads, count=count)
    late = len(bits_of(count)) - 1

    def stage(prefix, *keys):
        return [prefix + key for key in keys]

    def halving(prefix, first, end):
        keys = []
        for k in range(first, end):
            keys += [f"{prefix}recv{k}"] + ([f"{prefix}mid{k}"] if k < late else [])
        return keys

    reads, writes = ["cotangent", "hidden"], stage("d_", "away", "got", "far")
    call = remote_call(
        by_name(functools.partial(down_start, count=count), reads, writes, 0),
        reads,
        [shapes[key] for key in writes],
        [],
        0,
        "down_start",
    )
    done |= zip(writes, call(*[done[key] for key in reads]))

    reads = stage("d_", "got", "far") + ["cotangent", "hidden", "down_full", "gate_full", "up_full", "small_full"]
    reads += ["to_gate", "to_up", "second_low", "middle", "second_inverse", "gain_two", "attended"]
    writes = ["gate_back", "up_back", "second", "second_other", "feed0", "feed1", "feed_other0", "middle_low"]
    writes += ["grad_attended"] + stage("d_", "arrived", "near") + halving("d_", 0, 1)
    writes += stage("g_", "away", "got", "far", "arrived") + stage("u_", "away", "got", "far")
    writes += stage("o_", "away", "got", "far")
    call = remote_call(
        by_name(functools.partial(feed_back, **sizes), reads, writes, 1),
        reads,
        [shapes[key] for key in writes],
        [total],
        1,
        "feed_back",
    )
    done |= zip(writes, call(*[done[key] for key in reads]))

    reads = ["cotangent", "hidden", "gate_back", "up_back", "second_low", "first_low", "small_full", "feed1"]
    reads += ["queries", "window", "attended", "probs", "grad_attended", "u_far", "g_got", "g_arrived"]
    reads += ["d_near"] + halving("d_", 0, 1)
    writes = ["feed_other1", "u_arrived", "query_back", "window_back", "window_other", "keyval_own", "keyval_other"]
    writes += ["keyval_back", "share", "share_other0", "g_near"] + halving("g_", 0, 1) + halving("d_", 1, late + 1)
    writes += stage("q_", "away", "got", "far") + stage("k_", "away", "got", "far")
    call = remote_call(
        by_name(functools.partial(scores_back, hops=hops, **sizes), reads, writes, 1),
        reads,
        [shapes[key] for key in writes],
        [total],
        2,
        "scores_back",
    )
    done |= zip(writes, call(*[done[key] for key in reads]))

    reads = ["gate_back", "up_back", "second_low", "first_low", "middle_low", "attended", "query_back", "keyval_back"]
    reads += ["share", "u_got", "u_arrived", "g_near"] + halving("g_", 0, 1)
    reads += [prefix + key for prefix in ("o_", "q_", "k_") for key in ("got", "far")]
    writes = ["share_other1", "u_near"] + [prefix + key for prefix in ("o_", "q_", "k_") for key in ("arrived", "near")]
    writes += halving("g_", 1, late + 1)
    for prefix in ("u_", "o_", "q_", "k_"):
        writes += halving(prefix, 0, late + 1)
    call = remote_call(
        by_name(functools.partial(last_sums, **sizes), reads, writes, 1),
        reads,
        [shapes[key] for key in writes],
        [total],
        3,
        "last_sums",
    )
    done |= zip(writes, call(*[done[key] for key in reads]))
    share_other = jnp.concatenate([done["share_other0"], done["share_other1"]])
    feed = jnp.concatenate([done["feed0"], done["feed1"]]).astype(WIDE)
    feed_other = jnp.concatenate([done["feed_other0"], done["feed_other1"]]).astype(WIDE)
    (input_grad,) = by_rows(
        source_back,
        [tokens, done["middle_low"], done["share"], share_other, done["keyval_back"]],
        [gain_one, keyval_full],
        [(features, LOW)],
        block,
    )
    output = (middle.astype(WIDE) + (feed + feed_other)).astype(LOW)
    down_grad, gate_grad, up_grad, out_grad, query_grad, keyval_grad = (
        scatter_result(prefix, done) for prefix in ("d_", "g_", "u_", "o_", "q_", "k_")
    )

    def row_sum(weight, grad):
        return jnp.sum(weight.astype(WIDE) * grad, axis=1)

    sums = jnp.stack(
        [
            row_sum(query_weight, query_grad),
            row_sum(gate_weight, gate_grad) + row_sum(up_weight, up_grad),
        ]
    )
    sums = sums + swap_tp(sums)
    first_grad = (sums[0] + row_sum(keyval_weight, keyval_grad)) / (1.0 + first_gain.astype(WIDE))
    second_grad = sums[1] / (1.0 + second_gain.astype(WIDE))
    return (
        output,
        input_grad,
        query_grad,
        keyval_grad,
        out_grad,
        gate_grad,
        up_grad,
        down_grad,
        first_grad,
        second_grad,
    )


def solution(mesh):
    rows = P(("fsdp", "ctx"), None)
    split = P(("fsdp", "ctx"), "tp")
    vector = P(("fsdp", "ctx"))
    return jax.shard_map(
        on_device,
        mesh=mesh,
        in_specs=(rows, split, rows, split, split, split, split, vector, vector, rows),
        out_specs=(rows, rows, split, rows, split, split, split, split, vector, vector),
        check_vma=False,
    )
```

```python
import functools

import jax
import jax.numpy as jnp
from jax import lax
from jax.experimental import pallas as pl
from jax.experimental.pallas import tpu as pltpu
from jax.sharding import PartitionSpec as P

HD = 256
W = 2048
EPS = 1e-06
FAR = -1e30
LOW = jnp.bfloat16
WIDE = jnp.float32
CONTRACT_ROWS = (((0,), (0,)), ((), ()))
CONTRACT_LAST = (((1,), (1,)), ((), ()))
VMEM = 60 * 1024 * 1024


def matmul(left, right):
    return jnp.dot(left, right, preferred_element_type=WIDE)


def rows_product(left, right):
    return lax.dot_general(left, right, CONTRACT_ROWS, preferred_element_type=WIDE)


def right_transposed(left, right):
    return lax.dot_general(left, right, CONTRACT_LAST, preferred_element_type=WIDE)


def gelu_parts(gate):
    c = 0.7978845608028654
    inner = c * (gate + 0.044715 * gate * gate * gate)
    t = jnp.tanh(inner)
    value = 0.5 * gate * (1.0 + t)
    slope = 0.5 * (1.0 + t) + 0.5 * gate * (1.0 - t * t) * c * (1.0 + 3 * 0.044715 * gate * gate)
    return value, slope


def attend_kernel(place_ref, q_ref, win_ref, out_ref, probs_ref, bias_ref, *, heads, hops, rows, block):
    span = W + block
    start = pl.program_id(0) * block
    first = (hops - place_ref[0]) * rows - start
    row = lax.broadcasted_iota(jnp.int32, (block, span), 0)
    col = lax.broadcasted_iota(jnp.int32, (block, span), 1)
    live = (col > row) & (col <= row + W) & (col >= first)
    bias_ref[...] = jnp.where(live, 0.0, FAR)
    window = pl.ds(pl.multiple_of(start, block), span)
    for h in range(heads):
        cols = slice(h * HD, (h + 1) * HD)
        scores = right_transposed(q_ref[:, cols], win_ref[window, :HD]) + bias_ref[...]
        top = jnp.max(scores, axis=1, keepdims=True)
        weights = jnp.exp(scores - top)
        total = jnp.sum(weights, axis=1, keepdims=True)
        probs_ref[h] = (weights * (1.0 / total)).astype(LOW)
        out_ref[:, cols] = matmul(probs_ref[h], win_ref[window, HD:]).astype(LOW)


def attend(queries, window, place, hops):
    rows, width = queries.shape
    heads = width // HD
    block = min(256, rows)
    span = W + block
    return pl.pallas_call(
        functools.partial(attend_kernel, heads=heads, hops=hops, rows=rows, block=block),
        grid=(rows // block,),
        in_specs=[
            pl.BlockSpec(memory_space=pltpu.SMEM),
            pl.BlockSpec((block, width), lambda i: (i, 0)),
            pl.BlockSpec(window.shape, lambda i: (0, 0)),
        ],
        out_specs=[
            pl.BlockSpec((block, width), lambda i: (i, 0)),
            pl.BlockSpec((heads, block, span), lambda i: (0, i, 0)),
        ],
        out_shape=[
            jax.ShapeDtypeStruct((rows, width), LOW),
            jax.ShapeDtypeStruct((heads, rows, span), LOW),
        ],
        scratch_shapes=[pltpu.VMEM((block, span), WIDE)],
        compiler_params=pltpu.CompilerParams(vmem_limit_bytes=VMEM),
        name="attend",
    )(place, queries, window)


CONTRACT = {"nn": (((1,), (0,)), ((), ())), "nt": CONTRACT_LAST, "tn": CONTRACT_ROWS}


def products_body(kind, n_pairs, n_extras, finish, sub, keep):
    def body(*refs):
        pairs = [(refs[2 * p], refs[2 * p + 1]) for p in range(n_pairs)]
        extras = refs[2 * n_pairs : 2 * n_pairs + n_extras]
        outs = refs[2 * n_pairs + n_extras :]
        bn = pairs[0][1].shape[0 if kind == "nt" else 1]
        step = sub or bn
        for start in range(0, bn, step):
            cols = slice(start, start + step)
            total = None
            for left, right in pairs:
                part = right[cols, :] if kind == "nt" else right[:, cols]
                term = lax.dot_general(left[...], part, CONTRACT[kind], preferred_element_type=WIDE)
                total = term if total is None else total + term
            given = [e[:, cols].astype(WIDE) for e in extras]
            keep(outs, cols, finish(total, *given) if finish else [sum(given, total)])

    return body


def keep_blocks(outs, cols, results):
    for out, result in zip(outs, results, strict=True):
        out[:, cols] = result.astype(out.dtype)


def products_specs(kind, depths, bm, bn, left_block, right_col):
    specs = []
    for depth in depths:
        if kind == "tn":
            specs.append(pl.BlockSpec((depth, bm), lambda i, j: (0, left_block(i))))
        else:
            specs.append(pl.BlockSpec((bm, depth), lambda i, j: (left_block(i), 0)))
        if kind == "nt":
            specs.append(pl.BlockSpec((bn, depth), lambda i, j: (j, right_col)))
        else:
            specs.append(pl.BlockSpec((depth, bn), lambda i, j: (0, right_col + j)))
    return specs


def product(kind, left, right, *, bm, bn, width, col=0, extras=(), finish=None, outs=(LOW,), sub=0):
    depth = left.shape[1]
    by_block = pl.BlockSpec((bm, bn), lambda i, j: (i, j))
    return pl.pallas_call(
        products_body(kind, 1, len(extras), finish, sub, keep_blocks),
        grid=(left.shape[0] // bm, width // bn),
        in_specs=products_specs(kind, [depth], bm, bn, lambda i: i, col) + [by_block] * len(extras),
        out_specs=[by_block] * len(outs),
        out_shape=[jax.ShapeDtypeStruct((left.shape[0], width), each) for each in outs],
        compiler_params=pltpu.CompilerParams(vmem_limit_bytes=VMEM),
        name="product",
    )(left, right, *extras)


def by_rows(body, sliced, whole, outs, block):
    rows = sliced[0].shape[0]
    n_in = len(sliced) + len(whole)
    specs = [pl.BlockSpec((block, a.shape[1]), lambda i: (i, 0)) for a in sliced]
    specs += [pl.BlockSpec(a.shape, lambda i: (0, 0)) for a in whole]
    return pl.pallas_call(
        lambda *refs: body(refs[:n_in], refs[n_in:]),
        grid=(rows // block,),
        in_specs=specs,
        out_specs=[pl.BlockSpec((block, cols), lambda i: (i, 0)) for cols, _ in outs],
        out_shape=[jax.ShapeDtypeStruct((rows, cols), kind) for cols, kind in outs],
        compiler_params=pltpu.CompilerParams(vmem_limit_bytes=VMEM),
        name="by_rows",
    )(*sliced, *whole)


def add_norm(ins, outs):
    tokens, own, other, gain = ins
    middle = tokens[...].astype(WIDE) + (own[...].astype(WIDE) + other[...].astype(WIDE))
    inverse = lax.rsqrt(jnp.mean(middle * middle, axis=1, keepdims=True) + EPS)
    outs[0][...] = middle.astype(LOW)
    outs[1][...] = (middle * inverse * gain[...]).astype(LOW)
    outs[2][...] = jnp.broadcast_to(inverse, outs[2].shape)


def norm_back(values, grad, gain, inverse):
    scaled = grad * gain
    along = jnp.sum(scaled * values, axis=1, keepdims=True) * (1.0 / values.shape[1])
    return inverse * scaled - values * (inverse * inverse * inverse * along)


def middle_back(ins, outs):
    cotangent, middle, inverse, own, other, gain, out_full = ins
    grad = own[...].astype(WIDE) + other[...].astype(WIDE)
    back = norm_back(middle[...].astype(WIDE), grad, gain[...], inverse[:, :1])
    low = (cotangent[...].astype(WIDE) + back).astype(LOW)
    outs[0][...] = low
    outs[1][...] = matmul(low, out_full[...]).astype(LOW)


def source_back(ins, outs):
    tokens, middle_low, inverse, own, other, keyval_back, gain, keyval_full = ins
    grad = own[...].astype(WIDE) + other[...].astype(WIDE)
    grad = grad + right_transposed(keyval_back[...], keyval_full[...])
    back = norm_back(tokens[...].astype(WIDE), grad, gain[...], inverse[:, :1])
    outs[0][...] = (middle_low[...].astype(WIDE) + back).astype(LOW)


def add_feed(ins, outs):
    middle, own, other = ins
    outs[0][...] = (middle[...].astype(WIDE) + (own[...].astype(WIDE) + other[...].astype(WIDE))).astype(LOW)


def finish_up(upward, gate):
    value, slope = gelu_parts(gate)
    return value * upward, value, slope * upward


def finish_hidden(grad_hidden, to_gate, to_up):
    return grad_hidden * to_gate, grad_hidden * to_up


MESH = pl.DeviceIdType.MESH


class Links:
    def __init__(self, send_sems, recv_sems):
        self.send_sems, self.recv_sems = send_sems, recv_sems
        self.count = 0
        self.open = []
        self.fsdp = lax.axis_index("fsdp")
        self.place = lax.axis_index("ctx")
        self.core = {"fsdp": self.fsdp + 1 - 2 * lax.rem(self.fsdp, 2)}
        self.chip = {"fsdp": lax.rem(self.fsdp + 2, 4)}
        self.tp = {"tp": 1 - lax.axis_index("tp")}

    def block(self, flip):
        return (self.fsdp, self.core["fsdp"], self.chip["fsdp"], 3 - self.fsdp)[flip]

    def along(self, bit):
        return {"ctx": self.place + bit - 2 * bit * lax.rem(lax.div(self.place, bit), 2)}

    def meet(self, partners):
        barrier = pltpu.get_barrier_semaphore()
        for partner in partners:
            pl.semaphore_signal(barrier, inc=1, device_id=partner, device_id_type=MESH)
        pl.semaphore_wait(barrier, len(partners))

    def copy(self, source, target, partner):
        made = pltpu.make_async_remote_copy(
            src_ref=source,
            dst_ref=target,
            send_sem=self.send_sems.at[self.count],
            recv_sem=self.recv_sems.at[self.count],
            device_id=partner,
            device_id_type=MESH,
        )
        self.count += 1
        return made

    def send(self, source, target, partner):
        made = self.copy(source, target, partner)
        made.start()
        self.open.append(made)
        return made

    def close(self):
        for made in self.open:
            made.wait_send()


def job(kind, pairs, outs, *, bm, bn, steps=1, left_block=None, right_col=0, extras=(), finish=None, sub=0):
    depths = [left.shape[0 if kind == "tn" else 1] for left, _ in pairs]
    width = outs[0].shape[1]
    specs = products_specs(kind, depths, bm, bn, left_block or (lambda i: i), right_col)
    specs += [pl.BlockSpec((bm, bn), lambda i, j, at=at: (i + at, j)) for _, at in extras]
    pltpu.emit_pipeline(
        products_body(kind, len(pairs), len(extras), finish, sub, keep_blocks),
        grid=(steps, width // bn),
        in_specs=specs,
        out_specs=[pl.BlockSpec((bm, bn), lambda i, j: (i, j))] * len(outs),
    )(*[ref for pair in pairs for ref in pair], *[ref for ref, _ in extras], *outs)


def rows_job(body, sliced, whole, outs, block):
    n_in = len(sliced) + len(whole)
    specs = [pl.BlockSpec((block, a.shape[1]), lambda i: (i, 0)) for a in sliced]
    specs += [pl.BlockSpec(a.shape, lambda i: (0, 0)) for a in whole]
    pltpu.emit_pipeline(
        lambda *refs: body(refs[:n_in], refs[n_in:]),
        grid=(sliced[0].shape[0] // block,),
        in_specs=specs,
        out_specs=[pl.BlockSpec((block, a.shape[1]), lambda i: (i, 0)) for a in outs],
    )(*sliced, *whole, *outs)


def bits_of(count):
    bits = []
    while 1 << len(bits) < count:
        bits.append(1 << len(bits))
    return bits


def piece_order(count):
    order = [0]
    for bit in reversed(bits_of(count)):
        order = order + [r + bit for r in order]
    return order


class Scatter:
    @staticmethod
    def shapes(prefix, features, width, count):
        part = features // 4
        size = part // count
        out = {"away": (2 * part, width), "got": (2 * part, width), "far": (part, width), "arrived": (part, width)}
        left = count
        out["near"] = (left, size, width)
        for k in range(len(bits_of(count))):
            left //= 2
            out[f"recv{k}"] = (left, size, width)
            if left > 1:
                out[f"mid{k}"] = (left, size, width)
        return {prefix + key: jax.ShapeDtypeStruct(shape, LOW) for key, shape in out.items()}

    def __init__(self, prefix, refs, links, left, right, bn, count, total=None):
        self.refs, self.prefix, self.links, self.bn, self.total = refs, prefix, links, bn, total
        self.pairs = [(refs[left], refs[right])]
        self.part = refs[left].shape[1] // 4
        self.bits = bits_of(count)
        self.moving = {}

    def ref(self, key):
        return self.refs[self.prefix + key]

    def wait(self, key):
        if key in self.moving:
            self.moving.pop(key).wait_recv()

    def away(self):
        core, both = self.links.block(1), self.links.block(3)
        job(
            "tn",
            self.pairs,
            [self.ref("away")],
            bm=self.part,
            bn=self.bn,
            steps=2,
            left_block=lambda i: both + i * (core - both),
        )
        self.moving["got"] = self.links.send(self.ref("away"), self.ref("got"), self.links.core)

    def far(self):
        self.wait("got")
        chip = self.links.block(2)
        job(
            "tn",
            self.pairs,
            [self.ref("far")],
            bm=self.part,
            bn=self.bn,
            left_block=lambda i: chip,
            extras=[(self.ref("got"), 0)],
        )

    def cross(self):
        self.moving["arrived"] = self.links.send(self.ref("far"), self.ref("arrived"), self.links.chip)

    def near(self):
        self.wait("arrived")
        own, place = self.links.block(0), self.links.place
        near, total = self.ref("near"), self.total
        count, size = near.shape[0], near.shape[1]
        order = piece_order(count)

        def keep(outs, cols, results):
            total[:, cols] = results[0]
            for k in range(count):
                at = 0
                for bit in self.bits:
                    mine = lax.rem(lax.div(place, bit), 2)
                    at = at + bit * (1 - mine if order[k] & bit else mine)
                rows = pl.ds(pl.multiple_of(at * size, size), size)
                outs[0][k, :, cols] = total[rows, cols].astype(LOW)

        bm, bn = self.part, self.bn
        left, right = self.pairs[0]
        pltpu.emit_pipeline(
            products_body("tn", 1, 2, None, 0, keep),
            grid=(1, right.shape[1] // bn),
            in_specs=products_specs("tn", [left.shape[0]], bm, bn, lambda i: own, 0)
            + [pl.BlockSpec((bm, bn), lambda i, j: (1, j)), pl.BlockSpec((bm, bn), lambda i, j: (0, j))],
            out_specs=[pl.BlockSpec((count, size, bn), lambda i, j: (0, 0, j))],
        )(left, right, self.ref("got"), self.ref("arrived"), near)

    def kept(self, k):
        return self.ref(f"mid{k - 1}" if k else "near")

    def halve(self, k):
        now = self.kept(k)
        half = now.shape[0] // 2
        self.moving[f"recv{k}"] = self.links.send(
            now.at[pl.ds(half, half)], self.ref(f"recv{k}"), self.links.along(self.bits[k])
        )

    def add(self, k):
        self.wait(f"recv{k}")
        if k + 1 == len(self.bits):
            return
        now, mid = self.kept(k), self.ref(f"mid{k}")
        half, size, bn = mid.shape[0], mid.shape[1], self.bn

        def body(own, other, out):
            out[...] = (own[...].astype(WIDE) + other[...].astype(WIDE)).astype(LOW)

        block = pl.BlockSpec((half, size, bn), lambda j: (0, 0, j))
        pltpu.emit_pipeline(body, grid=(mid.shape[2] // bn,), in_specs=[block, block], out_specs=[block])(
            now, self.ref(f"recv{k}"), mid
        )

    def rest(self, k):
        self.add(k)
        for later in range(k + 1, len(self.bits)):
            self.halve(later)
            self.add(later)


def scatter_result(prefix, arrays):
    last = len(bits_of(arrays[prefix + "near"].shape[0])) - 1
    now = arrays[prefix + (f"mid{last - 1}" if last else "near")]
    return now[0].astype(WIDE) + arrays[prefix + f"recv{last}"][0].astype(WIDE)


def remote_call(kernel, inputs, outputs, scratch, collective_id, name):
    anywhere = pl.BlockSpec(memory_space=pl.ANY)
    sems = pltpu.SemaphoreType.DMA((32,))
    return pl.pallas_call(
        kernel,
        in_specs=[anywhere] * len(inputs),
        out_specs=[anywhere] * len(outputs),
        out_shape=outputs,
        scratch_shapes=scratch + [sems, sems],
        compiler_params=pltpu.CompilerParams(
            collective_id=collective_id, has_side_effects=True, vmem_limit_bytes=VMEM
        ),
        name=name,
    )


def by_name(body, reads, writes, n_scratch):
    names = reads + writes

    def kernel(*refs):
        rest = refs[len(names) :]
        body(dict(zip(names, refs)), Links(rest[-2], rest[-1]), *rest[:n_scratch])

    return kernel


def down_start(r, links, *, count):
    links.meet([links.core])
    down = Scatter("d_", r, links, "cotangent", "hidden", r["hidden"].shape[1] // 3, count)
    down.away()
    down.far()
    links.close()


def attend_back(refs, rows, heads, block):
    span = W + block
    steps = rows // block
    queries, backs, outs, probs = (refs[k] for k in ("queries", "grad_attended", "attended", "probs"))

    def scoped(win, dwin, q, back, out, dq, p, ds, sems):
        loads = [
            pltpu.make_async_copy(a, b, sems.at[k])
            for k, (a, b) in enumerate([(refs["window"], win), (queries, q), (backs, back), (outs, out)])
        ]

        def fetch(i):
            slot = lax.rem(i, 2)
            at = pl.ds(pl.multiple_of(i * block, block), block)
            return pltpu.make_async_copy(probs.at[:, at, :], p.at[slot], sems.at[4 + slot])

        fetch(0).start()
        for load in loads:
            load.start()
        dwin[...] = jnp.zeros_like(dwin)
        for load in loads:
            load.wait()

        def step(i, carry):
            @pl.when(i + 1 < steps)
            def _():
                fetch(i + 1).start()

            fetch(i).wait()
            slot = lax.rem(i, 2)
            at = pl.ds(pl.multiple_of(i * block, block), block)
            window = pl.ds(pl.multiple_of(i * block, block), span)
            for h in range(heads):
                cols = slice(h * HD, (h + 1) * HD)
                g = back[at, cols]
                along = jnp.sum(g.astype(WIDE) * out[at, cols].astype(WIDE), axis=1, keepdims=True)
                grad_probs = right_transposed(g, win[window, HD:])
                ds[h] = (p[slot, h].astype(WIDE) * (grad_probs - along)).astype(LOW)
                part = matmul(ds[h], win[window, :HD]).astype(LOW)
                dq[at, cols] = (part.astype(WIDE) * HD ** (-0.5)).astype(LOW)
            q_all = jnp.concatenate([q[at, h * HD : (h + 1) * HD] for h in range(heads)], axis=0)
            g_all = jnp.concatenate([back[at, h * HD : (h + 1) * HD] for h in range(heads)], axis=0)
            dwin[window, :HD] += rows_product(ds[...].reshape(heads * block, span), q_all)
            dwin[window, HD:] += rows_product(p[slot].reshape(heads * block, span), g_all)
            return carry

        lax.fori_loop(0, steps, step, 0)
        win[...] = dwin[...].astype(LOW)
        stores = [
            pltpu.make_async_copy(win, refs["window_back"], sems.at[0]),
            pltpu.make_async_copy(dq, refs["query_back"], sems.at[1]),
        ]
        for store in stores:
            store.start()
        for store in stores:
            store.wait()

    width = heads * HD
    length = refs["window"].shape[0]
    pl.run_scoped(
        scoped,
        pltpu.VMEM((length, 2 * HD), LOW),
        pltpu.VMEM((length, 2 * HD), WIDE),
        pltpu.VMEM((rows, width), LOW),
        pltpu.VMEM((rows, width), LOW),
        pltpu.VMEM((rows, width), LOW),
        pltpu.VMEM((rows, width), LOW),
        pltpu.VMEM((2, heads, block, span), LOW),
        pltpu.VMEM((heads, block, span), LOW),
        pltpu.SemaphoreType.DMA((6,)),
    )


def window_sum(place, count, hops):
    def body(ins, outs):
        total = ins[0][...].astype(WIDE)
        for by in range(1, hops + 1):
            total = total + jnp.where(place + by < count, ins[by][...].astype(WIDE), 0.0)
        outs[0][...] = total.astype(LOW)

    return body


def pair_sum(ins, outs):
    outs[0][...] = (ins[0][...].astype(WIDE) + ins[1][...].astype(WIDE)).astype(LOW)


def feed_back(r, links, total, *, rows, heads, count):
    half, block = rows // 2, min(256, rows)
    features = r["cotangent"].shape[1]
    width = heads * HD
    third = r["hidden"].shape[1] // 3
    bits = bits_of(count)
    links.meet([links.core, links.chip, links.tp] + [links.along(bit) for bit in bits])
    down = Scatter("d_", r, links, "cotangent", "hidden", third, count, total)
    gate = Scatter("g_", r, links, "second_low", "gate_back", third, count, total)
    up = Scatter("u_", r, links, "second_low", "up_back", third, count, total)
    out = Scatter("o_", r, links, "middle_low", "attended", width, count, total)
    top, bottom = pl.ds(0, half), pl.ds(half, half)

    down.cross()
    job(
        "nn",
        [(r["cotangent"], r["down_full"])],
        [r["gate_back"], r["up_back"]],
        bm=rows,
        bn=third * 3 // 5,
        sub=third // 5,
        extras=[(r["to_gate"], 0), (r["to_up"], 0)],
        finish=finish_hidden,
    )

    def second(part):
        job(
            "nt",
            [(r["gate_back"].at[part], r["gate_full"]), (r["up_back"].at[part], r["up_full"])],
            [r["second"].at[part]],
            bm=half,
            bn=256,
        )
        return links.send(r["second"].at[part], r["second_other"].at[part], links.tp)

    gate.away()
    first = second(top)
    gate.far()
    gate.cross()
    last = second(bottom)
    down.near()
    down.halve(0)
    up.away()
    job("nt", [(r["hidden"].at[top], r["down_full"])], [r["feed0"]], bm=half, bn=512)
    up.far()
    first.wait_recv()
    last.wait_recv()
    feed = links.send(r["feed0"], r["feed_other0"], links.tp)
    down.add(0)
    if len(bits) > 1:
        down.halve(1)
    rows_job(
        middle_back,
        [r["cotangent"], r["middle"], r["second_inverse"], r["second"], r["second_other"]],
        [r["gain_two"], r["small_full"].at[:, pl.ds(width, width)]],
        [r["middle_low"], r["grad_attended"]],
        block,
    )
    out.away()
    out.far()
    if len(bits) > 1:
        down.rest(1)
    gate.wait("arrived")
    feed.wait_recv()
    links.close()


def scores_back(r, links, total, *, rows, heads, hops, count):
    half, block = rows // 2, min(256, rows)
    width = heads * HD
    third = r["up_back"].shape[1] // 3
    links.meet([links.core, links.chip, links.tp] + [{"ctx": lax.rem(links.place + k, count)} for k in range(1, count)])
    gate = Scatter("g_", r, links, "second_low", "gate_back", third, count, total)
    up = Scatter("u_", r, links, "second_low", "up_back", third, count, total)
    query = Scatter("q_", r, links, "first_low", "query_back", width, count, total)
    top, bottom = pl.ds(0, half), pl.ds(half, half)

    up.cross()
    job("nt", [(r["hidden"].at[bottom], r["down_full"])], [r["feed1"]], bm=half, bn=512)
    feed = links.send(r["feed1"], r["feed_other1"], links.tp)
    attend_back(r, rows, heads, block)
    windows = []
    for by in range(1, hops + 1):
        move = links.copy(
            r["window_back"].at[pl.ds((hops - by) * rows, rows)],
            r["window_other"].at[by - 1],
            {"ctx": lax.rem(links.place + count - by, count)},
        )

        @pl.when(links.place >= by)
        def _(move=move):
            move.start()

        windows.append(move)
    job("nt", [(r["query_back"], r["small_full"].at[:, pl.ds(0, width)])], [r["share"]], bm=rows, bn=512)
    feed.wait_recv()
    share = links.send(r["share"].at[top], r["share_other0"], links.tp)
    query.away()
    gate.near()
    gate.halve(0)
    query.far()
    for by in range(1, hops + 1):

        @pl.when(links.place + by < count)
        def _(move=windows[by - 1]):
            move.wait_recv()

    rows_job(
        window_sum(links.place, count, hops),
        [r["window_back"].at[pl.ds(hops * rows, rows)]] + [r["window_other"].at[by] for by in range(hops)],
        [],
        [r["keyval_own"]],
        block,
    )
    up.wait("arrived")
    gate.wait("recv0")
    share.wait_recv()
    for by in range(1, hops + 1):

        @pl.when(links.place >= by)
        def _(move=windows[by - 1]):
            move.wait_send()

    links.close()


def last_sums(r, links, total, *, rows, heads, count):
    half = rows // 2
    block = min(256, half)
    width = heads * HD
    third = r["up_back"].shape[1] // 3
    bits = bits_of(count)
    links.meet([links.core, links.chip, links.tp] + [links.along(bit) for bit in bits])
    gate = Scatter("g_", r, links, "second_low", "gate_back", third, count, total)
    up = Scatter("u_", r, links, "second_low", "up_back", third, count, total)
    out = Scatter("o_", r, links, "middle_low", "attended", width, count, total)
    query = Scatter("q_", r, links, "first_low", "query_back", width, count, total)
    keyval = Scatter("k_", r, links, "first_low", "keyval_back", 2 * HD, count, total)
    parts = (pl.ds(0, half), pl.ds(half, half))

    def finish_source(k):
        part = parts[k]
        rows_job(
            source_back,
            [r[key].at[part] for key in ("tokens", "middle_low", "first_inverse", "share")]
            + [r[f"share_other{k}"], r["keyval_back"].at[part]],
            [r["gain_one"], r["small_full"].at[:, pl.ds(2 * width, 2 * HD)]],
            [r["input_grad"].at[part]],
            block,
        )

    def finish_output(k):
        part = parts[k]
        rows_job(add_feed, [r["middle"].at[part], r[f"feed{k}"], r[f"feed_other{k}"]], [], [r["output"].at[part]], block)

    swap = links.send(r["keyval_own"], r["keyval_other"], links.tp)
    out.cross()
    gate.add(0)
    gate.halve(1)
    share = links.send(r["share"].at[parts[1]], r["share_other1"], links.tp)
    up.near()
    up.halve(0)
    query.cross()
    swap.wait_recv()
    rows_job(pair_sum, [r["keyval_own"], r["keyval_other"]], [], [r["keyval_back"]], block)
    keyval.away()
    out.near()
    out.halve(0)
    keyval.far()
    keyval.cross()
    finish_source(0)
    up.add(0)
    up.halve(1)
    query.near()
    query.halve(0)
    finish_output(0)
    out.add(0)
    out.halve(1)
    keyval.near()
    keyval.halve(0)
    query.add(0)
    query.halve(1)
    share.wait_recv()
    finish_source(1)
    keyval.add(0)
    keyval.halve(1)
    finish_output(1)
    for each in (gate, up, out, query, keyval):
        each.rest(1)
    links.close()


def from_place(array, by):
    count = lax.axis_size("ctx")
    return lax.ppermute(array, "ctx", [(i, i + by) for i in range(count) if i + by < count])


def swap_tp(array):
    return lax.ppermute(array, "tp", [(0, 1), (1, 0)])


def gathered(shard):
    return lax.all_gather(shard, ("fsdp", "ctx"), axis=0, tiled=True)


def on_device(
    tokens,
    query_weight,
    keyval_weight,
    out_weight,
    gate_weight,
    up_weight,
    down_weight,
    first_gain,
    second_gain,
    cotangent,
):
    rows, features = tokens.shape
    width = query_weight.shape[1]
    units = gate_weight.shape[1]
    heads = width // HD
    scale = HD ** (-0.5)
    count = lax.axis_size("ctx")
    hops = min(-(-W // rows), count - 1)
    place = lax.axis_index("ctx")
    block = min(256, rows)

    gains = jnp.pad(jnp.stack([first_gain, second_gain], axis=1), ((0, 0), (0, 126)))
    small_full = gathered(jnp.concatenate([query_weight, out_weight, keyval_weight, gains], axis=1))
    gate_full = gathered(gate_weight)
    up_full = gathered(up_weight)
    down_full = gathered(down_weight)
    query_full = small_full[:, :width]
    keyval_full = small_full[:, 2 * width : 2 * width + 2 * HD]
    both_gains = 1.0 + small_full[:, 2 * width + 2 * HD :][:, :2].astype(WIDE).T
    gain_one, gain_two = both_gains[:1], both_gains[1:]

    source = tokens.astype(WIDE)
    first_inverse = lax.rsqrt(jnp.mean(source * source, axis=-1, keepdims=True) + EPS)
    first_low = (source * first_inverse * gain_one).astype(LOW)
    keyval = matmul(first_low, keyval_full).astype(LOW)
    first_tp = lax.axis_index("tp") == 0
    mine = jnp.where(first_tp, keyval[:, :HD], keyval[:, HD:])
    before = jnp.concatenate([from_place(mine, by) for by in range(hops, 0, -1)])
    theirs = swap_tp(before)
    queries = (matmul(first_low, query_full) * scale).astype(LOW)
    keys = jnp.where(first_tp, before, theirs)
    values = jnp.where(first_tp, theirs, before)
    window = jnp.concatenate([jnp.concatenate([keys, values], axis=1), keyval], axis=0)
    attended, probs = attend(queries, window, place.reshape(1), hops)
    (branch,) = product("nt", attended, small_full, bm=rows, bn=512, width=features, col=1)
    middle, second_low, second_inverse = by_rows(
        add_norm,
        [tokens, branch, swap_tp(branch)],
        [gain_two],
        [(features, LOW), (features, LOW), (128, WIDE)],
        block,
    )
    (gate,) = product("nn", second_low, gate_full, bm=rows, bn=768, width=units, outs=(WIDE,))
    hidden, to_up, to_gate = product(
        "nn",
        second_low,
        up_full,
        bm=rows,
        bn=768,
        width=units,
        sub=256,
        extras=[gate],
        finish=finish_up,
        outs=(LOW, LOW, LOW),
    )

    plain = {
        "gate_back": (rows, units),
        "up_back": (rows, units),
        "second": (rows, features),
        "second_other": (rows, features),
        "feed0": (rows // 2, features),
        "feed1": (rows // 2, features),
        "feed_other0": (rows // 2, features),
        "feed_other1": (rows // 2, features),
        "middle_low": (rows, features),
        "grad_attended": (rows, width),
        "query_back": (rows, width),
        "window_back": window.shape,
        "window_other": (hops, rows, 2 * HD),
        "keyval_own": (rows, 2 * HD),
        "keyval_other": (rows, 2 * HD),
        "keyval_back": (rows, 2 * HD),
        "share": (rows, features),
        "share_other0": (rows // 2, features),
        "share_other1": (rows // 2, features),
        "input_grad": (rows, features),
        "output": (rows, features),
    }
    shapes = {key: jax.ShapeDtypeStruct(shape, LOW) for key, shape in plain.items()}
    for prefix, each in (("d_", units), ("g_", units), ("u_", units), ("o_", width), ("q_", width), ("k_", 2 * HD)):
        shapes |= Scatter.shapes(prefix, features, each, count)
    done = dict(
        cotangent=cotangent,
        down_full=down_full,
        gate_full=gate_full,
        up_full=up_full,
        small_full=small_full,
        to_gate=to_gate,
        to_up=to_up,
        hidden=hidden,
        first_low=first_low,
        second_low=second_low,
        middle=middle,
        second_inverse=second_inverse,
        gain_two=gain_two,
        gain_one=gain_one,
        tokens=tokens,
        first_inverse=jnp.broadcast_to(first_inverse, (rows, 128)),
        queries=queries,
        window=window,
        attended=attended,
        probs=probs,
    )
    total = pltpu.VMEM((features // 4, max(width, units // 3)), WIDE)
    sizes = dict(rows=rows, heads=heads, count=count)
    late = len(bits_of(count)) - 1

    def stage(prefix, *keys):
        return [prefix + key for key in keys]

    def halving(prefix, first, end):
        keys = []
        for k in range(first, end):
            keys += [f"{prefix}recv{k}"] + ([f"{prefix}mid{k}"] if k < late else [])
        return keys

    reads, writes = ["cotangent", "hidden"], stage("d_", "away", "got", "far")
    call = remote_call(
        by_name(functools.partial(down_start, count=count), reads, writes, 0),
        reads,
        [shapes[key] for key in writes],
        [],
        0,
        "down_start",
    )
    done |= zip(writes, call(*[done[key] for key in reads]))

    reads = stage("d_", "got", "far") + ["cotangent", "hidden", "down_full", "gate_full", "up_full", "small_full"]
    reads += ["to_gate", "to_up", "second_low", "middle", "second_inverse", "gain_two", "attended"]
    writes = ["gate_back", "up_back", "second", "second_other", "feed0", "feed_other0", "middle_low"]
    writes += ["grad_attended"] + stage("d_", "arrived", "near") + halving("d_", 0, late + 1)
    writes += stage("g_", "away", "got", "far", "arrived") + stage("u_", "away", "got", "far")
    writes += stage("o_", "away", "got", "far")
    call = remote_call(
        by_name(functools.partial(feed_back, **sizes), reads, writes, 1),
        reads,
        [shapes[key] for key in writes],
        [total],
        1,
        "feed_back",
    )
    done |= zip(writes, call(*[done[key] for key in reads]))

    reads = ["down_full", "hidden", "gate_back", "up_back", "second_low", "first_low", "small_full"]
    reads += ["queries", "window", "attended", "probs", "grad_attended", "u_far", "g_got", "g_arrived"]
    writes = ["feed1", "feed_other1", "u_arrived", "query_back", "window_back", "window_other", "keyval_own"]
    writes += ["share", "share_other0", "g_near", "g_recv0"] + stage("q_", "away", "got", "far")
    call = remote_call(
        by_name(functools.partial(scores_back, hops=hops, **sizes), reads, writes, 1),
        reads,
        [shapes[key] for key in writes],
        [total],
        2,
        "scores_back",
    )
    done |= zip(writes, call(*[done[key] for key in reads]))

    reads = ["gate_back", "up_back", "second_low", "first_low", "middle_low", "attended", "query_back", "keyval_own"]
    reads += ["share", "share_other0", "tokens", "first_inverse", "gain_one", "small_full", "middle"]
    reads += ["feed0", "feed1", "feed_other0", "feed_other1", "u_got", "u_arrived", "g_near", "g_recv0"]
    reads += [prefix + key for prefix in ("o_", "q_") for key in ("got", "far")]
    writes = ["share_other1", "u_near", "keyval_other", "keyval_back", "input_grad", "output"]
    writes += stage("k_", "away", "got", "far")
    writes += [prefix + key for prefix in ("o_", "q_", "k_") for key in ("arrived", "near")]
    writes += [key for key in halving("g_", 0, late + 1) if key != "g_recv0"]
    for prefix in ("u_", "o_", "q_", "k_"):
        writes += halving(prefix, 0, late + 1)
    call = remote_call(
        by_name(functools.partial(last_sums, **sizes), reads, writes, 1),
        reads,
        [shapes[key] for key in writes],
        [total],
        3,
        "last_sums",
    )
    done |= zip(writes, call(*[done[key] for key in reads]))
    down_grad, gate_grad, up_grad, out_grad, query_grad, keyval_grad = (
        scatter_result(prefix, done) for prefix in ("d_", "g_", "u_", "o_", "q_", "k_")
    )

    def row_sum(weight, grad):
        return jnp.sum(weight.astype(WIDE) * grad, axis=1)

    sums = jnp.stack(
        [
            row_sum(query_weight, query_grad),
            row_sum(gate_weight, gate_grad) + row_sum(up_weight, up_grad),
        ]
    )
    sums = sums + swap_tp(sums)
    first_grad = (sums[0] + row_sum(keyval_weight, keyval_grad)) / (1.0 + first_gain.astype(WIDE))
    second_grad = sums[1] / (1.0 + second_gain.astype(WIDE))
    return (
        done["output"],
        done["input_grad"],
        query_grad,
        keyval_grad,
        out_grad,
        gate_grad,
        up_grad,
        down_grad,
        first_grad,
        second_grad,
    )


def solution(mesh):
    rows = P(("fsdp", "ctx"), None)
    split = P(("fsdp", "ctx"), "tp")
    vector = P(("fsdp", "ctx"))
    return jax.shard_map(
        on_device,
        mesh=mesh,
        in_specs=(rows, split, rows, split, split, split, split, vector, vector, rows),
        out_specs=(rows, rows, split, rows, split, split, split, split, vector, vector),
        check_vma=False,
    )
```

```python
import functools

import jax
import jax.numpy as jnp
from jax import lax
from jax.experimental import pallas as pl
from jax.experimental.pallas import tpu as pltpu
from jax.sharding import PartitionSpec as P

HD = 256
W = 2048
EPS = 1e-06
FAR = -1e30
LOW = jnp.bfloat16
WIDE = jnp.float32
CONTRACT_ROWS = (((0,), (0,)), ((), ()))
CONTRACT_LAST = (((1,), (1,)), ((), ()))
VMEM = 60 * 1024 * 1024


def matmul(left, right):
    return jnp.dot(left, right, preferred_element_type=WIDE)


def rows_product(left, right):
    return lax.dot_general(left, right, CONTRACT_ROWS, preferred_element_type=WIDE)


def right_transposed(left, right):
    return lax.dot_general(left, right, CONTRACT_LAST, preferred_element_type=WIDE)


def gelu_parts(gate):
    c = 0.7978845608028654
    inner = c * (gate + 0.044715 * gate * gate * gate)
    t = jnp.tanh(inner)
    value = 0.5 * gate * (1.0 + t)
    slope = 0.5 * (1.0 + t) + 0.5 * gate * (1.0 - t * t) * c * (1.0 + 3 * 0.044715 * gate * gate)
    return value, slope


def attend_kernel(place_ref, q_ref, win_ref, out_ref, probs_ref, bias_ref, *, heads, hops, rows, block):
    span = W + block
    start = pl.program_id(0) * block
    first = (hops - place_ref[0]) * rows - start
    row = lax.broadcasted_iota(jnp.int32, (block, span), 0)
    col = lax.broadcasted_iota(jnp.int32, (block, span), 1)
    live = (col > row) & (col <= row + W) & (col >= first)
    bias_ref[...] = jnp.where(live, 0.0, FAR)
    window = pl.ds(pl.multiple_of(start, block), span)
    for h in range(heads):
        cols = slice(h * HD, (h + 1) * HD)
        scores = right_transposed(q_ref[:, cols], win_ref[window, :HD]) + bias_ref[...]
        top = jnp.max(scores, axis=1, keepdims=True)
        weights = jnp.exp(scores - top)
        total = jnp.sum(weights, axis=1, keepdims=True)
        probs_ref[h] = (weights * (1.0 / total)).astype(LOW)
        out_ref[:, cols] = matmul(probs_ref[h], win_ref[window, HD:]).astype(LOW)


def attend(queries, window, place, hops):
    rows, width = queries.shape
    heads = width // HD
    block = min(256, rows)
    span = W + block
    return pl.pallas_call(
        functools.partial(attend_kernel, heads=heads, hops=hops, rows=rows, block=block),
        grid=(rows // block,),
        in_specs=[
            pl.BlockSpec(memory_space=pltpu.SMEM),
            pl.BlockSpec((block, width), lambda i: (i, 0)),
            pl.BlockSpec(window.shape, lambda i: (0, 0)),
        ],
        out_specs=[
            pl.BlockSpec((block, width), lambda i: (i, 0)),
            pl.BlockSpec((heads, block, span), lambda i: (0, i, 0)),
        ],
        out_shape=[
            jax.ShapeDtypeStruct((rows, width), LOW),
            jax.ShapeDtypeStruct((heads, rows, span), LOW),
        ],
        scratch_shapes=[pltpu.VMEM((block, span), WIDE)],
        compiler_params=pltpu.CompilerParams(vmem_limit_bytes=VMEM),
        name="attend",
    )(place, queries, window)


CONTRACT = {"nn": (((1,), (0,)), ((), ())), "nt": CONTRACT_LAST, "tn": CONTRACT_ROWS}


def products_body(kind, n_pairs, n_extras, finish, sub, keep):
    def body(*refs):
        pairs = [(refs[2 * p], refs[2 * p + 1]) for p in range(n_pairs)]
        extras = refs[2 * n_pairs : 2 * n_pairs + n_extras]
        outs = refs[2 * n_pairs + n_extras :]
        bn = pairs[0][1].shape[0 if kind == "nt" else 1]
        step = sub or bn
        for start in range(0, bn, step):
            cols = slice(start, start + step)
            total = None
            for left, right in pairs:
                part = right[cols, :] if kind == "nt" else right[:, cols]
                term = lax.dot_general(left[...], part, CONTRACT[kind], preferred_element_type=WIDE)
                total = term if total is None else total + term
            given = [e[:, cols].astype(WIDE) for e in extras]
            keep(outs, cols, finish(total, *given) if finish else [sum(given, total)])

    return body


def keep_blocks(outs, cols, results):
    for out, result in zip(outs, results, strict=True):
        out[:, cols] = result.astype(out.dtype)


def products_specs(kind, depths, bm, bn, left_block, right_col):
    specs = []
    for depth in depths:
        if kind == "tn":
            specs.append(pl.BlockSpec((depth, bm), lambda i, j: (0, left_block(i))))
        else:
            specs.append(pl.BlockSpec((bm, depth), lambda i, j: (left_block(i), 0)))
        if kind == "nt":
            specs.append(pl.BlockSpec((bn, depth), lambda i, j: (j, right_col)))
        else:
            specs.append(pl.BlockSpec((depth, bn), lambda i, j: (0, right_col + j)))
    return specs


def product(kind, left, right, *, bm, bn, width, col=0, extras=(), finish=None, outs=(LOW,), sub=0):
    depth = left.shape[1]
    by_block = pl.BlockSpec((bm, bn), lambda i, j: (i, j))
    return pl.pallas_call(
        products_body(kind, 1, len(extras), finish, sub, keep_blocks),
        grid=(left.shape[0] // bm, width // bn),
        in_specs=products_specs(kind, [depth], bm, bn, lambda i: i, col) + [by_block] * len(extras),
        out_specs=[by_block] * len(outs),
        out_shape=[jax.ShapeDtypeStruct((left.shape[0], width), each) for each in outs],
        compiler_params=pltpu.CompilerParams(vmem_limit_bytes=VMEM),
        name="product",
    )(left, right, *extras)


def by_rows(body, sliced, whole, outs, block):
    rows = sliced[0].shape[0]
    n_in = len(sliced) + len(whole)
    specs = [pl.BlockSpec((block, a.shape[1]), lambda i: (i, 0)) for a in sliced]
    specs += [pl.BlockSpec(a.shape, lambda i: (0, 0)) for a in whole]
    return pl.pallas_call(
        lambda *refs: body(refs[:n_in], refs[n_in:]),
        grid=(rows // block,),
        in_specs=specs,
        out_specs=[pl.BlockSpec((block, cols), lambda i: (i, 0)) for cols, _ in outs],
        out_shape=[jax.ShapeDtypeStruct((rows, cols), kind) for cols, kind in outs],
        compiler_params=pltpu.CompilerParams(vmem_limit_bytes=VMEM),
        name="by_rows",
    )(*sliced, *whole)


def add_norm(ins, outs):
    tokens, own, other, gain = ins
    middle = tokens[...].astype(WIDE) + (own[...].astype(WIDE) + other[...].astype(WIDE))
    inverse = lax.rsqrt(jnp.mean(middle * middle, axis=1, keepdims=True) + EPS)
    outs[0][...] = middle.astype(LOW)
    outs[1][...] = (middle * inverse * gain[...]).astype(LOW)
    outs[2][...] = jnp.broadcast_to(inverse, outs[2].shape)


def norm_back(values, grad, gain, inverse):
    scaled = grad * gain
    along = jnp.sum(scaled * values, axis=1, keepdims=True) * (1.0 / values.shape[1])
    return inverse * scaled - values * (inverse * inverse * inverse * along)


def middle_back(ins, outs):
    cotangent, middle, inverse, own, other, gain, out_full = ins
    grad = own[...].astype(WIDE) + other[...].astype(WIDE)
    back = norm_back(middle[...].astype(WIDE), grad, gain[...], inverse[:, :1])
    low = (cotangent[...].astype(WIDE) + back).astype(LOW)
    outs[0][...] = low
    outs[1][...] = matmul(low, out_full[...]).astype(LOW)


def source_back(ins, outs):
    tokens, middle_low, inverse, own, other, keyval_back, gain, keyval_full = ins
    grad = own[...].astype(WIDE) + other[...].astype(WIDE)
    grad = grad + right_transposed(keyval_back[...], keyval_full[...])
    back = norm_back(tokens[...].astype(WIDE), grad, gain[...], inverse[:, :1])
    outs[0][...] = (middle_low[...].astype(WIDE) + back).astype(LOW)


def add_feed(ins, outs):
    middle, own, other = ins
    outs[0][...] = (middle[...].astype(WIDE) + (own[...].astype(WIDE) + other[...].astype(WIDE))).astype(LOW)


def finish_up(upward, gate):
    value, slope = gelu_parts(gate)
    return value * upward, value, slope * upward


def finish_hidden(grad_hidden, to_gate, to_up):
    return grad_hidden * to_gate, grad_hidden * to_up


MESH = pl.DeviceIdType.MESH


class Links:
    def __init__(self, send_sems, recv_sems):
        self.send_sems, self.recv_sems = send_sems, recv_sems
        self.count = 0
        self.open = []
        self.fsdp = lax.axis_index("fsdp")
        self.place = lax.axis_index("ctx")
        self.core = {"fsdp": self.fsdp + 1 - 2 * lax.rem(self.fsdp, 2)}
        self.chip = {"fsdp": lax.rem(self.fsdp + 2, 4)}
        self.tp = {"tp": 1 - lax.axis_index("tp")}

    def block(self, flip):
        return (self.fsdp, self.core["fsdp"], self.chip["fsdp"], 3 - self.fsdp)[flip]

    def along(self, bit):
        return {"ctx": self.place + bit - 2 * bit * lax.rem(lax.div(self.place, bit), 2)}

    def meet(self, partners):
        barrier = pltpu.get_barrier_semaphore()
        for partner in partners:
            pl.semaphore_signal(barrier, inc=1, device_id=partner, device_id_type=MESH)
        pl.semaphore_wait(barrier, len(partners))

    def copy(self, source, target, partner):
        made = pltpu.make_async_remote_copy(
            src_ref=source,
            dst_ref=target,
            send_sem=self.send_sems.at[self.count],
            recv_sem=self.recv_sems.at[self.count],
            device_id=partner,
            device_id_type=MESH,
        )
        self.count += 1
        return made

    def send(self, source, target, partner):
        made = self.copy(source, target, partner)
        made.start()
        self.open.append(made)
        return made

    def close(self):
        for made in self.open:
            made.wait_send()


def job(kind, pairs, outs, *, bm, bn, steps=1, left_block=None, right_col=0, extras=(), finish=None, sub=0):
    depths = [left.shape[0 if kind == "tn" else 1] for left, _ in pairs]
    width = outs[0].shape[1]
    specs = products_specs(kind, depths, bm, bn, left_block or (lambda i: i), right_col)
    specs += [pl.BlockSpec((bm, bn), lambda i, j, at=at: (i + at, j)) for _, at in extras]
    pltpu.emit_pipeline(
        products_body(kind, len(pairs), len(extras), finish, sub, keep_blocks),
        grid=(steps, width // bn),
        in_specs=specs,
        out_specs=[pl.BlockSpec((bm, bn), lambda i, j: (i, j))] * len(outs),
    )(*[ref for pair in pairs for ref in pair], *[ref for ref, _ in extras], *outs)


def rows_job(body, sliced, whole, outs, block):
    n_in = len(sliced) + len(whole)
    specs = [pl.BlockSpec((block, a.shape[1]), lambda i: (i, 0)) for a in sliced]
    specs += [pl.BlockSpec(a.shape, lambda i: (0, 0)) for a in whole]
    pltpu.emit_pipeline(
        lambda *refs: body(refs[:n_in], refs[n_in:]),
        grid=(sliced[0].shape[0] // block,),
        in_specs=specs,
        out_specs=[pl.BlockSpec((block, a.shape[1]), lambda i: (i, 0)) for a in outs],
    )(*sliced, *whole, *outs)


def bits_of(count):
    bits = []
    while 1 << len(bits) < count:
        bits.append(1 << len(bits))
    return bits


def piece_order(count):
    order = [0]
    for bit in reversed(bits_of(count)):
        order = order + [r + bit for r in order]
    return order


class Scatter:
    @staticmethod
    def shapes(prefix, features, width, count):
        part = features // 4
        size = part // count
        out = {"away": (2 * part, width), "got": (2 * part, width), "far": (part, width), "arrived": (part, width)}
        left = count
        out["near"] = (left, size, width)
        for k in range(len(bits_of(count))):
            left //= 2
            out[f"recv{k}"] = (left, size, width)
            if left > 1:
                out[f"mid{k}"] = (left, size, width)
        return {prefix + key: jax.ShapeDtypeStruct(shape, LOW) for key, shape in out.items()}

    def __init__(self, prefix, refs, links, left, right, bn, count, total=None):
        self.refs, self.prefix, self.links, self.bn, self.total = refs, prefix, links, bn, total
        self.pairs = [(refs[left], refs[right])]
        self.part = refs[left].shape[1] // 4
        self.bits = bits_of(count)
        self.moving = {}

    def ref(self, key):
        return self.refs[self.prefix + key]

    def wait(self, key):
        if key in self.moving:
            self.moving.pop(key).wait_recv()

    def away(self):
        core, both = self.links.block(1), self.links.block(3)
        job(
            "tn",
            self.pairs,
            [self.ref("away")],
            bm=self.part,
            bn=self.bn,
            steps=2,
            left_block=lambda i: both + i * (core - both),
        )
        self.moving["got"] = self.links.send(self.ref("away"), self.ref("got"), self.links.core)

    def far(self):
        self.wait("got")
        chip = self.links.block(2)
        job(
            "tn",
            self.pairs,
            [self.ref("far")],
            bm=self.part,
            bn=self.bn,
            left_block=lambda i: chip,
            extras=[(self.ref("got"), 0)],
        )

    def cross(self):
        self.moving["arrived"] = self.links.send(self.ref("far"), self.ref("arrived"), self.links.chip)

    def near(self):
        self.wait("arrived")
        own, place = self.links.block(0), self.links.place
        near, total = self.ref("near"), self.total
        count, size = near.shape[0], near.shape[1]
        order = piece_order(count)

        def keep(outs, cols, results):
            total[:, cols] = results[0]
            for k in range(count):
                at = 0
                for bit in self.bits:
                    mine = lax.rem(lax.div(place, bit), 2)
                    at = at + bit * (1 - mine if order[k] & bit else mine)
                rows = pl.ds(pl.multiple_of(at * size, size), size)
                outs[0][k, :, cols] = total[rows, cols].astype(LOW)

        bm, bn = self.part, self.bn
        left, right = self.pairs[0]
        pltpu.emit_pipeline(
            products_body("tn", 1, 2, None, 0, keep),
            grid=(1, right.shape[1] // bn),
            in_specs=products_specs("tn", [left.shape[0]], bm, bn, lambda i: own, 0)
            + [pl.BlockSpec((bm, bn), lambda i, j: (1, j)), pl.BlockSpec((bm, bn), lambda i, j: (0, j))],
            out_specs=[pl.BlockSpec((count, size, bn), lambda i, j: (0, 0, j))],
        )(left, right, self.ref("got"), self.ref("arrived"), near)

    def kept(self, k):
        return self.ref(f"mid{k - 1}" if k else "near")

    def halve(self, k):
        now = self.kept(k)
        half = now.shape[0] // 2
        self.moving[f"recv{k}"] = self.links.send(
            now.at[pl.ds(half, half)], self.ref(f"recv{k}"), self.links.along(self.bits[k])
        )

    def add(self, k):
        self.wait(f"recv{k}")
        if k + 1 == len(self.bits):
            return
        now, mid = self.kept(k), self.ref(f"mid{k}")
        half, size, bn = mid.shape[0], mid.shape[1], self.bn

        def body(own, other, out):
            out[...] = (own[...].astype(WIDE) + other[...].astype(WIDE)).astype(LOW)

        block = pl.BlockSpec((half, size, bn), lambda j: (0, 0, j))
        pltpu.emit_pipeline(body, grid=(mid.shape[2] // bn,), in_specs=[block, block], out_specs=[block])(
            now, self.ref(f"recv{k}"), mid
        )

    def rest(self, k):
        self.add(k)
        for later in range(k + 1, len(self.bits)):
            self.halve(later)
            self.add(later)


def scatter_result(prefix, arrays):
    last = len(bits_of(arrays[prefix + "near"].shape[0])) - 1
    now = arrays[prefix + (f"mid{last - 1}" if last else "near")]
    return now[0].astype(WIDE) + arrays[prefix + f"recv{last}"][0].astype(WIDE)


def remote_call(kernel, inputs, outputs, scratch, collective_id, name):
    anywhere = pl.BlockSpec(memory_space=pl.ANY)
    sems = pltpu.SemaphoreType.DMA((64,))
    return pl.pallas_call(
        kernel,
        in_specs=[anywhere] * len(inputs),
        out_specs=[anywhere] * len(outputs),
        out_shape=outputs,
        scratch_shapes=scratch + [sems, sems],
        compiler_params=pltpu.CompilerParams(
            collective_id=collective_id, has_side_effects=True, vmem_limit_bytes=VMEM
        ),
        name=name,
    )


def by_name(body, reads, writes, n_scratch):
    names = reads + writes

    def kernel(*refs):
        rest = refs[len(names) :]
        body(dict(zip(names, refs)), Links(rest[-2], rest[-1]), *rest[:n_scratch])

    return kernel


def down_start(r, links, *, count):
    links.meet([links.core])
    down = Scatter("d_", r, links, "cotangent", "hidden", r["hidden"].shape[1] // 3, count)
    down.away()
    down.far()
    links.close()


def attend_back(refs, rows, heads, block):
    span = W + block
    steps = rows // block
    queries, backs, outs, probs = (refs[k] for k in ("queries", "grad_attended", "attended", "probs"))

    def scoped(win, dwin, q, back, out, dq, p, ds, sems):
        loads = [
            pltpu.make_async_copy(a, b, sems.at[k])
            for k, (a, b) in enumerate([(refs["window"], win), (queries, q), (backs, back), (outs, out)])
        ]

        def fetch(i):
            slot = lax.rem(i, 2)
            at = pl.ds(pl.multiple_of(i * block, block), block)
            return pltpu.make_async_copy(probs.at[:, at, :], p.at[slot], sems.at[4 + slot])

        fetch(0).start()
        for load in loads:
            load.start()
        dwin[...] = jnp.zeros_like(dwin)
        for load in loads:
            load.wait()

        def step(i, carry):
            @pl.when(i + 1 < steps)
            def _():
                fetch(i + 1).start()

            fetch(i).wait()
            slot = lax.rem(i, 2)
            at = pl.ds(pl.multiple_of(i * block, block), block)
            window = pl.ds(pl.multiple_of(i * block, block), span)
            for h in range(heads):
                cols = slice(h * HD, (h + 1) * HD)
                g = back[at, cols]
                along = jnp.sum(g.astype(WIDE) * out[at, cols].astype(WIDE), axis=1, keepdims=True)
                grad_probs = right_transposed(g, win[window, HD:])
                ds[h] = (p[slot, h].astype(WIDE) * (grad_probs - along)).astype(LOW)
                part = matmul(ds[h], win[window, :HD]).astype(LOW)
                dq[at, cols] = (part.astype(WIDE) * HD ** (-0.5)).astype(LOW)
            q_all = jnp.concatenate([q[at, h * HD : (h + 1) * HD] for h in range(heads)], axis=0)
            g_all = jnp.concatenate([back[at, h * HD : (h + 1) * HD] for h in range(heads)], axis=0)
            dwin[window, :HD] += rows_product(ds[...].reshape(heads * block, span), q_all)
            dwin[window, HD:] += rows_product(p[slot].reshape(heads * block, span), g_all)
            return carry

        lax.fori_loop(0, steps, step, 0)
        win[...] = dwin[...].astype(LOW)
        stores = [
            pltpu.make_async_copy(win, refs["window_back"], sems.at[0]),
            pltpu.make_async_copy(dq, refs["query_back"], sems.at[1]),
        ]
        for store in stores:
            store.start()
        for store in stores:
            store.wait()

    width = heads * HD
    length = refs["window"].shape[0]
    pl.run_scoped(
        scoped,
        pltpu.VMEM((length, 2 * HD), LOW),
        pltpu.VMEM((length, 2 * HD), WIDE),
        pltpu.VMEM((rows, width), LOW),
        pltpu.VMEM((rows, width), LOW),
        pltpu.VMEM((rows, width), LOW),
        pltpu.VMEM((rows, width), LOW),
        pltpu.VMEM((2, heads, block, span), LOW),
        pltpu.VMEM((heads, block, span), LOW),
        pltpu.SemaphoreType.DMA((6,)),
    )


def window_sum(place, count, hops):
    def body(ins, outs):
        total = ins[0][...].astype(WIDE)
        for by in range(1, hops + 1):
            total = total + jnp.where(place + by < count, ins[by][...].astype(WIDE), 0.0)
        outs[0][...] = total.astype(LOW)

    return body


def pair_sum(ins, outs):
    outs[0][...] = (ins[0][...].astype(WIDE) + ins[1][...].astype(WIDE)).astype(LOW)


def backward(r, links, total, *, rows, heads, hops, count):
    half = rows // 2
    block = min(256, half)
    features = r["cotangent"].shape[1]
    width = heads * HD
    third = r["hidden"].shape[1] // 3
    bits = bits_of(count)
    links.meet([links.core, links.chip, links.tp] + [{"ctx": lax.rem(links.place + k, count)} for k in range(1, count)])
    down = Scatter("d_", r, links, "cotangent", "hidden", third, count, total)
    gate = Scatter("g_", r, links, "second_low", "gate_back", third, count, total)
    up = Scatter("u_", r, links, "second_low", "up_back", third, count, total)
    out = Scatter("o_", r, links, "middle_low", "attended", width, count, total)
    query = Scatter("q_", r, links, "first_low", "query_back", width, count, total)
    keyval = Scatter("k_", r, links, "first_low", "keyval_back", 2 * HD, count, total)
    parts = (pl.ds(0, half), pl.ds(half, half))

    def second(part):
        job(
            "nt",
            [(r["gate_back"].at[part], r["gate_full"]), (r["up_back"].at[part], r["up_full"])],
            [r["second"].at[part]],
            bm=half,
            bn=256,
        )
        return links.send(r["second"].at[part], r["second_other"].at[part], links.tp)

    def feed(k):
        job("nt", [(r["hidden"].at[parts[k]], r["down_full"])], [r[f"feed{k}"]], bm=half, bn=512)
        return links.send(r[f"feed{k}"], r[f"feed_other{k}"], links.tp)

    def share(k):
        return links.send(r["share"].at[parts[k]], r[f"share_other{k}"], links.tp)

    def finish_source(k):
        part = parts[k]
        rows_job(
            source_back,
            [r[key].at[part] for key in ("tokens", "middle_low", "first_inverse", "share")]
            + [r[f"share_other{k}"], r["keyval_back"].at[part]],
            [r["gain_one"], r["small_full"].at[:, pl.ds(2 * width, 2 * HD)]],
            [r["input_grad"].at[part]],
            block,
        )

    def finish_output(k):
        part = parts[k]
        rows_job(add_feed, [r["middle"].at[part], r[f"feed{k}"], r[f"feed_other{k}"]], [], [r["output"].at[part]], block)

    def windows_to(place, by):
        return links.copy(
            r["window_back"].at[pl.ds((hops - by) * rows, rows)],
            r["window_other"].at[by - 1],
            {"ctx": lax.rem(place + count - by, count)},
        )

    down.cross()
    job(
        "nn",
        [(r["cotangent"], r["down_full"])],
        [r["gate_back"], r["up_back"]],
        bm=rows,
        bn=third * 3 // 5,
        sub=third // 5,
        extras=[(r["to_gate"], 0), (r["to_up"], 0)],
        finish=finish_hidden,
    )
    gate.away()
    second0 = second(parts[0])
    gate.far()
    gate.cross()
    second1 = second(parts[1])
    up.away()
    down.near()
    down.halve(0)
    up.far()
    feed0 = feed(0)
    second0.wait_recv()
    second1.wait_recv()
    rows_job(
        middle_back,
        [r["cotangent"], r["middle"], r["second_inverse"], r["second"], r["second_other"]],
        [r["gain_two"], r["small_full"].at[:, pl.ds(width, width)]],
        [r["middle_low"], r["grad_attended"]],
        block,
    )
    feed1 = feed(1)
    gate.wait("arrived")
    up.cross()
    down.add(0)
    if len(bits) > 1:
        down.halve(1)
    attend_back(r, rows, heads, min(256, rows))
    windows = []
    for by in range(1, hops + 1):
        move = windows_to(links.place, by)

        @pl.when(links.place >= by)
        def _(move=move):
            move.start()

        windows.append(move)
    gate.near()
    gate.halve(0)
    out.away()
    job("nt", [(r["query_back"], r["small_full"].at[:, pl.ds(0, width)])], [r["share"]], bm=rows, bn=512)
    share0 = share(0)
    out.far()
    query.away()
    feed0.wait_recv()
    finish_output(0)
    query.far()
    up.wait("arrived")
    out.cross()
    up.near()
    gate.add(0)
    if len(bits) > 1:
        gate.halve(1)
    up.halve(0)
    for by in range(1, hops + 1):

        @pl.when(links.place + by < count)
        def _(move=windows[by - 1]):
            move.wait_recv()

    rows_job(
        window_sum(links.place, count, hops),
        [r["window_back"].at[pl.ds(hops * rows, rows)]] + [r["window_other"].at[by] for by in range(hops)],
        [],
        [r["keyval_own"]],
        block,
    )
    swap = links.send(r["keyval_own"], r["keyval_other"], links.tp)
    share1 = share(1)
    out.near()
    out.halve(0)
    query.cross()
    feed1.wait_recv()
    finish_output(1)
    swap.wait_recv()
    rows_job(pair_sum, [r["keyval_own"], r["keyval_other"]], [], [r["keyval_back"]], block)
    keyval.away()
    up.add(0)
    if len(bits) > 1:
        up.halve(1)
    keyval.far()
    keyval.cross()
    query.near()
    query.halve(0)
    out.add(0)
    if len(bits) > 1:
        out.halve(1)
    share0.wait_recv()
    finish_source(0)
    keyval.near()
    keyval.halve(0)
    query.add(0)
    if len(bits) > 1:
        query.halve(1)
    share1.wait_recv()
    finish_source(1)
    keyval.add(0)
    if len(bits) > 1:
        keyval.halve(1)
        for each in (down, gate, up, out, query, keyval):
            each.rest(1)
    for by in range(1, hops + 1):

        @pl.when(links.place >= by)
        def _(move=windows[by - 1]):
            move.wait_send()

    links.close()


def from_place(array, by):
    count = lax.axis_size("ctx")
    return lax.ppermute(array, "ctx", [(i, i + by) for i in range(count) if i + by < count])


def swap_tp(array):
    return lax.ppermute(array, "tp", [(0, 1), (1, 0)])


def gathered(shard):
    return lax.all_gather(shard, ("fsdp", "ctx"), axis=0, tiled=True)


def on_device(
    tokens,
    query_weight,
    keyval_weight,
    out_weight,
    gate_weight,
    up_weight,
    down_weight,
    first_gain,
    second_gain,
    cotangent,
):
    rows, features = tokens.shape
    width = query_weight.shape[1]
    units = gate_weight.shape[1]
    heads = width // HD
    scale = HD ** (-0.5)
    count = lax.axis_size("ctx")
    hops = min(-(-W // rows), count - 1)
    place = lax.axis_index("ctx")
    block = min(256, rows)

    gains = jnp.pad(jnp.stack([first_gain, second_gain], axis=1), ((0, 0), (0, 126)))
    small_full = gathered(jnp.concatenate([query_weight, out_weight, keyval_weight, gains], axis=1))
    gate_full = gathered(gate_weight)
    up_full = gathered(up_weight)
    down_full = gathered(down_weight)
    query_full = small_full[:, :width]
    keyval_full = small_full[:, 2 * width : 2 * width + 2 * HD]
    both_gains = 1.0 + small_full[:, 2 * width + 2 * HD :][:, :2].astype(WIDE).T
    gain_one, gain_two = both_gains[:1], both_gains[1:]

    source = tokens.astype(WIDE)
    first_inverse = lax.rsqrt(jnp.mean(source * source, axis=-1, keepdims=True) + EPS)
    first_low = (source * first_inverse * gain_one).astype(LOW)
    keyval = matmul(first_low, keyval_full).astype(LOW)
    first_tp = lax.axis_index("tp") == 0
    mine = jnp.where(first_tp, keyval[:, :HD], keyval[:, HD:])
    before = jnp.concatenate([from_place(mine, by) for by in range(hops, 0, -1)])
    theirs = swap_tp(before)
    queries = (matmul(first_low, query_full) * scale).astype(LOW)
    keys = jnp.where(first_tp, before, theirs)
    values = jnp.where(first_tp, theirs, before)
    window = jnp.concatenate([jnp.concatenate([keys, values], axis=1), keyval], axis=0)
    attended, probs = attend(queries, window, place.reshape(1), hops)
    (branch,) = product("nt", attended, small_full, bm=rows, bn=512, width=features, col=1)
    middle, second_low, second_inverse = by_rows(
        add_norm,
        [tokens, branch, swap_tp(branch)],
        [gain_two],
        [(features, LOW), (features, LOW), (128, WIDE)],
        block,
    )
    (gate,) = product("nn", second_low, gate_full, bm=rows, bn=768, width=units, outs=(WIDE,))
    hidden, to_up, to_gate = product(
        "nn",
        second_low,
        up_full,
        bm=rows,
        bn=768,
        width=units,
        sub=256,
        extras=[gate],
        finish=finish_up,
        outs=(LOW, LOW, LOW),
    )

    plain = {
        "gate_back": (rows, units),
        "up_back": (rows, units),
        "second": (rows, features),
        "second_other": (rows, features),
        "feed0": (rows // 2, features),
        "feed1": (rows // 2, features),
        "feed_other0": (rows // 2, features),
        "feed_other1": (rows // 2, features),
        "middle_low": (rows, features),
        "grad_attended": (rows, width),
        "query_back": (rows, width),
        "window_back": window.shape,
        "window_other": (hops, rows, 2 * HD),
        "keyval_own": (rows, 2 * HD),
        "keyval_other": (rows, 2 * HD),
        "keyval_back": (rows, 2 * HD),
        "share": (rows, features),
        "share_other0": (rows // 2, features),
        "share_other1": (rows // 2, features),
        "input_grad": (rows, features),
        "output": (rows, features),
    }
    shapes = {key: jax.ShapeDtypeStruct(shape, LOW) for key, shape in plain.items()}
    for prefix, each in (("d_", units), ("g_", units), ("u_", units), ("o_", width), ("q_", width), ("k_", 2 * HD)):
        shapes |= Scatter.shapes(prefix, features, each, count)
    done = dict(
        cotangent=cotangent,
        down_full=down_full,
        gate_full=gate_full,
        up_full=up_full,
        small_full=small_full,
        to_gate=to_gate,
        to_up=to_up,
        hidden=hidden,
        first_low=first_low,
        second_low=second_low,
        middle=middle,
        second_inverse=second_inverse,
        gain_two=gain_two,
        gain_one=gain_one,
        tokens=tokens,
        first_inverse=jnp.broadcast_to(first_inverse, (rows, 128)),
        queries=queries,
        window=window,
        attended=attended,
        probs=probs,
    )
    total = pltpu.VMEM((features // 4, max(width, units // 3)), WIDE)
    sizes = dict(rows=rows, heads=heads, count=count)
    late = len(bits_of(count)) - 1

    def stage(prefix, *keys):
        return [prefix + key for key in keys]

    def halving(prefix, first, end):
        keys = []
        for k in range(first, end):
            keys += [f"{prefix}recv{k}"] + ([f"{prefix}mid{k}"] if k < late else [])
        return keys

    reads, writes = ["cotangent", "hidden"], stage("d_", "away", "got", "far")
    call = remote_call(
        by_name(functools.partial(down_start, count=count), reads, writes, 0),
        reads,
        [shapes[key] for key in writes],
        [],
        0,
        "down_start",
    )
    done |= zip(writes, call(*[done[key] for key in reads]))

    reads = stage("d_", "got", "far") + ["cotangent", "hidden", "down_full", "gate_full", "up_full", "small_full"]
    reads += ["to_gate", "to_up", "first_low", "second_low", "middle", "tokens", "first_inverse", "second_inverse"]
    reads += ["gain_one", "gain_two", "attended", "queries", "window", "probs"]
    writes = list(plain) + stage("d_", "arrived", "near") + halving("d_", 0, late + 1)
    for prefix in ("g_", "u_", "o_", "q_", "k_"):
        writes += stage(prefix, "away", "got", "far", "arrived", "near") + halving(prefix, 0, late + 1)
    call = remote_call(
        by_name(functools.partial(backward, hops=hops, **sizes), reads, writes, 1),
        reads,
        [shapes[key] for key in writes],
        [total],
        1,
        "backward",
    )
    done |= zip(writes, call(*[done[key] for key in reads]))
    down_grad, gate_grad, up_grad, out_grad, query_grad, keyval_grad = (
        scatter_result(prefix, done) for prefix in ("d_", "g_", "u_", "o_", "q_", "k_")
    )

    def row_sum(weight, grad):
        return jnp.sum(weight.astype(WIDE) * grad, axis=1)

    sums = jnp.stack(
        [
            row_sum(query_weight, query_grad),
            row_sum(gate_weight, gate_grad) + row_sum(up_weight, up_grad),
        ]
    )
    sums = sums + swap_tp(sums)
    first_grad = (sums[0] + row_sum(keyval_weight, keyval_grad)) / (1.0 + first_gain.astype(WIDE))
    second_grad = sums[1] / (1.0 + second_gain.astype(WIDE))
    return (
        done["output"],
        done["input_grad"],
        query_grad,
        keyval_grad,
        out_grad,
        gate_grad,
        up_grad,
        down_grad,
        first_grad,
        second_grad,
    )


def solution(mesh):
    rows = P(("fsdp", "ctx"), None)
    split = P(("fsdp", "ctx"), "tp")
    vector = P(("fsdp", "ctx"))
    return jax.shard_map(
        on_device,
        mesh=mesh,
        in_specs=(rows, split, rows, split, split, split, split, vector, vector, rows),
        out_specs=(rows, rows, split, rows, split, split, split, split, vector, vector),
        check_vma=False,
    )
```

```python
import functools

import jax
import jax.numpy as jnp
from jax import lax
from jax.experimental import pallas as pl
from jax.experimental.pallas import tpu as pltpu
from jax.sharding import PartitionSpec as P

HD = 256
W = 2048
EPS = 1e-06
FAR = -1e30
LOW = jnp.bfloat16
WIDE = jnp.float32
CONTRACT_ROWS = (((0,), (0,)), ((), ()))
CONTRACT_LAST = (((1,), (1,)), ((), ()))
VMEM = 60 * 1024 * 1024


def matmul(left, right):
    return jnp.dot(left, right, preferred_element_type=WIDE)


def rows_product(left, right):
    return lax.dot_general(left, right, CONTRACT_ROWS, preferred_element_type=WIDE)


def right_transposed(left, right):
    return lax.dot_general(left, right, CONTRACT_LAST, preferred_element_type=WIDE)


def gelu_parts(gate):
    c = 0.7978845608028654
    inner = c * (gate + 0.044715 * gate * gate * gate)
    t = jnp.tanh(inner)
    value = 0.5 * gate * (1.0 + t)
    slope = 0.5 * (1.0 + t) + 0.5 * gate * (1.0 - t * t) * c * (1.0 + 3 * 0.044715 * gate * gate)
    return value, slope


def attend_kernel(place_ref, q_ref, win_ref, out_ref, probs_ref, bias_ref, *, heads, hops, rows, block):
    span = W + block
    start = pl.program_id(0) * block
    first = (hops - place_ref[0]) * rows - start
    row = lax.broadcasted_iota(jnp.int32, (block, span), 0)
    col = lax.broadcasted_iota(jnp.int32, (block, span), 1)
    live = (col > row) & (col <= row + W) & (col >= first)
    bias_ref[...] = jnp.where(live, 0.0, FAR)
    window = pl.ds(pl.multiple_of(start, block), span)
    for h in range(heads):
        cols = slice(h * HD, (h + 1) * HD)
        scores = right_transposed(q_ref[:, cols], win_ref[window, :HD]) + bias_ref[...]
        top = jnp.max(scores, axis=1, keepdims=True)
        weights = jnp.exp(scores - top)
        total = jnp.sum(weights, axis=1, keepdims=True)
        probs_ref[h] = (weights * (1.0 / total)).astype(LOW)
        out_ref[:, cols] = matmul(probs_ref[h], win_ref[window, HD:]).astype(LOW)


def attend(queries, window, place, hops):
    rows, width = queries.shape
    heads = width // HD
    block = min(256, rows)
    span = W + block
    return pl.pallas_call(
        functools.partial(attend_kernel, heads=heads, hops=hops, rows=rows, block=block),
        grid=(rows // block,),
        in_specs=[
            pl.BlockSpec(memory_space=pltpu.SMEM),
            pl.BlockSpec((block, width), lambda i: (i, 0)),
            pl.BlockSpec(window.shape, lambda i: (0, 0)),
        ],
        out_specs=[
            pl.BlockSpec((block, width), lambda i: (i, 0)),
            pl.BlockSpec((heads, block, span), lambda i: (0, i, 0)),
        ],
        out_shape=[
            jax.ShapeDtypeStruct((rows, width), LOW),
            jax.ShapeDtypeStruct((heads, rows, span), LOW),
        ],
        scratch_shapes=[pltpu.VMEM((block, span), WIDE)],
        compiler_params=pltpu.CompilerParams(vmem_limit_bytes=VMEM),
        name="attend",
    )(place, queries, window)


CONTRACT = {"nn": (((1,), (0,)), ((), ())), "nt": CONTRACT_LAST, "tn": CONTRACT_ROWS}


def products_body(kind, n_pairs, n_extras, finish, sub, keep):
    def body(*refs):
        pairs = [(refs[2 * p], refs[2 * p + 1]) for p in range(n_pairs)]
        extras = refs[2 * n_pairs : 2 * n_pairs + n_extras]
        outs = refs[2 * n_pairs + n_extras :]
        bn = pairs[0][1].shape[0 if kind == "nt" else 1]
        step = sub or bn
        for start in range(0, bn, step):
            cols = slice(start, start + step)
            total = None
            for left, right in pairs:
                part = right[cols, :] if kind == "nt" else right[:, cols]
                term = lax.dot_general(left[...], part, CONTRACT[kind], preferred_element_type=WIDE)
                total = term if total is None else total + term
            given = [e[:, cols].astype(WIDE) for e in extras]
            keep(outs, cols, finish(total, *given) if finish else [sum(given, total)])

    return body


def keep_blocks(outs, cols, results):
    for out, result in zip(outs, results, strict=True):
        out[:, cols] = result.astype(out.dtype)


def products_specs(kind, depths, bm, bn, left_block, right_col):
    specs = []
    for depth in depths:
        if kind == "tn":
            specs.append(pl.BlockSpec((depth, bm), lambda i, j: (0, left_block(i))))
        else:
            specs.append(pl.BlockSpec((bm, depth), lambda i, j: (left_block(i), 0)))
        if kind == "nt":
            specs.append(pl.BlockSpec((bn, depth), lambda i, j: (j, right_col)))
        else:
            specs.append(pl.BlockSpec((depth, bn), lambda i, j: (0, right_col + j)))
    return specs


def product(kind, left, right, *, bm, bn, width, col=0, extras=(), finish=None, outs=(LOW,), sub=0):
    depth = left.shape[1]
    by_block = pl.BlockSpec((bm, bn), lambda i, j: (i, j))
    return pl.pallas_call(
        products_body(kind, 1, len(extras), finish, sub, keep_blocks),
        grid=(left.shape[0] // bm, width // bn),
        in_specs=products_specs(kind, [depth], bm, bn, lambda i: i, col) + [by_block] * len(extras),
        out_specs=[by_block] * len(outs),
        out_shape=[jax.ShapeDtypeStruct((left.shape[0], width), each) for each in outs],
        compiler_params=pltpu.CompilerParams(vmem_limit_bytes=VMEM),
        name="product",
    )(left, right, *extras)


def by_rows(body, sliced, whole, outs, block):
    rows = sliced[0].shape[0]
    n_in = len(sliced) + len(whole)
    specs = [pl.BlockSpec((block, a.shape[1]), lambda i: (i, 0)) for a in sliced]
    specs += [pl.BlockSpec(a.shape, lambda i: (0, 0)) for a in whole]
    return pl.pallas_call(
        lambda *refs: body(refs[:n_in], refs[n_in:]),
        grid=(rows // block,),
        in_specs=specs,
        out_specs=[pl.BlockSpec((block, cols), lambda i: (i, 0)) for cols, _ in outs],
        out_shape=[jax.ShapeDtypeStruct((rows, cols), kind) for cols, kind in outs],
        compiler_params=pltpu.CompilerParams(vmem_limit_bytes=VMEM),
        name="by_rows",
    )(*sliced, *whole)


def add_norm(ins, outs):
    tokens, own, other, gain = ins
    middle = tokens[...].astype(WIDE) + (own[...].astype(WIDE) + other[...].astype(WIDE))
    inverse = lax.rsqrt(jnp.mean(middle * middle, axis=1, keepdims=True) + EPS)
    outs[0][...] = middle.astype(LOW)
    outs[1][...] = (middle * inverse * gain[...]).astype(LOW)
    outs[2][...] = jnp.broadcast_to(inverse, outs[2].shape)


def norm_back(values, grad, gain, inverse):
    scaled = grad * gain
    along = jnp.sum(scaled * values, axis=1, keepdims=True) * (1.0 / values.shape[1])
    return inverse * scaled - values * (inverse * inverse * inverse * along)


def middle_back(ins, outs):
    cotangent, middle, inverse, own, other, gain, out_full = ins
    grad = own[...].astype(WIDE) + other[...].astype(WIDE)
    back = norm_back(middle[...].astype(WIDE), grad, gain[...], inverse[:, :1])
    low = (cotangent[...].astype(WIDE) + back).astype(LOW)
    outs[0][...] = low
    outs[1][...] = matmul(low, out_full[...]).astype(LOW)


def source_back(ins, outs):
    tokens, middle_low, inverse, own, other, keyval_back, gain, keyval_full = ins
    grad = own[...].astype(WIDE) + other[...].astype(WIDE)
    grad = grad + right_transposed(keyval_back[...], keyval_full[...])
    back = norm_back(tokens[...].astype(WIDE), grad, gain[...], inverse[:, :1])
    outs[0][...] = (middle_low[...].astype(WIDE) + back).astype(LOW)


def add_feed(ins, outs):
    middle, own, other = ins
    outs[0][...] = (middle[...].astype(WIDE) + (own[...].astype(WIDE) + other[...].astype(WIDE))).astype(LOW)


def finish_up(upward, gate):
    value, slope = gelu_parts(gate)
    return value * upward, value, slope * upward


def finish_hidden(grad_hidden, to_gate, to_up):
    return grad_hidden * to_gate, grad_hidden * to_up


MESH = pl.DeviceIdType.MESH


class Links:
    def __init__(self, send_sems, recv_sems):
        self.send_sems, self.recv_sems = send_sems, recv_sems
        self.count = 0
        self.open = []
        self.fsdp = lax.axis_index("fsdp")
        self.place = lax.axis_index("ctx")
        self.core = {"fsdp": self.fsdp + 1 - 2 * lax.rem(self.fsdp, 2)}
        self.chip = {"fsdp": lax.rem(self.fsdp + 2, 4)}
        self.tp = {"tp": 1 - lax.axis_index("tp")}

    def block(self, flip):
        return (self.fsdp, self.core["fsdp"], self.chip["fsdp"], 3 - self.fsdp)[flip]

    def along(self, bit):
        return {"ctx": self.place + bit - 2 * bit * lax.rem(lax.div(self.place, bit), 2)}

    def meet(self, partners):
        barrier = pltpu.get_barrier_semaphore()
        for partner in partners:
            pl.semaphore_signal(barrier, inc=1, device_id=partner, device_id_type=MESH)
        pl.semaphore_wait(barrier, len(partners))

    def copy(self, source, target, partner):
        made = pltpu.make_async_remote_copy(
            src_ref=source,
            dst_ref=target,
            send_sem=self.send_sems.at[self.count],
            recv_sem=self.recv_sems.at[self.count],
            device_id=partner,
            device_id_type=MESH,
        )
        self.count += 1
        return made

    def send(self, source, target, partner):
        made = self.copy(source, target, partner)
        made.start()
        self.open.append(made)
        return made

    def close(self):
        for made in self.open:
            made.wait_send()


def job(kind, pairs, outs, *, bm, bn, steps=1, left_block=None, right_col=0, extras=(), finish=None, sub=0):
    depths = [left.shape[0 if kind == "tn" else 1] for left, _ in pairs]
    width = outs[0].shape[1]
    specs = products_specs(kind, depths, bm, bn, left_block or (lambda i: i), right_col)
    specs += [pl.BlockSpec((bm, bn), lambda i, j, at=at: (i + at, j)) for _, at in extras]
    pltpu.emit_pipeline(
        products_body(kind, len(pairs), len(extras), finish, sub, keep_blocks),
        grid=(steps, width // bn),
        in_specs=specs,
        out_specs=[pl.BlockSpec((bm, bn), lambda i, j: (i, j))] * len(outs),
    )(*[ref for pair in pairs for ref in pair], *[ref for ref, _ in extras], *outs)


def rows_job(body, sliced, whole, outs, block):
    n_in = len(sliced) + len(whole)
    specs = [pl.BlockSpec((block, a.shape[1]), lambda i: (i, 0)) for a in sliced]
    specs += [pl.BlockSpec(a.shape, lambda i: (0, 0)) for a in whole]
    pltpu.emit_pipeline(
        lambda *refs: body(refs[:n_in], refs[n_in:]),
        grid=(sliced[0].shape[0] // block,),
        in_specs=specs,
        out_specs=[pl.BlockSpec((block, a.shape[1]), lambda i: (i, 0)) for a in outs],
    )(*sliced, *whole, *outs)


def bits_of(count):
    bits = []
    while 1 << len(bits) < count:
        bits.append(1 << len(bits))
    return bits


def piece_order(count):
    order = [0]
    for bit in reversed(bits_of(count)):
        order = order + [r + bit for r in order]
    return order


class Scatter:
    add_last = False

    @staticmethod
    def shapes(prefix, features, width, count):
        part = features // 4
        size = part // count
        out = {"away": (2 * part, width), "got": (2 * part, width), "far": (part, width), "arrived": (part, width)}
        left = count
        out["near"] = (left, size, width)
        for k in range(len(bits_of(count))):
            left //= 2
            out[f"recv{k}"] = (left, size, width)
            if left > 1:
                out[f"mid{k}"] = (left, size, width)
        return {prefix + key: jax.ShapeDtypeStruct(shape, LOW) for key, shape in out.items()}

    def __init__(self, prefix, refs, links, left, right, bn, count, total=None):
        self.refs, self.prefix, self.links, self.bn, self.total = refs, prefix, links, bn, total
        self.pairs = [(refs[left], refs[right])]
        self.part = refs[left].shape[1] // 4
        self.bits = bits_of(count)
        self.moving = {}

    def ref(self, key):
        return self.refs[self.prefix + key]

    def wait(self, key):
        if key in self.moving:
            self.moving.pop(key).wait_recv()

    def away(self):
        core, both = self.links.block(1), self.links.block(3)
        job(
            "tn",
            self.pairs,
            [self.ref("away")],
            bm=self.part,
            bn=self.bn,
            steps=2,
            left_block=lambda i: both + i * (core - both),
        )
        self.moving["got"] = self.links.send(self.ref("away"), self.ref("got"), self.links.core)

    def far(self):
        self.wait("got")
        chip = self.links.block(2)
        job(
            "tn",
            self.pairs,
            [self.ref("far")],
            bm=self.part,
            bn=self.bn,
            left_block=lambda i: chip,
            extras=[(self.ref("got"), 0)],
        )

    def cross(self):
        self.moving["arrived"] = self.links.send(self.ref("far"), self.ref("arrived"), self.links.chip)

    def near(self):
        self.wait("arrived")
        own = self.links.block(0)
        extras = [pl.BlockSpec((self.part, self.bn), lambda i, j: (1, j)), pl.BlockSpec((self.part, self.bn), lambda i, j: (0, j))]
        self.make_near(1, lambda i: own, [self.ref("got"), self.ref("arrived")], extras)

    def make_near(self, steps, left_block, given, extras):
        place = self.links.place
        near, total = self.ref("near"), self.total
        count = near.shape[0]
        size = self.part // count
        order = piece_order(count)

        def keep(outs, cols, results):
            total[:, cols] = results[0]
            for k in range(count):
                at = 0
                for bit in self.bits:
                    mine = lax.rem(lax.div(place, bit), 2)
                    at = at + bit * (1 - mine if order[k] & bit else mine)
                rows = pl.ds(pl.multiple_of(at * size, size), size)
                outs[0][k, :, cols] = total[rows, cols].astype(LOW)

        bm, bn = self.part, self.bn
        left, right = self.pairs[0]
        pltpu.emit_pipeline(
            products_body("tn", 1, len(given), None, 0, keep),
            grid=(steps, right.shape[1] // bn),
            in_specs=products_specs("tn", [left.shape[0]], bm, bn, left_block, 0) + extras,
            out_specs=[pl.BlockSpec((count, size, bn), lambda i, j: (0, i, j))],
        )(left, right, *given, near)

    def kept(self, k):
        return self.ref(f"mid{k - 1}" if k else "near")

    def halve(self, k):
        now = self.kept(k)
        half = now.shape[0] // 2
        self.moving[f"recv{k}"] = self.links.send(
            now.at[pl.ds(half, half)], self.ref(f"recv{k}"), self.links.along(self.bits[k])
        )

    def add(self, k):
        self.wait(f"recv{k}")
        if k + 1 == len(self.bits) and not self.add_last:
            return
        now, mid = self.kept(k), self.ref(f"mid{k}")
        half, size, bn = mid.shape[0], mid.shape[1], self.bn

        def body(own, other, out):
            out[...] = (own[...].astype(WIDE) + other[...].astype(WIDE)).astype(LOW)

        block = pl.BlockSpec((half, size, bn), lambda j: (0, 0, j))
        pltpu.emit_pipeline(body, grid=(mid.shape[2] // bn,), in_specs=[block, block], out_specs=[block])(
            now, self.ref(f"recv{k}"), mid
        )

    def rest(self, k):
        self.add(k)
        for later in range(k + 1, len(self.bits)):
            self.halve(later)
            self.add(later)


class ScatterFirst(Scatter):
    add_last = True

    @staticmethod
    def shapes(prefix, features, width, count):
        part = features // 4
        size = part // count
        out = {"away": (2 * part, width), "got": (2 * part, width), "near": (count, 2 * size, width)}
        left = count
        for k in range(len(bits_of(count))):
            left //= 2
            out[f"recv{k}"] = out[f"mid{k}"] = (left, 2 * size, width)
        out["arrived"] = (size, width)
        return {prefix + key: jax.ShapeDtypeStruct(shape, LOW) for key, shape in out.items()}

    def near(self):
        self.wait("got")
        chip, own = self.links.block(2), self.links.block(0)
        extras = [pl.BlockSpec((self.part, self.bn), lambda i, j: (i, j))]
        self.make_near(2, lambda i: chip + i * (own - chip), [self.ref("got")], extras)

    def cross(self):
        last = self.kept(len(self.bits))
        size = last.shape[1] // 2
        self.moving["arrived"] = self.links.send(
            last.at[0, pl.ds(0, size)], self.ref("arrived"), self.links.chip
        )


def scatter_result(prefix, arrays):
    last = len(bits_of(arrays[prefix + "near"].shape[0])) - 1
    now = arrays[prefix + (f"mid{last - 1}" if last else "near")]
    return now[0].astype(WIDE) + arrays[prefix + f"recv{last}"][0].astype(WIDE)


def scatter_first_result(prefix, arrays):
    size = arrays[prefix + "arrived"].shape[0]
    last = len(bits_of(arrays[prefix + "near"].shape[0])) - 1
    return arrays[prefix + f"mid{last}"][0, size:].astype(WIDE) + arrays[prefix + "arrived"].astype(WIDE)


def remote_call(kernel, inputs, outputs, scratch, collective_id, name):
    anywhere = pl.BlockSpec(memory_space=pl.ANY)
    sems = pltpu.SemaphoreType.DMA((64,))
    return pl.pallas_call(
        kernel,
        in_specs=[anywhere] * len(inputs),
        out_specs=[anywhere] * len(outputs),
        out_shape=outputs,
        scratch_shapes=scratch + [sems, sems],
        compiler_params=pltpu.CompilerParams(
            collective_id=collective_id, has_side_effects=True, vmem_limit_bytes=VMEM
        ),
        name=name,
    )


def by_name(body, reads, writes, n_scratch):
    names = reads + writes

    def kernel(*refs):
        rest = refs[len(names) :]
        body(dict(zip(names, refs)), Links(rest[-2], rest[-1]), *rest[:n_scratch])

    return kernel


def down_start(r, links, total, *, count):
    links.meet([links.core])
    down = ScatterFirst("d_", r, links, "cotangent", "hidden", r["hidden"].shape[1] // 3, count, total)
    down.away()
    down.near()
    links.close()


def attend_back(refs, rows, heads, block):
    span = W + block
    steps = rows // block
    queries, backs, outs, probs = (refs[k] for k in ("queries", "grad_attended", "attended", "probs"))

    def scoped(win, dwin, q, back, out, dq, p, ds, sems):
        loads = [
            pltpu.make_async_copy(a, b, sems.at[k])
            for k, (a, b) in enumerate([(refs["window"], win), (queries, q), (backs, back), (outs, out)])
        ]

        def fetch(i):
            slot = lax.rem(i, 2)
            at = pl.ds(pl.multiple_of(i * block, block), block)
            return pltpu.make_async_copy(probs.at[:, at, :], p.at[slot], sems.at[4 + slot])

        fetch(0).start()
        for load in loads:
            load.start()
        dwin[...] = jnp.zeros_like(dwin)
        for load in loads:
            load.wait()

        def step(i, carry):
            @pl.when(i + 1 < steps)
            def _():
                fetch(i + 1).start()

            fetch(i).wait()
            slot = lax.rem(i, 2)
            at = pl.ds(pl.multiple_of(i * block, block), block)
            window = pl.ds(pl.multiple_of(i * block, block), span)
            for h in range(heads):
                cols = slice(h * HD, (h + 1) * HD)
                g = back[at, cols]
                along = jnp.sum(g.astype(WIDE) * out[at, cols].astype(WIDE), axis=1, keepdims=True)
                grad_probs = right_transposed(g, win[window, HD:])
                ds[h] = (p[slot, h].astype(WIDE) * (grad_probs - along)).astype(LOW)
                part = matmul(ds[h], win[window, :HD]).astype(LOW)
                dq[at, cols] = (part.astype(WIDE) * HD ** (-0.5)).astype(LOW)
            q_all = jnp.concatenate([q[at, h * HD : (h + 1) * HD] for h in range(heads)], axis=0)
            g_all = jnp.concatenate([back[at, h * HD : (h + 1) * HD] for h in range(heads)], axis=0)
            dwin[window, :HD] += rows_product(ds[...].reshape(heads * block, span), q_all)
            dwin[window, HD:] += rows_product(p[slot].reshape(heads * block, span), g_all)
            return carry

        lax.fori_loop(0, steps, step, 0)
        win[...] = dwin[...].astype(LOW)
        stores = [
            pltpu.make_async_copy(win, refs["window_back"], sems.at[0]),
            pltpu.make_async_copy(dq, refs["query_back"], sems.at[1]),
        ]
        for store in stores:
            store.start()
        for store in stores:
            store.wait()

    width = heads * HD
    length = refs["window"].shape[0]
    pl.run_scoped(
        scoped,
        pltpu.VMEM((length, 2 * HD), LOW),
        pltpu.VMEM((length, 2 * HD), WIDE),
        pltpu.VMEM((rows, width), LOW),
        pltpu.VMEM((rows, width), LOW),
        pltpu.VMEM((rows, width), LOW),
        pltpu.VMEM((rows, width), LOW),
        pltpu.VMEM((2, heads, block, span), LOW),
        pltpu.VMEM((heads, block, span), LOW),
        pltpu.SemaphoreType.DMA((6,)),
    )


def window_sum(place, count, hops):
    def body(ins, outs):
        total = ins[0][...].astype(WIDE)
        for by in range(1, hops + 1):
            total = total + jnp.where(place + by < count, ins[by][...].astype(WIDE), 0.0)
        outs[0][...] = total.astype(LOW)

    return body


def pair_sum(ins, outs):
    outs[0][...] = (ins[0][...].astype(WIDE) + ins[1][...].astype(WIDE)).astype(LOW)


def backward(r, links, total, *, rows, heads, hops, count):
    half = rows // 2
    block = min(256, half)
    features = r["cotangent"].shape[1]
    width = heads * HD
    third = r["hidden"].shape[1] // 3
    bits = bits_of(count)
    links.meet([links.core, links.chip, links.tp] + [{"ctx": lax.rem(links.place + k, count)} for k in range(1, count)])
    down = ScatterFirst("d_", r, links, "cotangent", "hidden", third, count, total)
    gate = Scatter("g_", r, links, "second_low", "gate_back", third, count, total)
    up = Scatter("u_", r, links, "second_low", "up_back", third, count, total)
    out = Scatter("o_", r, links, "middle_low", "attended", width, count, total)
    query = Scatter("q_", r, links, "first_low", "query_back", width, count, total)
    keyval = Scatter("k_", r, links, "first_low", "keyval_back", 2 * HD, count, total)
    parts = (pl.ds(0, half), pl.ds(half, half))

    def second(part):
        job(
            "nt",
            [(r["gate_back"].at[part], r["gate_full"]), (r["up_back"].at[part], r["up_full"])],
            [r["second"].at[part]],
            bm=half,
            bn=256,
        )
        return links.send(r["second"].at[part], r["second_other"].at[part], links.tp)

    def feed(k):
        job("nt", [(r["hidden"].at[parts[k]], r["down_full"])], [r[f"feed{k}"]], bm=half, bn=512)
        return links.send(r[f"feed{k}"], r[f"feed_other{k}"], links.tp)

    def share(k):
        return links.send(r["share"].at[parts[k]], r[f"share_other{k}"], links.tp)

    def finish_source(k):
        part = parts[k]
        rows_job(
            source_back,
            [r[key].at[part] for key in ("tokens", "middle_low", "first_inverse", "share")]
            + [r[f"share_other{k}"], r["keyval_back"].at[part]],
            [r["gain_one"], r["small_full"].at[:, pl.ds(2 * width, 2 * HD)]],
            [r["input_grad"].at[part]],
            block,
        )

    def finish_output(k):
        part = parts[k]
        rows_job(add_feed, [r["middle"].at[part], r[f"feed{k}"], r[f"feed_other{k}"]], [], [r["output"].at[part]], block)

    def windows_to(place, by):
        return links.copy(
            r["window_back"].at[pl.ds((hops - by) * rows, rows)],
            r["window_other"].at[by - 1],
            {"ctx": lax.rem(place + count - by, count)},
        )

    down.halve(0)
    job(
        "nn",
        [(r["cotangent"], r["down_full"])],
        [r["gate_back"], r["up_back"]],
        bm=rows,
        bn=third * 3 // 5,
        sub=third // 5,
        extras=[(r["to_gate"], 0), (r["to_up"], 0)],
        finish=finish_hidden,
    )
    gate.away()
    second0 = second(parts[0])
    gate.far()
    gate.cross()
    second1 = second(parts[1])
    up.away()
    down.add(0)
    if len(bits) > 1:
        down.halve(1)
    up.far()
    feed1 = feed(1)
    feed0 = feed(0)
    up.cross()
    gate.near()
    gate.halve(0)
    second0.wait_recv()
    second1.wait_recv()
    rows_job(
        middle_back,
        [r["cotangent"], r["middle"], r["second_inverse"], r["second"], r["second_other"]],
        [r["gain_two"], r["small_full"].at[:, pl.ds(width, width)]],
        [r["middle_low"], r["grad_attended"]],
        block,
    )
    attend_back(r, rows, heads, min(256, rows))
    windows = []
    for by in range(1, hops + 1):
        move = windows_to(links.place, by)

        @pl.when(links.place >= by)
        def _(move=move):
            move.start()

        windows.append(move)
    out.away()
    out.far()
    gate.add(0)
    if len(bits) > 1:
        gate.halve(1)
    job("nt", [(r["query_back"], r["small_full"].at[:, pl.ds(0, width)])], [r["share"]], bm=rows, bn=512)
    share0 = share(0)
    up.near()
    up.halve(0)
    out.cross()
    query.away()
    query.far()
    query.cross()
    if len(bits) > 1:
        down.rest(1)
    down.cross()
    for by in range(1, hops + 1):

        @pl.when(links.place + by < count)
        def _(move=windows[by - 1]):
            move.wait_recv()

    rows_job(
        window_sum(links.place, count, hops),
        [r["window_back"].at[pl.ds(hops * rows, rows)]] + [r["window_other"].at[by] for by in range(hops)],
        [],
        [r["keyval_own"]],
        block,
    )
    swap = links.send(r["keyval_own"], r["keyval_other"], links.tp)
    out.near()
    out.halve(0)
    up.add(0)
    if len(bits) > 1:
        up.halve(1)
    swap.wait_recv()
    rows_job(pair_sum, [r["keyval_own"], r["keyval_other"]], [], [r["keyval_back"]], block)
    share0.wait_recv()
    finish_source(0)
    share1 = share(1)
    feed0.wait_recv()
    finish_output(0)
    query.near()
    query.halve(0)
    keyval.away()
    feed1.wait_recv()
    finish_output(1)
    keyval.far()
    out.add(0)
    if len(bits) > 1:
        out.halve(1)
    keyval.cross()
    query.add(0)
    if len(bits) > 1:
        query.halve(1)
    keyval.near()
    keyval.halve(0)
    keyval.add(0)
    if len(bits) > 1:
        keyval.halve(1)
    share1.wait_recv()
    finish_source(1)
    if len(bits) > 1:
        for each in (gate, up, out, query, keyval):
            each.rest(1)
    down.wait("arrived")
    for by in range(1, hops + 1):

        @pl.when(links.place >= by)
        def _(move=windows[by - 1]):
            move.wait_send()

    links.close()


def from_place(array, by):
    count = lax.axis_size("ctx")
    return lax.ppermute(array, "ctx", [(i, i + by) for i in range(count) if i + by < count])


def swap_tp(array):
    return lax.ppermute(array, "tp", [(0, 1), (1, 0)])


def gathered(shard):
    return lax.all_gather(shard, ("fsdp", "ctx"), axis=0, tiled=True)


def on_device(
    tokens,
    query_weight,
    keyval_weight,
    out_weight,
    gate_weight,
    up_weight,
    down_weight,
    first_gain,
    second_gain,
    cotangent,
):
    rows, features = tokens.shape
    width = query_weight.shape[1]
    units = gate_weight.shape[1]
    heads = width // HD
    scale = HD ** (-0.5)
    count = lax.axis_size("ctx")
    hops = min(-(-W // rows), count - 1)
    place = lax.axis_index("ctx")
    block = min(256, rows)

    gains = jnp.pad(jnp.stack([first_gain, second_gain], axis=1), ((0, 0), (0, 126)))
    small_full = gathered(jnp.concatenate([query_weight, out_weight, keyval_weight, gains], axis=1))
    gate_full = gathered(gate_weight)
    up_full = gathered(up_weight)
    down_full = gathered(down_weight)
    query_full = small_full[:, :width]
    keyval_full = small_full[:, 2 * width : 2 * width + 2 * HD]
    both_gains = 1.0 + small_full[:, 2 * width + 2 * HD :][:, :2].astype(WIDE).T
    gain_one, gain_two = both_gains[:1], both_gains[1:]

    source = tokens.astype(WIDE)
    first_inverse = lax.rsqrt(jnp.mean(source * source, axis=-1, keepdims=True) + EPS)
    first_low = (source * first_inverse * gain_one).astype(LOW)
    keyval = matmul(first_low, keyval_full).astype(LOW)
    first_tp = lax.axis_index("tp") == 0
    mine = jnp.where(first_tp, keyval[:, :HD], keyval[:, HD:])
    before = jnp.concatenate([from_place(mine, by) for by in range(hops, 0, -1)])
    theirs = swap_tp(before)
    queries = (matmul(first_low, query_full) * scale).astype(LOW)
    keys = jnp.where(first_tp, before, theirs)
    values = jnp.where(first_tp, theirs, before)
    window = jnp.concatenate([jnp.concatenate([keys, values], axis=1), keyval], axis=0)
    attended, probs = attend(queries, window, place.reshape(1), hops)
    (branch,) = product("nt", attended, small_full, bm=rows, bn=512, width=features, col=1)
    middle, second_low, second_inverse = by_rows(
        add_norm,
        [tokens, branch, swap_tp(branch)],
        [gain_two],
        [(features, LOW), (features, LOW), (128, WIDE)],
        block,
    )
    (gate,) = product("nn", second_low, gate_full, bm=rows, bn=768, width=units, outs=(WIDE,))
    hidden, to_up, to_gate = product(
        "nn",
        second_low,
        up_full,
        bm=rows,
        bn=768,
        width=units,
        sub=256,
        extras=[gate],
        finish=finish_up,
        outs=(LOW, LOW, LOW),
    )

    plain = {
        "gate_back": (rows, units),
        "up_back": (rows, units),
        "second": (rows, features),
        "second_other": (rows, features),
        "feed0": (rows // 2, features),
        "feed1": (rows // 2, features),
        "feed_other0": (rows // 2, features),
        "feed_other1": (rows // 2, features),
        "middle_low": (rows, features),
        "grad_attended": (rows, width),
        "query_back": (rows, width),
        "window_back": window.shape,
        "window_other": (hops, rows, 2 * HD),
        "keyval_own": (rows, 2 * HD),
        "keyval_other": (rows, 2 * HD),
        "keyval_back": (rows, 2 * HD),
        "share": (rows, features),
        "share_other0": (rows // 2, features),
        "share_other1": (rows // 2, features),
        "input_grad": (rows, features),
        "output": (rows, features),
    }
    shapes = {key: jax.ShapeDtypeStruct(shape, LOW) for key, shape in plain.items()}
    shapes |= ScatterFirst.shapes("d_", features, units, count)
    for prefix, each in (("g_", units), ("u_", units), ("o_", width), ("q_", width), ("k_", 2 * HD)):
        shapes |= Scatter.shapes(prefix, features, each, count)
    done = dict(
        cotangent=cotangent,
        down_full=down_full,
        gate_full=gate_full,
        up_full=up_full,
        small_full=small_full,
        to_gate=to_gate,
        to_up=to_up,
        hidden=hidden,
        first_low=first_low,
        second_low=second_low,
        middle=middle,
        second_inverse=second_inverse,
        gain_two=gain_two,
        gain_one=gain_one,
        tokens=tokens,
        first_inverse=jnp.broadcast_to(first_inverse, (rows, 128)),
        queries=queries,
        window=window,
        attended=attended,
        probs=probs,
    )
    total = pltpu.VMEM((features // 4, max(width, units // 3)), WIDE)
    sizes = dict(rows=rows, heads=heads, count=count)
    late = len(bits_of(count)) - 1

    def stage(prefix, *keys):
        return [prefix + key for key in keys]

    def halving(prefix, first, end):
        keys = []
        for k in range(first, end):
            keys += [f"{prefix}recv{k}"] + ([f"{prefix}mid{k}"] if k < late else [])
        return keys

    reads, writes = ["cotangent", "hidden"], stage("d_", "away", "got", "near")
    call = remote_call(
        by_name(functools.partial(down_start, count=count), reads, writes, 1),
        reads,
        [shapes[key] for key in writes],
        [total],
        0,
        "down_start",
    )
    done |= zip(writes, call(*[done[key] for key in reads]))

    reads = ["d_near", "cotangent", "hidden", "down_full", "gate_full", "up_full", "small_full"]
    reads += ["to_gate", "to_up", "first_low", "second_low", "middle", "tokens", "first_inverse", "second_inverse"]
    reads += ["gain_one", "gain_two", "attended", "queries", "window", "probs"]
    writes = list(plain) + ["d_arrived"] + halving("d_", 0, late + 1) + [f"d_mid{late}"]
    for prefix in ("g_", "u_", "o_", "q_", "k_"):
        writes += stage(prefix, "away", "got", "far", "arrived", "near") + halving(prefix, 0, late + 1)
    call = remote_call(
        by_name(functools.partial(backward, hops=hops, **sizes), reads, writes, 1),
        reads,
        [shapes[key] for key in writes],
        [total],
        1,
        "backward",
    )
    done |= zip(writes, call(*[done[key] for key in reads]))
    down_grad = scatter_first_result("d_", done)
    gate_grad, up_grad, out_grad, query_grad, keyval_grad = (
        scatter_result(prefix, done) for prefix in ("g_", "u_", "o_", "q_", "k_")
    )

    def row_sum(weight, grad):
        return jnp.sum(weight.astype(WIDE) * grad, axis=1)

    sums = jnp.stack(
        [
            row_sum(query_weight, query_grad),
            row_sum(gate_weight, gate_grad) + row_sum(up_weight, up_grad),
        ]
    )
    sums = sums + swap_tp(sums)
    first_grad = (sums[0] + row_sum(keyval_weight, keyval_grad)) / (1.0 + first_gain.astype(WIDE))
    second_grad = sums[1] / (1.0 + second_gain.astype(WIDE))
    return (
        done["output"],
        done["input_grad"],
        query_grad,
        keyval_grad,
        out_grad,
        gate_grad,
        up_grad,
        down_grad,
        first_grad,
        second_grad,
    )


def solution(mesh):
    rows = P(("fsdp", "ctx"), None)
    split = P(("fsdp", "ctx"), "tp")
    vector = P(("fsdp", "ctx"))
    return jax.shard_map(
        on_device,
        mesh=mesh,
        in_specs=(rows, split, rows, split, split, split, split, vector, vector, rows),
        out_specs=(rows, rows, split, rows, split, split, split, split, vector, vector),
        check_vma=False,
    )
```

```python
import functools

import jax
import jax.numpy as jnp
from jax import lax
from jax.experimental import pallas as pl
from jax.experimental.pallas import tpu as pltpu
from jax.sharding import PartitionSpec as P

HD = 256
W = 2048
EPS = 1e-06
FAR = -1e30
LOW = jnp.bfloat16
WIDE = jnp.float32
CONTRACT_ROWS = (((0,), (0,)), ((), ()))
CONTRACT_LAST = (((1,), (1,)), ((), ()))
VMEM = 60 * 1024 * 1024


def matmul(left, right):
    return jnp.dot(left, right, preferred_element_type=WIDE)


def rows_product(left, right):
    return lax.dot_general(left, right, CONTRACT_ROWS, preferred_element_type=WIDE)


def right_transposed(left, right):
    return lax.dot_general(left, right, CONTRACT_LAST, preferred_element_type=WIDE)


def gelu_parts(gate):
    c = 0.7978845608028654
    inner = c * (gate + 0.044715 * gate * gate * gate)
    t = jnp.tanh(inner)
    value = 0.5 * gate * (1.0 + t)
    slope = 0.5 * (1.0 + t) + 0.5 * gate * (1.0 - t * t) * c * (1.0 + 3 * 0.044715 * gate * gate)
    return value, slope


def attend_kernel(place_ref, q_ref, win_ref, out_ref, probs_ref, bias_ref, *, heads, hops, rows, block):
    span = W + block
    start = pl.program_id(0) * block
    first = (hops - place_ref[0]) * rows - start
    row = lax.broadcasted_iota(jnp.int32, (block, span), 0)
    col = lax.broadcasted_iota(jnp.int32, (block, span), 1)
    live = (col > row) & (col <= row + W) & (col >= first)
    bias_ref[...] = jnp.where(live, 0.0, FAR)
    window = pl.ds(pl.multiple_of(start, block), span)
    for h in range(heads):
        cols = slice(h * HD, (h + 1) * HD)
        scores = right_transposed(q_ref[:, cols], win_ref[window, :HD]) + bias_ref[...]
        top = jnp.max(scores, axis=1, keepdims=True)
        weights = jnp.exp(scores - top)
        total = jnp.sum(weights, axis=1, keepdims=True)
        probs_ref[h] = (weights * (1.0 / total)).astype(LOW)
        out_ref[:, cols] = matmul(probs_ref[h], win_ref[window, HD:]).astype(LOW)


def attend(queries, window, place, hops):
    rows, width = queries.shape
    heads = width // HD
    block = min(256, rows)
    span = W + block
    return pl.pallas_call(
        functools.partial(attend_kernel, heads=heads, hops=hops, rows=rows, block=block),
        grid=(rows // block,),
        in_specs=[
            pl.BlockSpec(memory_space=pltpu.SMEM),
            pl.BlockSpec((block, width), lambda i: (i, 0)),
            pl.BlockSpec(window.shape, lambda i: (0, 0)),
        ],
        out_specs=[
            pl.BlockSpec((block, width), lambda i: (i, 0)),
            pl.BlockSpec((heads, block, span), lambda i: (0, i, 0)),
        ],
        out_shape=[
            jax.ShapeDtypeStruct((rows, width), LOW),
            jax.ShapeDtypeStruct((heads, rows, span), LOW),
        ],
        scratch_shapes=[pltpu.VMEM((block, span), WIDE)],
        compiler_params=pltpu.CompilerParams(vmem_limit_bytes=VMEM),
        name="attend",
    )(place, queries, window)


CONTRACT = {"nn": (((1,), (0,)), ((), ())), "nt": CONTRACT_LAST, "tn": CONTRACT_ROWS}


def products_body(kind, n_pairs, n_extras, finish, sub, keep):
    def body(*refs):
        pairs = [(refs[2 * p], refs[2 * p + 1]) for p in range(n_pairs)]
        extras = refs[2 * n_pairs : 2 * n_pairs + n_extras]
        outs = refs[2 * n_pairs + n_extras :]
        bn = pairs[0][1].shape[0 if kind == "nt" else 1]
        step = sub or bn
        for start in range(0, bn, step):
            cols = slice(start, start + step)
            total = None
            for left, right in pairs:
                part = right[cols, :] if kind == "nt" else right[:, cols]
                term = lax.dot_general(left[...], part, CONTRACT[kind], preferred_element_type=WIDE)
                total = term if total is None else total + term
            given = [e[:, cols].astype(WIDE) for e in extras]
            keep(outs, cols, finish(total, *given) if finish else [sum(given, total)])

    return body


def keep_blocks(outs, cols, results):
    for out, result in zip(outs, results, strict=True):
        out[:, cols] = result.astype(out.dtype)


def products_specs(kind, depths, bm, bn, left_block, right_col):
    specs = []
    for depth in depths:
        if kind == "tn":
            specs.append(pl.BlockSpec((depth, bm), lambda i, j: (0, left_block(i))))
        else:
            specs.append(pl.BlockSpec((bm, depth), lambda i, j: (left_block(i), 0)))
        if kind == "nt":
            specs.append(pl.BlockSpec((bn, depth), lambda i, j: (j, right_col)))
        else:
            specs.append(pl.BlockSpec((depth, bn), lambda i, j: (0, right_col + j)))
    return specs


def product(kind, left, right, *, bm, bn, width, col=0, extras=(), finish=None, outs=(LOW,), sub=0):
    depth = left.shape[1]
    by_block = pl.BlockSpec((bm, bn), lambda i, j: (i, j))
    return pl.pallas_call(
        products_body(kind, 1, len(extras), finish, sub, keep_blocks),
        grid=(left.shape[0] // bm, width // bn),
        in_specs=products_specs(kind, [depth], bm, bn, lambda i: i, col) + [by_block] * len(extras),
        out_specs=[by_block] * len(outs),
        out_shape=[jax.ShapeDtypeStruct((left.shape[0], width), each) for each in outs],
        compiler_params=pltpu.CompilerParams(vmem_limit_bytes=VMEM),
        name="product",
    )(left, right, *extras)


def by_rows(body, sliced, whole, outs, block):
    rows = sliced[0].shape[0]
    n_in = len(sliced) + len(whole)
    specs = [pl.BlockSpec((block, a.shape[1]), lambda i: (i, 0)) for a in sliced]
    specs += [pl.BlockSpec(a.shape, lambda i: (0, 0)) for a in whole]
    return pl.pallas_call(
        lambda *refs: body(refs[:n_in], refs[n_in:]),
        grid=(rows // block,),
        in_specs=specs,
        out_specs=[pl.BlockSpec((block, cols), lambda i: (i, 0)) for cols, _ in outs],
        out_shape=[jax.ShapeDtypeStruct((rows, cols), kind) for cols, kind in outs],
        compiler_params=pltpu.CompilerParams(vmem_limit_bytes=VMEM),
        name="by_rows",
    )(*sliced, *whole)


def add_norm(ins, outs):
    tokens, own, other, gain = ins
    middle = tokens[...].astype(WIDE) + (own[...].astype(WIDE) + other[...].astype(WIDE))
    inverse = lax.rsqrt(jnp.mean(middle * middle, axis=1, keepdims=True) + EPS)
    outs[0][...] = middle.astype(LOW)
    outs[1][...] = (middle * inverse * gain[...]).astype(LOW)
    outs[2][...] = jnp.broadcast_to(inverse, outs[2].shape)


def norm_back(values, grad, gain, inverse):
    scaled = grad * gain
    along = jnp.sum(scaled * values, axis=1, keepdims=True) * (1.0 / values.shape[1])
    return inverse * scaled - values * (inverse * inverse * inverse * along)


def middle_back(ins, outs):
    cotangent, middle, inverse, own, other, gain, out_full = ins
    grad = own[...].astype(WIDE) + other[...].astype(WIDE)
    back = norm_back(middle[...].astype(WIDE), grad, gain[...], inverse[:, :1])
    low = (cotangent[...].astype(WIDE) + back).astype(LOW)
    outs[0][...] = low
    outs[1][...] = matmul(low, out_full[...]).astype(LOW)


def source_back(ins, outs):
    tokens, middle_low, inverse, own, other, keyval_back, gain, keyval_full = ins
    grad = own[...].astype(WIDE) + other[...].astype(WIDE)
    grad = grad + right_transposed(keyval_back[...], keyval_full[...])
    back = norm_back(tokens[...].astype(WIDE), grad, gain[...], inverse[:, :1])
    outs[0][...] = (middle_low[...].astype(WIDE) + back).astype(LOW)


def add_feed(ins, outs):
    middle, own, other = ins
    outs[0][...] = (middle[...].astype(WIDE) + (own[...].astype(WIDE) + other[...].astype(WIDE))).astype(LOW)


def finish_up(upward, gate):
    value, slope = gelu_parts(gate)
    return value * upward, value, slope * upward


def finish_hidden(grad_hidden, to_gate, to_up):
    return grad_hidden * to_gate, grad_hidden * to_up


MESH = pl.DeviceIdType.MESH


class Links:
    def __init__(self, send_sems, recv_sems):
        self.send_sems, self.recv_sems = send_sems, recv_sems
        self.count = 0
        self.open = []
        self.fsdp = lax.axis_index("fsdp")
        self.place = lax.axis_index("ctx")
        self.core = {"fsdp": self.fsdp + 1 - 2 * lax.rem(self.fsdp, 2)}
        self.chip = {"fsdp": lax.rem(self.fsdp + 2, 4)}
        self.tp = {"tp": 1 - lax.axis_index("tp")}

    def block(self, flip):
        return (self.fsdp, self.core["fsdp"], self.chip["fsdp"], 3 - self.fsdp)[flip]

    def along(self, bit):
        return {"ctx": self.place + bit - 2 * bit * lax.rem(lax.div(self.place, bit), 2)}

    def meet(self, partners):
        barrier = pltpu.get_barrier_semaphore()
        for partner in partners:
            pl.semaphore_signal(barrier, inc=1, device_id=partner, device_id_type=MESH)
        pl.semaphore_wait(barrier, len(partners))

    def copy(self, source, target, partner):
        made = pltpu.make_async_remote_copy(
            src_ref=source,
            dst_ref=target,
            send_sem=self.send_sems.at[self.count],
            recv_sem=self.recv_sems.at[self.count],
            device_id=partner,
            device_id_type=MESH,
        )
        self.count += 1
        return made

    def send(self, source, target, partner):
        made = self.copy(source, target, partner)
        made.start()
        self.open.append(made)
        return made

    def close(self):
        for made in self.open:
            made.wait_send()


def job(kind, pairs, outs, *, bm, bn, steps=1, left_block=None, right_col=0, extras=(), finish=None, sub=0):
    depths = [left.shape[0 if kind == "tn" else 1] for left, _ in pairs]
    width = outs[0].shape[1]
    specs = products_specs(kind, depths, bm, bn, left_block or (lambda i: i), right_col)
    specs += [pl.BlockSpec((bm, bn), lambda i, j, at=at: (i + at, j)) for _, at in extras]
    pltpu.emit_pipeline(
        products_body(kind, len(pairs), len(extras), finish, sub, keep_blocks),
        grid=(steps, width // bn),
        in_specs=specs,
        out_specs=[pl.BlockSpec((bm, bn), lambda i, j: (i, j))] * len(outs),
    )(*[ref for pair in pairs for ref in pair], *[ref for ref, _ in extras], *outs)


def rows_job(body, sliced, whole, outs, block):
    n_in = len(sliced) + len(whole)
    specs = [pl.BlockSpec((block, a.shape[1]), lambda i: (i, 0)) for a in sliced]
    specs += [pl.BlockSpec(a.shape, lambda i: (0, 0)) for a in whole]
    pltpu.emit_pipeline(
        lambda *refs: body(refs[:n_in], refs[n_in:]),
        grid=(sliced[0].shape[0] // block,),
        in_specs=specs,
        out_specs=[pl.BlockSpec((block, a.shape[1]), lambda i: (i, 0)) for a in outs],
    )(*sliced, *whole, *outs)


def bits_of(count):
    bits = []
    while 1 << len(bits) < count:
        bits.append(1 << len(bits))
    return bits


def piece_order(count):
    order = [0]
    for bit in reversed(bits_of(count)):
        order = order + [r + bit for r in order]
    return order


class Scatter:
    add_last = False

    @staticmethod
    def shapes(prefix, features, width, count):
        part = features // 4
        size = part // count
        out = {"away": (2 * part, width), "got": (2 * part, width), "far": (part, width), "arrived": (part, width)}
        left = count
        out["near"] = (left, size, width)
        for k in range(len(bits_of(count))):
            left //= 2
            out[f"recv{k}"] = (left, size, width)
            if left > 1:
                out[f"mid{k}"] = (left, size, width)
        return {prefix + key: jax.ShapeDtypeStruct(shape, LOW) for key, shape in out.items()}

    def __init__(self, prefix, refs, links, left, right, bn, count, total=None):
        self.refs, self.prefix, self.links, self.bn, self.total = refs, prefix, links, bn, total
        self.pairs = [(refs[left], refs[right])]
        self.part = refs[left].shape[1] // 4
        self.bits = bits_of(count)
        self.moving = {}

    def ref(self, key):
        return self.refs[self.prefix + key]

    def wait(self, key):
        if key in self.moving:
            self.moving.pop(key).wait_recv()

    def away(self):
        core, both = self.links.block(1), self.links.block(3)
        job(
            "tn",
            self.pairs,
            [self.ref("away")],
            bm=self.part,
            bn=self.bn,
            steps=2,
            left_block=lambda i: both + i * (core - both),
        )
        self.moving["got"] = self.links.send(self.ref("away"), self.ref("got"), self.links.core)

    def far(self):
        self.wait("got")
        chip = self.links.block(2)
        job(
            "tn",
            self.pairs,
            [self.ref("far")],
            bm=self.part,
            bn=self.bn,
            left_block=lambda i: chip,
            extras=[(self.ref("got"), 0)],
        )

    def cross(self):
        self.moving["arrived"] = self.links.send(self.ref("far"), self.ref("arrived"), self.links.chip)

    def near(self):
        self.wait("arrived")
        own = self.links.block(0)
        extras = [pl.BlockSpec((self.part, self.bn), lambda i, j: (1, j)), pl.BlockSpec((self.part, self.bn), lambda i, j: (0, j))]
        self.make_near(1, lambda i: own, [self.ref("got"), self.ref("arrived")], extras)

    def make_near(self, steps, left_block, given, extras):
        place = self.links.place
        near, total = self.ref("near"), self.total
        count = near.shape[0]
        size = self.part // count
        order = piece_order(count)

        def keep(outs, cols, results):
            total[:, cols] = results[0]
            for k in range(count):
                at = 0
                for bit in self.bits:
                    mine = lax.rem(lax.div(place, bit), 2)
                    at = at + bit * (1 - mine if order[k] & bit else mine)
                rows = pl.ds(pl.multiple_of(at * size, size), size)
                outs[0][k, :, cols] = total[rows, cols].astype(LOW)

        bm, bn = self.part, self.bn
        left, right = self.pairs[0]
        pltpu.emit_pipeline(
            products_body("tn", 1, len(given), None, 0, keep),
            grid=(steps, right.shape[1] // bn),
            in_specs=products_specs("tn", [left.shape[0]], bm, bn, left_block, 0) + extras,
            out_specs=[pl.BlockSpec((count, size, bn), lambda i, j: (0, i, j))],
        )(left, right, *given, near)

    def kept(self, k):
        return self.ref(f"mid{k - 1}" if k else "near")

    def halve(self, k):
        now = self.kept(k)
        half = now.shape[0] // 2
        self.moving[f"recv{k}"] = self.links.send(
            now.at[pl.ds(half, half)], self.ref(f"recv{k}"), self.links.along(self.bits[k])
        )

    def add(self, k):
        self.wait(f"recv{k}")
        if k + 1 == len(self.bits) and not self.add_last:
            return
        now, mid = self.kept(k), self.ref(f"mid{k}")
        half, size, bn = mid.shape[0], mid.shape[1], self.bn

        def body(own, other, out):
            out[...] = (own[...].astype(WIDE) + other[...].astype(WIDE)).astype(LOW)

        block = pl.BlockSpec((half, size, bn), lambda j: (0, 0, j))
        pltpu.emit_pipeline(body, grid=(mid.shape[2] // bn,), in_specs=[block, block], out_specs=[block])(
            now, self.ref(f"recv{k}"), mid
        )

    def rest(self, k):
        self.add(k)
        for later in range(k + 1, len(self.bits)):
            self.halve(later)
            self.add(later)


class ScatterFirst(Scatter):
    add_last = True

    @staticmethod
    def shapes(prefix, features, width, count):
        part = features // 4
        size = part // count
        out = {"away": (2 * part, width), "got": (2 * part, width), "near": (count, 2 * size, width)}
        left = count
        for k in range(len(bits_of(count))):
            left //= 2
            out[f"recv{k}"] = out[f"mid{k}"] = (left, 2 * size, width)
        out["arrived"] = (size, width)
        return {prefix + key: jax.ShapeDtypeStruct(shape, LOW) for key, shape in out.items()}

    def near(self):
        self.wait("got")
        chip, own = self.links.block(2), self.links.block(0)
        extras = [pl.BlockSpec((self.part, self.bn), lambda i, j: (i, j))]
        self.make_near(2, lambda i: chip + i * (own - chip), [self.ref("got")], extras)

    def cross(self):
        last = self.kept(len(self.bits))
        size = last.shape[1] // 2
        self.moving["arrived"] = self.links.send(
            last.at[0, pl.ds(0, size)], self.ref("arrived"), self.links.chip
        )


def scatter_result(prefix, arrays):
    last = len(bits_of(arrays[prefix + "near"].shape[0])) - 1
    now = arrays[prefix + (f"mid{last - 1}" if last else "near")]
    return now[0].astype(WIDE) + arrays[prefix + f"recv{last}"][0].astype(WIDE)


def scatter_first_result(prefix, arrays):
    size = arrays[prefix + "arrived"].shape[0]
    last = len(bits_of(arrays[prefix + "near"].shape[0])) - 1
    return arrays[prefix + f"mid{last}"][0, size:].astype(WIDE) + arrays[prefix + "arrived"].astype(WIDE)


def remote_call(kernel, inputs, outputs, scratch, collective_id, name):
    anywhere = pl.BlockSpec(memory_space=pl.ANY)
    sems = pltpu.SemaphoreType.DMA((64,))
    return pl.pallas_call(
        kernel,
        in_specs=[anywhere] * len(inputs),
        out_specs=[anywhere] * len(outputs),
        out_shape=outputs,
        scratch_shapes=scratch + [sems, sems],
        compiler_params=pltpu.CompilerParams(
            collective_id=collective_id, has_side_effects=True, vmem_limit_bytes=VMEM
        ),
        name=name,
    )


def by_name(body, reads, writes, n_scratch):
    names = reads + writes

    def kernel(*refs):
        rest = refs[len(names) :]
        body(dict(zip(names, refs)), Links(rest[-2], rest[-1]), *rest[:n_scratch])

    return kernel


def down_start(r, links, total, *, count):
    links.meet([links.core])
    down = ScatterFirst("d_", r, links, "cotangent", "hidden", r["hidden"].shape[1] // 3, count, total)
    down.away()
    down.near()
    links.close()


def attend_back(refs, rows, heads, block):
    span = W + block
    steps = rows // block
    queries, backs, outs, probs = (refs[k] for k in ("queries", "grad_attended", "attended", "probs"))

    def scoped(win, dwin, q, back, out, dq, p, ds, sems):
        loads = [
            pltpu.make_async_copy(a, b, sems.at[k])
            for k, (a, b) in enumerate([(refs["window"], win), (queries, q), (backs, back), (outs, out)])
        ]

        def fetch(i):
            slot = lax.rem(i, 2)
            at = pl.ds(pl.multiple_of(i * block, block), block)
            return pltpu.make_async_copy(probs.at[:, at, :], p.at[slot], sems.at[4 + slot])

        fetch(0).start()
        for load in loads:
            load.start()
        dwin[...] = jnp.zeros_like(dwin)
        for load in loads:
            load.wait()

        def step(i, carry):
            @pl.when(i + 1 < steps)
            def _():
                fetch(i + 1).start()

            fetch(i).wait()
            slot = lax.rem(i, 2)
            at = pl.ds(pl.multiple_of(i * block, block), block)
            window = pl.ds(pl.multiple_of(i * block, block), span)
            for h in range(heads):
                cols = slice(h * HD, (h + 1) * HD)
                g = back[at, cols]
                along = jnp.sum(g.astype(WIDE) * out[at, cols].astype(WIDE), axis=1, keepdims=True)
                grad_probs = right_transposed(g, win[window, HD:])
                ds[h] = (p[slot, h].astype(WIDE) * (grad_probs - along)).astype(LOW)
                part = matmul(ds[h], win[window, :HD]).astype(LOW)
                dq[at, cols] = (part.astype(WIDE) * HD ** (-0.5)).astype(LOW)
            q_all = jnp.concatenate([q[at, h * HD : (h + 1) * HD] for h in range(heads)], axis=0)
            g_all = jnp.concatenate([back[at, h * HD : (h + 1) * HD] for h in range(heads)], axis=0)
            dwin[window, :HD] += rows_product(ds[...].reshape(heads * block, span), q_all)
            dwin[window, HD:] += rows_product(p[slot].reshape(heads * block, span), g_all)
            return carry

        lax.fori_loop(0, steps, step, 0)
        win[...] = dwin[...].astype(LOW)
        stores = [
            pltpu.make_async_copy(win, refs["window_back"], sems.at[0]),
            pltpu.make_async_copy(dq, refs["query_back"], sems.at[1]),
        ]
        for store in stores:
            store.start()
        for store in stores:
            store.wait()

    width = heads * HD
    length = refs["window"].shape[0]
    pl.run_scoped(
        scoped,
        pltpu.VMEM((length, 2 * HD), LOW),
        pltpu.VMEM((length, 2 * HD), WIDE),
        pltpu.VMEM((rows, width), LOW),
        pltpu.VMEM((rows, width), LOW),
        pltpu.VMEM((rows, width), LOW),
        pltpu.VMEM((rows, width), LOW),
        pltpu.VMEM((2, heads, block, span), LOW),
        pltpu.VMEM((heads, block, span), LOW),
        pltpu.SemaphoreType.DMA((6,)),
    )


def window_sum(place, count, hops):
    def body(ins, outs):
        total = ins[0][...].astype(WIDE)
        for by in range(1, hops + 1):
            total = total + jnp.where(place + by < count, ins[by][...].astype(WIDE), 0.0)
        outs[0][...] = total.astype(LOW)

    return body


def pair_sum(ins, outs):
    outs[0][...] = (ins[0][...].astype(WIDE) + ins[1][...].astype(WIDE)).astype(LOW)


def backward(r, links, total, *, rows, heads, hops, count):
    half = rows // 2
    block = min(256, half)
    features = r["cotangent"].shape[1]
    width = heads * HD
    third = r["hidden"].shape[1] // 3
    bits = bits_of(count)
    links.meet([links.core, links.chip, links.tp] + [{"ctx": lax.rem(links.place + k, count)} for k in range(1, count)])
    down = ScatterFirst("d_", r, links, "cotangent", "hidden", third, count, total)
    gate = Scatter("g_", r, links, "second_low", "gate_back", third, count, total)
    up = Scatter("u_", r, links, "second_low", "up_back", third, count, total)
    out = Scatter("o_", r, links, "middle_low", "attended", width, count, total)
    query = Scatter("q_", r, links, "first_low", "query_back", width, count, total)
    keyval = Scatter("k_", r, links, "first_low", "keyval_back", 2 * HD, count, total)
    parts = (pl.ds(0, half), pl.ds(half, half))

    def second(part):
        job(
            "nt",
            [(r["gate_back"].at[part], r["gate_full"]), (r["up_back"].at[part], r["up_full"])],
            [r["second"].at[part]],
            bm=half,
            bn=256,
        )
        return links.send(r["second"].at[part], r["second_other"].at[part], links.tp)

    def feed(k):
        job("nt", [(r["hidden"].at[parts[k]], r["down_full"])], [r[f"feed{k}"]], bm=half, bn=512)
        return links.send(r[f"feed{k}"], r[f"feed_other{k}"], links.tp)

    def share(k):
        return links.send(r["share"].at[parts[k]], r[f"share_other{k}"], links.tp)

    def finish_source(k):
        part = parts[k]
        rows_job(
            source_back,
            [r[key].at[part] for key in ("tokens", "middle_low", "first_inverse", "share")]
            + [r[f"share_other{k}"], r["keyval_back"].at[part]],
            [r["gain_one"], r["small_full"].at[:, pl.ds(2 * width, 2 * HD)]],
            [r["input_grad"].at[part]],
            block,
        )

    def finish_output(k):
        part = parts[k]
        rows_job(add_feed, [r["middle"].at[part], r[f"feed{k}"], r[f"feed_other{k}"]], [], [r["output"].at[part]], block)

    def windows_to(place, by):
        return links.copy(
            r["window_back"].at[pl.ds((hops - by) * rows, rows)],
            r["window_other"].at[by - 1],
            {"ctx": lax.rem(place + count - by, count)},
        )

    job(
        "nn",
        [(r["cotangent"], r["down_full"])],
        [r["gate_back"], r["up_back"]],
        bm=rows,
        bn=third * 3 // 5,
        sub=third // 5,
        extras=[(r["to_gate"], 0), (r["to_up"], 0)],
        finish=finish_hidden,
    )
    gate.away()
    down.halve(0)
    second0 = second(parts[0])
    gate.far()
    gate.cross()
    second1 = second(parts[1])
    up.away()
    down.add(0)
    if len(bits) > 1:
        down.halve(1)
    up.far()
    feed1 = feed(1)
    feed0 = feed(0)
    up.cross()
    gate.near()
    gate.halve(0)
    second0.wait_recv()
    second1.wait_recv()
    rows_job(
        middle_back,
        [r["cotangent"], r["middle"], r["second_inverse"], r["second"], r["second_other"]],
        [r["gain_two"], r["small_full"].at[:, pl.ds(width, width)]],
        [r["middle_low"], r["grad_attended"]],
        block,
    )
    attend_back(r, rows, heads, min(256, rows))
    windows = []
    for by in range(1, hops + 1):
        move = windows_to(links.place, by)

        @pl.when(links.place >= by)
        def _(move=move):
            move.start()

        windows.append(move)
    gate.add(0)
    if len(bits) > 1:
        gate.halve(1)
    job("nt", [(r["query_back"], r["small_full"].at[:, pl.ds(0, width)])], [r["share"]], bm=rows, bn=512)
    share1 = share(1)
    feed1.wait_recv()
    finish_output(1)
    out.away()
    query.away()
    query.far()
    query.cross()
    up.near()
    up.halve(0)
    out.far()
    out.cross()
    for by in range(1, hops + 1):

        @pl.when(links.place + by < count)
        def _(move=windows[by - 1]):
            move.wait_recv()

    rows_job(
        window_sum(links.place, count, hops),
        [r["window_back"].at[pl.ds(hops * rows, rows)]] + [r["window_other"].at[by] for by in range(hops)],
        [],
        [r["keyval_own"]],
        block,
    )
    swap = links.send(r["keyval_own"], r["keyval_other"], links.tp)
    query.near()
    query.halve(0)
    share0 = share(0)
    swap.wait_recv()
    rows_job(pair_sum, [r["keyval_own"], r["keyval_other"]], [], [r["keyval_back"]], block)
    up.add(0)
    if len(bits) > 1:
        up.halve(1)
    out.near()
    out.halve(0)
    keyval.away()
    keyval.far()
    keyval.cross()
    share1.wait_recv()
    finish_source(1)
    query.add(0)
    if len(bits) > 1:
        query.halve(1)
    if len(bits) > 1:
        down.rest(1)
    down.cross()
    keyval.near()
    keyval.halve(0)
    out.add(0)
    if len(bits) > 1:
        out.halve(1)
    share0.wait_recv()
    finish_source(0)
    keyval.add(0)
    if len(bits) > 1:
        keyval.halve(1)
    feed0.wait_recv()
    finish_output(0)
    if len(bits) > 1:
        for each in (gate, up, out, query, keyval):
            each.rest(1)
    down.wait("arrived")
    for by in range(1, hops + 1):

        @pl.when(links.place >= by)
        def _(move=windows[by - 1]):
            move.wait_send()

    links.close()


def from_place(array, by):
    count = lax.axis_size("ctx")
    return lax.ppermute(array, "ctx", [(i, i + by) for i in range(count) if i + by < count])


def swap_tp(array):
    return lax.ppermute(array, "tp", [(0, 1), (1, 0)])


def gathered(shard):
    return lax.all_gather(shard, ("fsdp", "ctx"), axis=0, tiled=True)


def on_device(
    tokens,
    query_weight,
    keyval_weight,
    out_weight,
    gate_weight,
    up_weight,
    down_weight,
    first_gain,
    second_gain,
    cotangent,
):
    rows, features = tokens.shape
    width = query_weight.shape[1]
    units = gate_weight.shape[1]
    heads = width // HD
    scale = HD ** (-0.5)
    count = lax.axis_size("ctx")
    hops = min(-(-W // rows), count - 1)
    place = lax.axis_index("ctx")
    block = min(256, rows)

    spare = units - 2 * width - 2 * HD - 2
    gains = jnp.pad(jnp.stack([first_gain, second_gain], axis=1), ((0, 0), (0, spare)))
    small_full = gathered(jnp.concatenate([query_weight, out_weight, keyval_weight, gains], axis=1))
    gate_full = gathered(gate_weight)
    up_full = gathered(up_weight)
    down_full = gathered(down_weight)
    query_full = small_full[:, :width]
    keyval_full = small_full[:, 2 * width : 2 * width + 2 * HD]
    both_gains = 1.0 + small_full[:, 2 * width + 2 * HD :][:, :2].astype(WIDE).T
    gain_one, gain_two = both_gains[:1], both_gains[1:]

    source = tokens.astype(WIDE)
    first_inverse = lax.rsqrt(jnp.mean(source * source, axis=-1, keepdims=True) + EPS)
    first_low = (source * first_inverse * gain_one).astype(LOW)
    keyval = matmul(first_low, keyval_full).astype(LOW)
    first_tp = lax.axis_index("tp") == 0
    mine = jnp.where(first_tp, keyval[:, :HD], keyval[:, HD:])
    before = jnp.concatenate([from_place(mine, by) for by in range(hops, 0, -1)])
    theirs = swap_tp(before)
    queries = (matmul(first_low, query_full) * scale).astype(LOW)
    keys = jnp.where(first_tp, before, theirs)
    values = jnp.where(first_tp, theirs, before)
    window = jnp.concatenate([jnp.concatenate([keys, values], axis=1), keyval], axis=0)
    attended, probs = attend(queries, window, place.reshape(1), hops)
    (branch,) = product("nt", attended, small_full, bm=rows, bn=512, width=features, col=1)
    middle, second_low, second_inverse = by_rows(
        add_norm,
        [tokens, branch, swap_tp(branch)],
        [gain_two],
        [(features, LOW), (features, LOW), (128, WIDE)],
        block,
    )
    (gate,) = product("nn", second_low, gate_full, bm=rows, bn=768, width=units, outs=(WIDE,))
    hidden, to_up, to_gate = product(
        "nn",
        second_low,
        up_full,
        bm=rows,
        bn=768,
        width=units,
        sub=256,
        extras=[gate],
        finish=finish_up,
        outs=(LOW, LOW, LOW),
    )

    plain = {
        "gate_back": (rows, units),
        "up_back": (rows, units),
        "second": (rows, features),
        "second_other": (rows, features),
        "feed0": (rows // 2, features),
        "feed1": (rows // 2, features),
        "feed_other0": (rows // 2, features),
        "feed_other1": (rows // 2, features),
        "middle_low": (rows, features),
        "grad_attended": (rows, width),
        "query_back": (rows, width),
        "window_back": window.shape,
        "window_other": (hops, rows, 2 * HD),
        "keyval_own": (rows, 2 * HD),
        "keyval_other": (rows, 2 * HD),
        "keyval_back": (rows, 2 * HD),
        "share": (rows, features),
        "share_other0": (rows // 2, features),
        "share_other1": (rows // 2, features),
        "input_grad": (rows, features),
        "output": (rows, features),
    }
    shapes = {key: jax.ShapeDtypeStruct(shape, LOW) for key, shape in plain.items()}
    shapes |= ScatterFirst.shapes("d_", features, units, count)
    for prefix, each in (("g_", units), ("u_", units), ("o_", width), ("q_", width), ("k_", 2 * HD)):
        shapes |= Scatter.shapes(prefix, features, each, count)
    done = dict(
        cotangent=cotangent,
        down_full=down_full,
        gate_full=gate_full,
        up_full=up_full,
        small_full=small_full,
        to_gate=to_gate,
        to_up=to_up,
        hidden=hidden,
        first_low=first_low,
        second_low=second_low,
        middle=middle,
        second_inverse=second_inverse,
        gain_two=gain_two,
        gain_one=gain_one,
        tokens=tokens,
        first_inverse=jnp.broadcast_to(first_inverse, (rows, 128)),
        queries=queries,
        window=window,
        attended=attended,
        probs=probs,
    )
    total = pltpu.VMEM((features // 4, max(width, units // 3)), WIDE)
    sizes = dict(rows=rows, heads=heads, count=count)
    late = len(bits_of(count)) - 1

    def stage(prefix, *keys):
        return [prefix + key for key in keys]

    def halving(prefix, first, end):
        keys = []
        for k in range(first, end):
            keys += [f"{prefix}recv{k}"] + ([f"{prefix}mid{k}"] if k < late else [])
        return keys

    reads, writes = ["cotangent", "hidden"], stage("d_", "away", "got", "near")
    call = remote_call(
        by_name(functools.partial(down_start, count=count), reads, writes, 1),
        reads,
        [shapes[key] for key in writes],
        [total],
        0,
        "down_start",
    )
    done |= zip(writes, call(*[done[key] for key in reads]))

    reads = ["d_near", "cotangent", "hidden", "down_full", "gate_full", "up_full", "small_full"]
    reads += ["to_gate", "to_up", "first_low", "second_low", "middle", "tokens", "first_inverse", "second_inverse"]
    reads += ["gain_one", "gain_two", "attended", "queries", "window", "probs"]
    writes = list(plain) + ["d_arrived"] + halving("d_", 0, late + 1) + [f"d_mid{late}"]
    for prefix in ("g_", "u_", "o_", "q_", "k_"):
        writes += stage(prefix, "away", "got", "far", "arrived", "near") + halving(prefix, 0, late + 1)
    call = remote_call(
        by_name(functools.partial(backward, hops=hops, **sizes), reads, writes, 1),
        reads,
        [shapes[key] for key in writes],
        [total],
        1,
        "backward",
    )
    done |= zip(writes, call(*[done[key] for key in reads]))
    down_grad = scatter_first_result("d_", done)
    gate_grad, up_grad, out_grad, query_grad, keyval_grad = (
        scatter_result(prefix, done) for prefix in ("g_", "u_", "o_", "q_", "k_")
    )

    def row_sum(weight, grad):
        return jnp.sum(weight.astype(WIDE) * grad, axis=1)

    sums = jnp.stack(
        [
            row_sum(query_weight, query_grad),
            row_sum(gate_weight, gate_grad) + row_sum(up_weight, up_grad),
        ]
    )
    sums = sums + swap_tp(sums)
    first_grad = (sums[0] + row_sum(keyval_weight, keyval_grad)) / (1.0 + first_gain.astype(WIDE))
    second_grad = sums[1] / (1.0 + second_gain.astype(WIDE))
    return (
        done["output"],
        done["input_grad"],
        query_grad,
        keyval_grad,
        out_grad,
        gate_grad,
        up_grad,
        down_grad,
        first_grad,
        second_grad,
    )


def solution(mesh):
    rows = P(("fsdp", "ctx"), None)
    split = P(("fsdp", "ctx"), "tp")
    vector = P(("fsdp", "ctx"))
    return jax.shard_map(
        on_device,
        mesh=mesh,
        in_specs=(rows, split, rows, split, split, split, split, vector, vector, rows),
        out_specs=(rows, rows, split, rows, split, split, split, split, vector, vector),
        check_vma=False,
    )
```

```python
import functools

import jax
import jax.numpy as jnp
from jax import lax
from jax.experimental import pallas as pl
from jax.experimental.pallas import tpu as pltpu
from jax.sharding import PartitionSpec as P

HD = 256
W = 2048
EPS = 1e-06
FAR = -1e30
LOW = jnp.bfloat16
WIDE = jnp.float32
CONTRACT_ROWS = (((0,), (0,)), ((), ()))
CONTRACT_LAST = (((1,), (1,)), ((), ()))
VMEM = 60 * 1024 * 1024


def matmul(left, right):
    return jnp.dot(left, right, preferred_element_type=WIDE)


def rows_product(left, right):
    return lax.dot_general(left, right, CONTRACT_ROWS, preferred_element_type=WIDE)


def right_transposed(left, right):
    return lax.dot_general(left, right, CONTRACT_LAST, preferred_element_type=WIDE)


def gelu_parts(gate):
    c = 0.7978845608028654
    inner = c * (gate + 0.044715 * gate * gate * gate)
    t = jnp.tanh(inner)
    value = 0.5 * gate * (1.0 + t)
    slope = 0.5 * (1.0 + t) + 0.5 * gate * (1.0 - t * t) * c * (1.0 + 3 * 0.044715 * gate * gate)
    return value, slope


def attend_kernel(place_ref, q_ref, win_ref, out_ref, probs_ref, bias_ref, *, heads, hops, rows, block):
    span = W + block
    start = pl.program_id(0) * block
    first = (hops - place_ref[0]) * rows - start
    row = lax.broadcasted_iota(jnp.int32, (block, span), 0)
    col = lax.broadcasted_iota(jnp.int32, (block, span), 1)
    live = (col > row) & (col <= row + W) & (col >= first)
    bias_ref[...] = jnp.where(live, 0.0, FAR)
    window = pl.ds(pl.multiple_of(start, block), span)
    for h in range(heads):
        cols = slice(h * HD, (h + 1) * HD)
        scores = right_transposed(q_ref[:, cols], win_ref[window, :HD]) + bias_ref[...]
        top = jnp.max(scores, axis=1, keepdims=True)
        weights = jnp.exp(scores - top)
        total = jnp.sum(weights, axis=1, keepdims=True)
        probs_ref[h] = (weights * (1.0 / total)).astype(LOW)
        out_ref[:, cols] = matmul(probs_ref[h], win_ref[window, HD:]).astype(LOW)


def attend(queries, window, place, hops):
    rows, width = queries.shape
    heads = width // HD
    block = min(256, rows)
    span = W + block
    return pl.pallas_call(
        functools.partial(attend_kernel, heads=heads, hops=hops, rows=rows, block=block),
        grid=(rows // block,),
        in_specs=[
            pl.BlockSpec(memory_space=pltpu.SMEM),
            pl.BlockSpec((block, width), lambda i: (i, 0)),
            pl.BlockSpec(window.shape, lambda i: (0, 0)),
        ],
        out_specs=[
            pl.BlockSpec((block, width), lambda i: (i, 0)),
            pl.BlockSpec((heads, block, span), lambda i: (0, i, 0)),
        ],
        out_shape=[
            jax.ShapeDtypeStruct((rows, width), LOW),
            jax.ShapeDtypeStruct((heads, rows, span), LOW),
        ],
        scratch_shapes=[pltpu.VMEM((block, span), WIDE)],
        compiler_params=pltpu.CompilerParams(vmem_limit_bytes=VMEM),
        name="attend",
    )(place, queries, window)


CONTRACT = {"nn": (((1,), (0,)), ((), ())), "nt": CONTRACT_LAST, "tn": CONTRACT_ROWS}


def products_body(kind, n_pairs, n_extras, finish, sub, keep):
    def body(*refs):
        pairs = [(refs[2 * p], refs[2 * p + 1]) for p in range(n_pairs)]
        extras = refs[2 * n_pairs : 2 * n_pairs + n_extras]
        outs = refs[2 * n_pairs + n_extras :]
        bn = pairs[0][1].shape[0 if kind == "nt" else 1]
        step = sub or bn
        for start in range(0, bn, step):
            cols = slice(start, start + step)
            total = None
            for left, right in pairs:
                part = right[cols, :] if kind == "nt" else right[:, cols]
                term = lax.dot_general(left[...], part, CONTRACT[kind], preferred_element_type=WIDE)
                total = term if total is None else total + term
            given = [e[:, cols].astype(WIDE) for e in extras]
            keep(outs, cols, finish(total, *given) if finish else [sum(given, total)])

    return body


def keep_blocks(outs, cols, results):
    for out, result in zip(outs, results, strict=True):
        out[:, cols] = result.astype(out.dtype)


def products_specs(kind, depths, bm, bn, left_block, right_col):
    specs = []
    for depth in depths:
        if kind == "tn":
            specs.append(pl.BlockSpec((depth, bm), lambda i, j: (0, left_block(i))))
        else:
            specs.append(pl.BlockSpec((bm, depth), lambda i, j: (left_block(i), 0)))
        if kind == "nt":
            specs.append(pl.BlockSpec((bn, depth), lambda i, j: (j, right_col)))
        else:
            specs.append(pl.BlockSpec((depth, bn), lambda i, j: (0, right_col + j)))
    return specs


def product(kind, left, right, *, bm, bn, width, col=0, extras=(), finish=None, outs=(LOW,), sub=0):
    depth = left.shape[1]
    by_block = pl.BlockSpec((bm, bn), lambda i, j: (i, j))
    return pl.pallas_call(
        products_body(kind, 1, len(extras), finish, sub, keep_blocks),
        grid=(left.shape[0] // bm, width // bn),
        in_specs=products_specs(kind, [depth], bm, bn, lambda i: i, col) + [by_block] * len(extras),
        out_specs=[by_block] * len(outs),
        out_shape=[jax.ShapeDtypeStruct((left.shape[0], width), each) for each in outs],
        compiler_params=pltpu.CompilerParams(vmem_limit_bytes=VMEM),
        name="product",
    )(left, right, *extras)


def by_rows(body, sliced, whole, outs, block):
    rows = sliced[0].shape[0]
    n_in = len(sliced) + len(whole)
    specs = [pl.BlockSpec((block, a.shape[1]), lambda i: (i, 0)) for a in sliced]
    specs += [pl.BlockSpec(a.shape, lambda i: (0, 0)) for a in whole]
    return pl.pallas_call(
        lambda *refs: body(refs[:n_in], refs[n_in:]),
        grid=(rows // block,),
        in_specs=specs,
        out_specs=[pl.BlockSpec((block, cols), lambda i: (i, 0)) for cols, _ in outs],
        out_shape=[jax.ShapeDtypeStruct((rows, cols), kind) for cols, kind in outs],
        compiler_params=pltpu.CompilerParams(vmem_limit_bytes=VMEM),
        name="by_rows",
    )(*sliced, *whole)


def add_norm(ins, outs):
    tokens, own, other, gain = ins
    middle = tokens[...].astype(WIDE) + (own[...].astype(WIDE) + other[...].astype(WIDE))
    inverse = lax.rsqrt(jnp.mean(middle * middle, axis=1, keepdims=True) + EPS)
    outs[0][...] = middle.astype(LOW)
    outs[1][...] = (middle * inverse * gain[...]).astype(LOW)
    outs[2][...] = jnp.broadcast_to(inverse, outs[2].shape)


def norm_back(values, grad, gain, inverse):
    scaled = grad * gain
    along = jnp.sum(scaled * values, axis=1, keepdims=True) * (1.0 / values.shape[1])
    return inverse * scaled - values * (inverse * inverse * inverse * along)


def middle_back(ins, outs):
    cotangent, middle, inverse, own, other, gain, out_full = ins
    grad = own[...].astype(WIDE) + other[...].astype(WIDE)
    back = norm_back(middle[...].astype(WIDE), grad, gain[...], inverse[:, :1])
    low = (cotangent[...].astype(WIDE) + back).astype(LOW)
    outs[0][...] = low
    outs[1][...] = matmul(low, out_full[...]).astype(LOW)


def source_back(ins, outs):
    tokens, middle_low, inverse, own, other, keyval_back, gain, keyval_full = ins
    grad = own[...].astype(WIDE) + other[...].astype(WIDE)
    grad = grad + right_transposed(keyval_back[...], keyval_full[...])
    back = norm_back(tokens[...].astype(WIDE), grad, gain[...], inverse[:, :1])
    outs[0][...] = (middle_low[...].astype(WIDE) + back).astype(LOW)


def add_feed(ins, outs):
    middle, own, other = ins
    outs[0][...] = (middle[...].astype(WIDE) + (own[...].astype(WIDE) + other[...].astype(WIDE))).astype(LOW)


def finish_up(upward, gate):
    value, slope = gelu_parts(gate)
    return value * upward, value, slope * upward


def finish_hidden(grad_hidden, to_gate, to_up):
    return grad_hidden * to_gate, grad_hidden * to_up


MESH = pl.DeviceIdType.MESH


class Links:
    def __init__(self, send_sems, recv_sems):
        self.send_sems, self.recv_sems = send_sems, recv_sems
        self.count = 0
        self.open = []
        self.fsdp = lax.axis_index("fsdp")
        self.place = lax.axis_index("ctx")
        self.core = {"fsdp": self.fsdp + 1 - 2 * lax.rem(self.fsdp, 2)}
        self.chip = {"fsdp": lax.rem(self.fsdp + 2, 4)}
        self.tp = {"tp": 1 - lax.axis_index("tp")}

    def block(self, flip):
        return (self.fsdp, self.core["fsdp"], self.chip["fsdp"], 3 - self.fsdp)[flip]

    def along(self, bit):
        return {"ctx": self.place + bit - 2 * bit * lax.rem(lax.div(self.place, bit), 2)}

    def meet(self, partners):
        barrier = pltpu.get_barrier_semaphore()
        for partner in partners:
            pl.semaphore_signal(barrier, inc=1, device_id=partner, device_id_type=MESH)
        pl.semaphore_wait(barrier, len(partners))

    def copy(self, source, target, partner):
        made = pltpu.make_async_remote_copy(
            src_ref=source,
            dst_ref=target,
            send_sem=self.send_sems.at[self.count],
            recv_sem=self.recv_sems.at[self.count],
            device_id=partner,
            device_id_type=MESH,
        )
        self.count += 1
        return made

    def send(self, source, target, partner):
        made = self.copy(source, target, partner)
        made.start()
        self.open.append(made)
        return made

    def close(self):
        for made in self.open:
            made.wait_send()


def job(kind, pairs, outs, *, bm, bn, steps=1, left_block=None, right_col=0, extras=(), finish=None, sub=0):
    depths = [left.shape[0 if kind == "tn" else 1] for left, _ in pairs]
    width = outs[0].shape[1]
    specs = products_specs(kind, depths, bm, bn, left_block or (lambda i: i), right_col)
    specs += [pl.BlockSpec((bm, bn), lambda i, j, at=at: (i + at, j)) for _, at in extras]
    pltpu.emit_pipeline(
        products_body(kind, len(pairs), len(extras), finish, sub, keep_blocks),
        grid=(steps, width // bn),
        in_specs=specs,
        out_specs=[pl.BlockSpec((bm, bn), lambda i, j: (i, j))] * len(outs),
    )(*[ref for pair in pairs for ref in pair], *[ref for ref, _ in extras], *outs)


def rows_job(body, sliced, whole, outs, block):
    n_in = len(sliced) + len(whole)
    specs = [pl.BlockSpec((block, a.shape[1]), lambda i: (i, 0)) for a in sliced]
    specs += [pl.BlockSpec(a.shape, lambda i: (0, 0)) for a in whole]
    pltpu.emit_pipeline(
        lambda *refs: body(refs[:n_in], refs[n_in:]),
        grid=(sliced[0].shape[0] // block,),
        in_specs=specs,
        out_specs=[pl.BlockSpec((block, a.shape[1]), lambda i: (i, 0)) for a in outs],
    )(*sliced, *whole, *outs)


def bits_of(count):
    bits = []
    while 1 << len(bits) < count:
        bits.append(1 << len(bits))
    return bits


def piece_order(count):
    order = [0]
    for bit in reversed(bits_of(count)):
        order = order + [r + bit for r in order]
    return order


class Scatter:
    add_last = False

    @staticmethod
    def shapes(prefix, features, width, count):
        part = features // 4
        size = part // count
        out = {"away": (2 * part, width), "got": (2 * part, width), "far": (part, width), "arrived": (part, width)}
        left = count
        out["near"] = (left, size, width)
        for k in range(len(bits_of(count))):
            left //= 2
            out[f"recv{k}"] = (left, size, width)
            if left > 1:
                out[f"mid{k}"] = (left, size, width)
        return {prefix + key: jax.ShapeDtypeStruct(shape, LOW) for key, shape in out.items()}

    def __init__(self, prefix, refs, links, left, right, bn, count, total=None):
        self.refs, self.prefix, self.links, self.bn, self.total = refs, prefix, links, bn, total
        self.pairs = [(refs[left], refs[right])]
        self.part = refs[left].shape[1] // 4
        self.bits = bits_of(count)
        self.moving = {}

    def ref(self, key):
        return self.refs[self.prefix + key]

    def wait(self, key):
        if key in self.moving:
            self.moving.pop(key).wait_recv()

    def away(self):
        core, both = self.links.block(1), self.links.block(3)
        job(
            "tn",
            self.pairs,
            [self.ref("away")],
            bm=self.part,
            bn=self.bn,
            steps=2,
            left_block=lambda i: both + i * (core - both),
        )
        self.moving["got"] = self.links.send(self.ref("away"), self.ref("got"), self.links.core)

    def far(self):
        self.wait("got")
        chip = self.links.block(2)
        job(
            "tn",
            self.pairs,
            [self.ref("far")],
            bm=self.part,
            bn=self.bn,
            left_block=lambda i: chip,
            extras=[(self.ref("got"), 0)],
        )

    def cross(self):
        self.moving["arrived"] = self.links.send(self.ref("far"), self.ref("arrived"), self.links.chip)

    def near(self):
        self.wait("arrived")
        own = self.links.block(0)
        extras = [pl.BlockSpec((self.part, self.bn), lambda i, j: (1, j)), pl.BlockSpec((self.part, self.bn), lambda i, j: (0, j))]
        self.make_near(1, lambda i: own, [self.ref("got"), self.ref("arrived")], extras)

    def make_near(self, steps, left_block, given, extras):
        place = self.links.place
        near, total = self.ref("near"), self.total
        count = near.shape[0]
        size = self.part // count
        order = piece_order(count)

        def keep(outs, cols, results):
            total[:, cols] = results[0]
            for k in range(count):
                at = 0
                for bit in self.bits:
                    mine = lax.rem(lax.div(place, bit), 2)
                    at = at + bit * (1 - mine if order[k] & bit else mine)
                rows = pl.ds(pl.multiple_of(at * size, size), size)
                outs[0][k, :, cols] = total[rows, cols].astype(LOW)

        bm, bn = self.part, self.bn
        left, right = self.pairs[0]
        pltpu.emit_pipeline(
            products_body("tn", 1, len(given), None, 0, keep),
            grid=(steps, right.shape[1] // bn),
            in_specs=products_specs("tn", [left.shape[0]], bm, bn, left_block, 0) + extras,
            out_specs=[pl.BlockSpec((count, size, bn), lambda i, j: (0, i, j))],
        )(left, right, *given, near)

    def kept(self, k):
        return self.ref(f"mid{k - 1}" if k else "near")

    def halve(self, k):
        now = self.kept(k)
        half = now.shape[0] // 2
        self.moving[f"recv{k}"] = self.links.send(
            now.at[pl.ds(half, half)], self.ref(f"recv{k}"), self.links.along(self.bits[k])
        )

    def add(self, k):
        self.wait(f"recv{k}")
        if k + 1 == len(self.bits) and not self.add_last:
            return
        now, mid = self.kept(k), self.ref(f"mid{k}")
        half, size, bn = mid.shape[0], mid.shape[1], self.bn

        def body(own, other, out):
            out[...] = (own[...].astype(WIDE) + other[...].astype(WIDE)).astype(LOW)

        block = pl.BlockSpec((half, size, bn), lambda j: (0, 0, j))
        pltpu.emit_pipeline(body, grid=(mid.shape[2] // bn,), in_specs=[block, block], out_specs=[block])(
            now, self.ref(f"recv{k}"), mid
        )

    def rest(self, k):
        self.add(k)
        for later in range(k + 1, len(self.bits)):
            self.halve(later)
            self.add(later)


class ScatterFirst(Scatter):
    add_last = True

    @staticmethod
    def shapes(prefix, features, width, count):
        part = features // 4
        size = part // count
        out = {"away": (2 * part, width), "got": (2 * part, width), "near": (count, 2 * size, width)}
        left = count
        for k in range(len(bits_of(count))):
            left //= 2
            out[f"recv{k}"] = out[f"mid{k}"] = (left, 2 * size, width)
        out["arrived"] = (size, width)
        return {prefix + key: jax.ShapeDtypeStruct(shape, LOW) for key, shape in out.items()}

    def near(self):
        self.wait("got")
        chip, own = self.links.block(2), self.links.block(0)
        extras = [pl.BlockSpec((self.part, self.bn), lambda i, j: (i, j))]
        self.make_near(2, lambda i: chip + i * (own - chip), [self.ref("got")], extras)

    def cross(self):
        last = self.kept(len(self.bits))
        size = last.shape[1] // 2
        self.moving["arrived"] = self.links.send(
            last.at[0, pl.ds(0, size)], self.ref("arrived"), self.links.chip
        )


def scatter_result(prefix, arrays):
    last = len(bits_of(arrays[prefix + "near"].shape[0])) - 1
    now = arrays[prefix + (f"mid{last - 1}" if last else "near")]
    return now[0].astype(WIDE) + arrays[prefix + f"recv{last}"][0].astype(WIDE)


def scatter_first_result(prefix, arrays):
    size = arrays[prefix + "arrived"].shape[0]
    last = len(bits_of(arrays[prefix + "near"].shape[0])) - 1
    return arrays[prefix + f"mid{last}"][0, size:].astype(WIDE) + arrays[prefix + "arrived"].astype(WIDE)


def remote_call(kernel, inputs, outputs, scratch, collective_id, name):
    anywhere = pl.BlockSpec(memory_space=pl.ANY)
    sems = pltpu.SemaphoreType.DMA((64,))
    return pl.pallas_call(
        kernel,
        in_specs=[anywhere] * len(inputs),
        out_specs=[anywhere] * len(outputs),
        out_shape=outputs,
        scratch_shapes=scratch + [sems, sems],
        compiler_params=pltpu.CompilerParams(
            collective_id=collective_id, has_side_effects=True, vmem_limit_bytes=VMEM
        ),
        name=name,
    )


def by_name(body, reads, writes, n_scratch):
    names = reads + writes

    def kernel(*refs):
        rest = refs[len(names) :]
        body(dict(zip(names, refs)), Links(rest[-2], rest[-1]), *rest[:n_scratch])

    return kernel


def down_start(r, links, total, *, count):
    links.meet([links.core])
    down = ScatterFirst("d_", r, links, "cotangent", "hidden", r["hidden"].shape[1] // 3, count, total)
    down.away()
    down.near()
    links.close()


def attend_back(refs, rows, heads, block):
    span = W + block
    steps = rows // block
    queries, backs, outs, probs = (refs[k] for k in ("queries", "grad_attended", "attended", "probs"))

    def scoped(win, dwin, q, back, out, dq, p, ds, sems):
        loads = [
            pltpu.make_async_copy(a, b, sems.at[k])
            for k, (a, b) in enumerate([(refs["window"], win), (queries, q), (backs, back), (outs, out)])
        ]

        def fetch(i):
            slot = lax.rem(i, 2)
            at = pl.ds(pl.multiple_of(i * block, block), block)
            return pltpu.make_async_copy(probs.at[:, at, :], p.at[slot], sems.at[4 + slot])

        fetch(0).start()
        for load in loads:
            load.start()
        dwin[...] = jnp.zeros_like(dwin)
        for load in loads:
            load.wait()

        def step(i, carry):
            @pl.when(i + 1 < steps)
            def _():
                fetch(i + 1).start()

            fetch(i).wait()
            slot = lax.rem(i, 2)
            at = pl.ds(pl.multiple_of(i * block, block), block)
            window = pl.ds(pl.multiple_of(i * block, block), span)
            for h in range(heads):
                cols = slice(h * HD, (h + 1) * HD)
                g = back[at, cols]
                along = jnp.sum(g.astype(WIDE) * out[at, cols].astype(WIDE), axis=1, keepdims=True)
                grad_probs = right_transposed(g, win[window, HD:])
                ds[h] = (p[slot, h].astype(WIDE) * (grad_probs - along)).astype(LOW)
                part = matmul(ds[h], win[window, :HD]).astype(LOW)
                dq[at, cols] = (part.astype(WIDE) * HD ** (-0.5)).astype(LOW)
            q_all = jnp.concatenate([q[at, h * HD : (h + 1) * HD] for h in range(heads)], axis=0)
            g_all = jnp.concatenate([back[at, h * HD : (h + 1) * HD] for h in range(heads)], axis=0)
            dwin[window, :HD] += rows_product(ds[...].reshape(heads * block, span), q_all)
            dwin[window, HD:] += rows_product(p[slot].reshape(heads * block, span), g_all)
            return carry

        lax.fori_loop(0, steps, step, 0)
        win[...] = dwin[...].astype(LOW)
        stores = [
            pltpu.make_async_copy(win, refs["window_back"], sems.at[0]),
            pltpu.make_async_copy(dq, refs["query_back"], sems.at[1]),
        ]
        for store in stores:
            store.start()
        for store in stores:
            store.wait()

    width = heads * HD
    length = refs["window"].shape[0]
    pl.run_scoped(
        scoped,
        pltpu.VMEM((length, 2 * HD), LOW),
        pltpu.VMEM((length, 2 * HD), WIDE),
        pltpu.VMEM((rows, width), LOW),
        pltpu.VMEM((rows, width), LOW),
        pltpu.VMEM((rows, width), LOW),
        pltpu.VMEM((rows, width), LOW),
        pltpu.VMEM((2, heads, block, span), LOW),
        pltpu.VMEM((heads, block, span), LOW),
        pltpu.SemaphoreType.DMA((6,)),
    )


def window_sum(place, count, hops):
    def body(ins, outs):
        total = ins[0][...].astype(WIDE)
        for by in range(1, hops + 1):
            total = total + jnp.where(place + by < count, ins[by][...].astype(WIDE), 0.0)
        outs[0][...] = total.astype(LOW)

    return body


def pair_sum(ins, outs):
    outs[0][...] = (ins[0][...].astype(WIDE) + ins[1][...].astype(WIDE)).astype(LOW)


def backward(r, links, total, *, rows, heads, hops, count):
    half = rows // 2
    block = min(256, half)
    features = r["cotangent"].shape[1]
    width = heads * HD
    third = r["hidden"].shape[1] // 3
    bits = bits_of(count)
    links.meet([links.core, links.chip, links.tp] + [{"ctx": lax.rem(links.place + k, count)} for k in range(1, count)])
    down = ScatterFirst("d_", r, links, "cotangent", "hidden", third, count, total)
    gate = Scatter("g_", r, links, "second_low", "gate_back", third, count, total)
    up = Scatter("u_", r, links, "second_low", "up_back", third, count, total)
    out = Scatter("o_", r, links, "middle_low", "attended", width, count, total)
    query = Scatter("q_", r, links, "first_low", "query_back", width, count, total)
    keyval = Scatter("k_", r, links, "first_low", "keyval_back", 2 * HD, count, total)
    parts = (pl.ds(0, half), pl.ds(half, half))

    def second(part):
        job(
            "nt",
            [(r["gate_back"].at[part], r["gate_full"]), (r["up_back"].at[part], r["up_full"])],
            [r["second"].at[part]],
            bm=half,
            bn=256,
        )
        return links.send(r["second"].at[part], r["second_other"].at[part], links.tp)

    def feed(k):
        job("nt", [(r["hidden"].at[parts[k]], r["down_full"])], [r[f"feed{k}"]], bm=half, bn=512)
        return links.send(r[f"feed{k}"], r[f"feed_other{k}"], links.tp)

    def share(k):
        return links.send(r["share"].at[parts[k]], r[f"share_other{k}"], links.tp)

    def finish_source(k):
        part = parts[k]
        rows_job(
            source_back,
            [r[key].at[part] for key in ("tokens", "middle_low", "first_inverse", "share")]
            + [r[f"share_other{k}"], r["keyval_back"].at[part]],
            [r["gain_one"], r["small_full"].at[:, pl.ds(2 * width, 2 * HD)]],
            [r["input_grad"].at[part]],
            block,
        )

    def finish_output(k):
        part = parts[k]
        rows_job(add_feed, [r["middle"].at[part], r[f"feed{k}"], r[f"feed_other{k}"]], [], [r["output"].at[part]], block)

    def windows_to(place, by):
        return links.copy(
            r["window_back"].at[pl.ds((hops - by) * rows, rows)],
            r["window_other"].at[by - 1],
            {"ctx": lax.rem(place + count - by, count)},
        )

    down.halve(0)
    job(
        "nn",
        [(r["cotangent"], r["down_full"])],
        [r["gate_back"], r["up_back"]],
        bm=rows,
        bn=third * 3 // 5,
        sub=third // 5,
        extras=[(r["to_gate"], 0), (r["to_up"], 0)],
        finish=finish_hidden,
    )
    gate.away()
    second0 = second(parts[0])
    gate.far()
    gate.cross()
    second1 = second(parts[1])
    up.away()
    down.add(0)
    if len(bits) > 1:
        down.halve(1)
    up.far()
    feed1 = feed(1)
    feed0 = feed(0)
    up.cross()
    gate.near()
    gate.halve(0)
    second0.wait_recv()
    second1.wait_recv()
    rows_job(
        middle_back,
        [r["cotangent"], r["middle"], r["second_inverse"], r["second"], r["second_other"]],
        [r["gain_two"], r["small_full"].at[:, pl.ds(width, width)]],
        [r["middle_low"], r["grad_attended"]],
        block,
    )
    attend_back(r, rows, heads, min(256, rows))
    windows = []
    for by in range(1, hops + 1):
        move = windows_to(links.place, by)

        @pl.when(links.place >= by)
        def _(move=move):
            move.start()

        windows.append(move)
    out.away()
    out.far()
    gate.add(0)
    if len(bits) > 1:
        gate.halve(1)
    job("nt", [(r["query_back"], r["small_full"].at[:, pl.ds(0, width)])], [r["share"]], bm=rows, bn=512)
    share0 = share(0)
    up.near()
    up.halve(0)
    out.cross()
    query.away()
    query.far()
    query.cross()
    if len(bits) > 1:
        down.rest(1)
    down.cross()
    for by in range(1, hops + 1):

        @pl.when(links.place + by < count)
        def _(move=windows[by - 1]):
            move.wait_recv()

    rows_job(
        window_sum(links.place, count, hops),
        [r["window_back"].at[pl.ds(hops * rows, rows)]] + [r["window_other"].at[by] for by in range(hops)],
        [],
        [r["keyval_own"]],
        block,
    )
    swap = links.send(r["keyval_own"], r["keyval_other"], links.tp)
    out.near()
    out.halve(0)
    up.add(0)
    if len(bits) > 1:
        up.halve(1)
    swap.wait_recv()
    rows_job(pair_sum, [r["keyval_own"], r["keyval_other"]], [], [r["keyval_back"]], block)
    share0.wait_recv()
    finish_source(0)
    share1 = share(1)
    feed0.wait_recv()
    finish_output(0)
    query.near()
    query.halve(0)
    keyval.away()
    feed1.wait_recv()
    finish_output(1)
    keyval.far()
    out.add(0)
    if len(bits) > 1:
        out.halve(1)
    keyval.cross()
    query.add(0)
    if len(bits) > 1:
        query.halve(1)
    keyval.near()
    keyval.halve(0)
    keyval.add(0)
    if len(bits) > 1:
        keyval.halve(1)
    share1.wait_recv()
    finish_source(1)
    if len(bits) > 1:
        for each in (gate, up, out, query, keyval):
            each.rest(1)
    down.wait("arrived")
    for by in range(1, hops + 1):

        @pl.when(links.place >= by)
        def _(move=windows[by - 1]):
            move.wait_send()

    links.close()


def from_place(array, by):
    count = lax.axis_size("ctx")
    return lax.ppermute(array, "ctx", [(i, i + by) for i in range(count) if i + by < count])


def swap_tp(array):
    return lax.ppermute(array, "tp", [(0, 1), (1, 0)])


def gathered(shard):
    return lax.all_gather(shard, ("fsdp", "ctx"), axis=0, tiled=True)


def on_device(
    tokens,
    query_weight,
    keyval_weight,
    out_weight,
    gate_weight,
    up_weight,
    down_weight,
    first_gain,
    second_gain,
    cotangent,
):
    rows, features = tokens.shape
    width = query_weight.shape[1]
    units = gate_weight.shape[1]
    heads = width // HD
    scale = HD ** (-0.5)
    count = lax.axis_size("ctx")
    hops = min(-(-W // rows), count - 1)
    place = lax.axis_index("ctx")
    block = min(256, rows)

    spare = units - 2 * width - 2 * HD - 2
    gains = jnp.pad(jnp.stack([first_gain, second_gain], axis=1), ((0, 0), (0, spare)))
    small_full = gathered(jnp.concatenate([query_weight, out_weight, keyval_weight, gains], axis=1))
    gate_full = gathered(gate_weight)
    up_full = gathered(up_weight)
    down_full = gathered(down_weight)
    query_full = small_full[:, :width]
    keyval_full = small_full[:, 2 * width : 2 * width + 2 * HD]
    both_gains = 1.0 + small_full[:, 2 * width + 2 * HD :][:, :2].astype(WIDE).T
    gain_one, gain_two = both_gains[:1], both_gains[1:]

    source = tokens.astype(WIDE)
    first_inverse = lax.rsqrt(jnp.mean(source * source, axis=-1, keepdims=True) + EPS)
    first_low = (source * first_inverse * gain_one).astype(LOW)
    keyval = matmul(first_low, keyval_full).astype(LOW)
    first_tp = lax.axis_index("tp") == 0
    mine = jnp.where(first_tp, keyval[:, :HD], keyval[:, HD:])
    before = jnp.concatenate([from_place(mine, by) for by in range(hops, 0, -1)])
    theirs = swap_tp(before)
    queries = (matmul(first_low, query_full) * scale).astype(LOW)
    keys = jnp.where(first_tp, before, theirs)
    values = jnp.where(first_tp, theirs, before)
    window = jnp.concatenate([jnp.concatenate([keys, values], axis=1), keyval], axis=0)
    attended, probs = attend(queries, window, place.reshape(1), hops)
    (branch,) = product("nt", attended, small_full, bm=rows, bn=512, width=features, col=1)
    middle, second_low, second_inverse = by_rows(
        add_norm,
        [tokens, branch, swap_tp(branch)],
        [gain_two],
        [(features, LOW), (features, LOW), (128, WIDE)],
        block,
    )
    (gate,) = product("nn", second_low, gate_full, bm=rows, bn=768, width=units, outs=(WIDE,))
    hidden, to_up, to_gate = product(
        "nn",
        second_low,
        up_full,
        bm=rows,
        bn=768,
        width=units,
        sub=256,
        extras=[gate],
        finish=finish_up,
        outs=(LOW, LOW, LOW),
    )

    plain = {
        "gate_back": (rows, units),
        "up_back": (rows, units),
        "second": (rows, features),
        "second_other": (rows, features),
        "feed0": (rows // 2, features),
        "feed1": (rows // 2, features),
        "feed_other0": (rows // 2, features),
        "feed_other1": (rows // 2, features),
        "middle_low": (rows, features),
        "grad_attended": (rows, width),
        "query_back": (rows, width),
        "window_back": window.shape,
        "window_other": (hops, rows, 2 * HD),
        "keyval_own": (rows, 2 * HD),
        "keyval_other": (rows, 2 * HD),
        "keyval_back": (rows, 2 * HD),
        "share": (rows, features),
        "share_other0": (rows // 2, features),
        "share_other1": (rows // 2, features),
        "input_grad": (rows, features),
        "output": (rows, features),
    }
    shapes = {key: jax.ShapeDtypeStruct(shape, LOW) for key, shape in plain.items()}
    shapes |= ScatterFirst.shapes("d_", features, units, count)
    for prefix, each in (("g_", units), ("u_", units), ("o_", width), ("q_", width), ("k_", 2 * HD)):
        shapes |= Scatter.shapes(prefix, features, each, count)
    done = dict(
        cotangent=cotangent,
        down_full=down_full,
        gate_full=gate_full,
        up_full=up_full,
        small_full=small_full,
        to_gate=to_gate,
        to_up=to_up,
        hidden=hidden,
        first_low=first_low,
        second_low=second_low,
        middle=middle,
        second_inverse=second_inverse,
        gain_two=gain_two,
        gain_one=gain_one,
        tokens=tokens,
        first_inverse=jnp.broadcast_to(first_inverse, (rows, 128)),
        queries=queries,
        window=window,
        attended=attended,
        probs=probs,
    )
    total = pltpu.VMEM((features // 4, max(width, units // 3)), WIDE)
    sizes = dict(rows=rows, heads=heads, count=count)
    late = len(bits_of(count)) - 1

    def stage(prefix, *keys):
        return [prefix + key for key in keys]

    def halving(prefix, first, end):
        keys = []
        for k in range(first, end):
            keys += [f"{prefix}recv{k}"] + ([f"{prefix}mid{k}"] if k < late else [])
        return keys

    reads, writes = ["cotangent", "hidden"], stage("d_", "away", "got", "near")
    call = remote_call(
        by_name(functools.partial(down_start, count=count), reads, writes, 1),
        reads,
        [shapes[key] for key in writes],
        [total],
        0,
        "down_start",
    )
    done |= zip(writes, call(*[done[key] for key in reads]))

    reads = ["d_near", "cotangent", "hidden", "down_full", "gate_full", "up_full", "small_full"]
    reads += ["to_gate", "to_up", "first_low", "second_low", "middle", "tokens", "first_inverse", "second_inverse"]
    reads += ["gain_one", "gain_two", "attended", "queries", "window", "probs"]
    writes = list(plain) + ["d_arrived"] + halving("d_", 0, late + 1) + [f"d_mid{late}"]
    for prefix in ("g_", "u_", "o_", "q_", "k_"):
        writes += stage(prefix, "away", "got", "far", "arrived", "near") + halving(prefix, 0, late + 1)
    call = remote_call(
        by_name(functools.partial(backward, hops=hops, **sizes), reads, writes, 1),
        reads,
        [shapes[key] for key in writes],
        [total],
        1,
        "backward",
    )
    done |= zip(writes, call(*[done[key] for key in reads]))
    down_grad = scatter_first_result("d_", done)
    gate_grad, up_grad, out_grad, query_grad, keyval_grad = (
        scatter_result(prefix, done) for prefix in ("g_", "u_", "o_", "q_", "k_")
    )

    def row_sum(weight, grad):
        return jnp.sum(weight.astype(WIDE) * grad, axis=1)

    sums = jnp.stack(
        [
            row_sum(query_weight, query_grad),
            row_sum(gate_weight, gate_grad) + row_sum(up_weight, up_grad),
        ]
    )
    sums = sums + swap_tp(sums)
    first_grad = (sums[0] + row_sum(keyval_weight, keyval_grad)) / (1.0 + first_gain.astype(WIDE))
    second_grad = sums[1] / (1.0 + second_gain.astype(WIDE))
    return (
        done["output"],
        done["input_grad"],
        query_grad,
        keyval_grad,
        out_grad,
        gate_grad,
        up_grad,
        down_grad,
        first_grad,
        second_grad,
    )


def solution(mesh):
    rows = P(("fsdp", "ctx"), None)
    split = P(("fsdp", "ctx"), "tp")
    vector = P(("fsdp", "ctx"))
    return jax.shard_map(
        on_device,
        mesh=mesh,
        in_specs=(rows, split, rows, split, split, split, split, vector, vector, rows),
        out_specs=(rows, rows, split, rows, split, split, split, split, vector, vector),
        check_vma=False,
    )
```
